32 devices in a mesh: group: 2 (over x), space: 8 (over z, y), rep: 2 (over core).
Axes of the slice: x: 2, y: 2, z: 4, core: 2. Of those that a mesh axis runs over, the one named last changes fastest.
Arguments:
- latent: bfloat16 [4, 128, 8, 256], P(('group', 'rep'), None, 'space'), parts along dimension 0, may hold values from -12 to 12
- first_weight: bfloat16 [64, 64, 128], replicated, may hold values from -0.1875 to 0.1875
- first_norm_gain: float32 [64], replicated, may hold values from 0.25 to 1.75
- first_norm_shift: float32 [64], replicated, may hold values from -0.5 to 0.5
- second_weight: bfloat16 [64, 32, 64], replicated, may hold values from -0.25 to 0.25
- second_norm_gain: float32 [32], replicated, may hold values from 0.25 to 1.75
- second_norm_shift: float32 [32], replicated, may hold values from -0.5 to 0.5
- cotangent: bfloat16 [4, 32, 32, 4096], P(('group', 'rep'), None, 'space'), parts along dimension 0, may hold values from -6 to 6
Outputs:
- features: bfloat16 [4, 32, 32, 4096], P(('group', 'rep'), None, 'space'), parts along dimension 0
- latent_grad: float32 [4, 128, 8, 256], P(('group', 'rep'), None, 'space'), parts along dimension 0
- first_weight_grad: float32 [128, 64, 128], P('group'), parts along dimension 0
- second_weight_grad: float32 [128, 32, 64], P('group'), parts along dimension 0
- first_batchnorm_gradients: float32 [4, 64], P('group'), parts along dimension 0
- second_batchnorm_gradients: float32 [4, 32], P('group'), parts along dimension 0
The draws below stay inside these ranges and needn't reach their ends.
There are 2 independent parts, one for each index of `group`. The reference program is written for one: setup_inputs(seed, part) draws one part's arguments, and reference() takes and returns one part's arrays. A program takes and returns all parts, laid end to end along the dimension named above; an argument that names none is the same for every part. Nothing has to cross between parts.
All inputs are finite; a program needn't handle non-finite values.
Results may differ from the reference program's by a relative error of at most 0.0054.
Values may be sent and summed in bfloat16 or wider, within the bound.
No kernel may reach another device: no remote copies, remote signals or barrier semaphores. Data moves between devices by JAX's collectives and lax.ppermute only.
A program may use at most 64 MiB of HBM per device.

```python
import jax
import jax.numpy as jnp
from jax import lax

C0 = 128
C1 = 64
C2 = 32
TAPS = 64
H0 = 4
W0 = 64
SAMPLES = 2
DEPTH0 = 8
DEPTH2 = 32
HW0 = 256
HW2 = 4096


def draw_latent(key, part):
    key = jax.random.fold_in(key, 3)
    noise_key = jax.random.fold_in(key, 0)
    drift_key = jax.random.fold_in(key, 1)
    offset_key = jax.random.fold_in(key, 3)
    shape = (SAMPLES, C0, DEPTH0, HW0)
    depth_pos = (jnp.arange(DEPTH0, dtype=jnp.float32) / max(DEPTH0 - 1, 1))[None, None, :, None]
    ramp = 1.0 + 2.0 * depth_pos
    drift = jax.random.normal(drift_key, (1, C0, 1, 1), jnp.float32)
    sample_half = (jnp.arange(SAMPLES) * 2 // SAMPLES).astype(jnp.float32)
    sample_scale = (0.6 + 0.8 * sample_half)[:, None, None, None]
    sample_offset = 0.5 * jax.random.normal(offset_key, (SAMPLES, C0, 1, 1), jnp.float32)
    base = jax.random.normal(noise_key, shape, jnp.float32)
    values = base * ramp * sample_scale + drift * depth_pos + sample_offset
    return jnp.clip(values, -12.0, 12.0).astype(jnp.bfloat16)


def draw_cotangent(key, part):
    key = jax.random.fold_in(key, 7)
    noise_key, offset_key = jax.random.split(key, 2)
    shape = (SAMPLES, C2, DEPTH2, HW2)
    sample_offset = 0.5 * jax.random.normal(offset_key, (SAMPLES, C2, 1, 1), jnp.float32)
    base = jax.random.normal(noise_key, shape, jnp.float32)
    values = base + sample_offset
    return jnp.clip(values, -6.0, 6.0).astype(jnp.bfloat16)


def bell_draw(key, dims, scale, reach, kind=jnp.bfloat16):
    return jnp.clip(scale * jax.random.normal(key, dims, jnp.float32), -reach, reach).astype(kind)


def setup_inputs(seed: int = 0, part: int = 0) -> dict:
    key_of = jax.random.split(jax.random.key(seed), 9)
    part_splits = jax.random.split(jax.random.fold_in(key_of[8], part), 9)
    return {
        "latent": draw_latent(jax.random.fold_in(jax.random.fold_in(key_of[8], part), 71), part),
        "first_weight": bell_draw(key_of[1], (TAPS, C1, C0), (8 * C0) ** -0.5, 0.1875),
        "first_norm_gain": jnp.clip(1.0 + 0.15 * jax.random.normal(key_of[2], (C1,), jnp.float32), 0.25, 1.75),
        "first_norm_shift": jnp.clip(jax.random.uniform(key_of[3], (C1,), jnp.float32, -0.5, 0.5), -0.5, 0.5),
        "second_weight": bell_draw(key_of[4], (TAPS, C2, C1), (8 * C1) ** -0.5, 0.25),
        "second_norm_gain": jnp.clip(1.0 + 0.15 * jax.random.normal(key_of[5], (C2,), jnp.float32), 0.25, 1.75),
        "second_norm_shift": jnp.clip(jax.random.uniform(key_of[6], (C2,), jnp.float32, -0.5, 0.5), -0.5, 0.5),
        "cotangent": draw_cotangent(jax.random.fold_in(jax.random.fold_in(key_of[8], part), 71), part),
    }


norm_epsilon = 1e-05
PHASE_TAPS = (((1, 1), (3, 0)), ((0, 2), (2, 1)))

def activate(values):
    return values * jax.nn.sigmoid(values)

def activate_slope(values):
    gate = jax.nn.sigmoid(values)
    return gate * (1.0 + values * (1.0 - gate))

def expand(field, weight, height, width):
    samples, cin, depth, _ = field.shape
    cout = weight.shape[1]
    kernel = weight.astype(jnp.float32).reshape(4, 4, 4, cout, cin)
    padded = jnp.pad(field.astype(jnp.float32).reshape(samples, cin, depth, height, width), ((0, 0), (0, 0), (1, 1), (1, 1), (1, 1)))
    phases = []
    for depth_phase in range(2):
        for row_phase in range(2):
            for col_phase in range(2):
                total = jnp.zeros((samples, cout, depth, height, width), jnp.float32)
                for depth_tap, depth_start in PHASE_TAPS[depth_phase]:
                    for row_tap, row_start in PHASE_TAPS[row_phase]:
                        for col_tap, col_start in PHASE_TAPS[col_phase]:
                            window = padded[:, :, depth_start:depth_start + depth, row_start:row_start + height, col_start:col_start + width]
                            total = total + jnp.einsum('oc,scdhw->sodhw', kernel[depth_tap, row_tap, col_tap], window, precision=lax.Precision.HIGHEST)
                phases.append(total)
    stacked = jnp.stack(phases).reshape(2, 2, 2, samples, cout, depth, height, width)
    stacked = stacked.transpose(3, 4, 5, 0, 6, 1, 7, 2)
    return stacked.reshape(samples, cout, 2 * depth, 4 * height * width)

def adjoint(upstream_gradient, field, weight, height, width):
    samples, cout, depth_out, _ = upstream_gradient.shape
    depth = depth_out // 2
    cin = field.shape[1]
    kernel = weight.astype(jnp.float32).reshape(4, 4, 4, cout, cin)
    volume_in = field.astype(jnp.float32).reshape(samples, cin, depth, height, width)
    padded = jnp.pad(upstream_gradient.astype(jnp.float32).reshape(samples, cout, depth_out, 2 * height, 2 * width), ((0, 0), (0, 0), (1, 1), (1, 1), (1, 1)))
    padded = padded.reshape(samples, cout, depth + 1, 2, height + 1, 2, width + 1, 2)
    field_grad = jnp.zeros((samples, cin, depth, height, width), jnp.float32)
    kernel_grad = []
    for depth_tap in range(4):
        for row_tap in range(4):
            for col_tap in range(4):
                window = padded[:, :, depth_tap // 2:depth_tap // 2 + depth, depth_tap % 2, row_tap // 2:row_tap // 2 + height, row_tap % 2, col_tap // 2:col_tap // 2 + width, col_tap % 2]
                field_grad = field_grad + jnp.einsum('oc,sodhw->scdhw', kernel[depth_tap, row_tap, col_tap], window, precision=lax.Precision.HIGHEST)
                kernel_grad.append(jnp.einsum('sodhw,scdhw->oc', window, volume_in, precision=lax.Precision.HIGHEST))
    return (field_grad.reshape(samples, cin, depth, height * width), jnp.stack(kernel_grad))

def batch_normalize(pre, norm_gain, norm_shift):
    element_count = pre.shape[0] * pre.shape[2] * pre.shape[3]
    mean = lax.optimization_barrier(jnp.sum(pre, axis=(0, 2, 3))) / element_count
    centred_input = pre - mean[None, :, None, None]
    variance = lax.optimization_barrier(jnp.sum(centred_input * centred_input, axis=(0, 2, 3))) / element_count
    inverse_deviation = lax.rsqrt(variance + norm_epsilon)
    normalized_input = centred_input * inverse_deviation[None, :, None, None]
    return (normalized_input, inverse_deviation, norm_gain[None, :, None, None] * normalized_input + norm_shift[None, :, None, None])

def batch_normalize_backward(upstream_gradient, normalized_input, inverse_deviation, norm_gain):
    element_count = upstream_gradient.shape[0] * upstream_gradient.shape[2] * upstream_gradient.shape[3]
    gain_gradient = lax.optimization_barrier(jnp.sum(upstream_gradient * normalized_input, axis=(0, 2, 3)))
    shift_gradient = lax.optimization_barrier(jnp.sum(upstream_gradient, axis=(0, 2, 3)))
    scale_factor = (norm_gain * inverse_deviation)[None, :, None, None]
    preact_gradient = scale_factor * (upstream_gradient - shift_gradient[None, :, None, None] / element_count - normalized_input * gain_gradient[None, :, None, None] / element_count)
    return (preact_gradient.astype(jnp.bfloat16), jnp.stack([gain_gradient, shift_gradient]))

def reference(latent, first_weight, first_norm_gain, first_norm_shift, second_weight, second_norm_gain, second_norm_shift, cotangent):
    first_preactivation = expand(latent, first_weight, H0, W0)
    first_normalized_input, first_inverse_deviation, first_norm_output = batch_normalize(first_preactivation, first_norm_gain, first_norm_shift)
    act_one = activate(first_norm_output).astype(jnp.bfloat16)
    second_preactivation = expand(act_one, second_weight, 2 * H0, 2 * W0)
    second_normalized_input, second_inverse_deviation, second_norm_output = batch_normalize(second_preactivation, second_norm_gain, second_norm_shift)
    features = activate(second_norm_output).astype(jnp.bfloat16)
    second_block_gradient = cotangent.astype(jnp.float32) * activate_slope(second_norm_output)
    second_preact_gradient, second_batchnorm_gradients = batch_normalize_backward(second_block_gradient, second_normalized_input, second_inverse_deviation, second_norm_gain)
    act_grad, second_weight_grad = adjoint(second_preact_gradient, act_one, second_weight, 2 * H0, 2 * W0)
    first_block_gradient = act_grad * activate_slope(first_norm_output)
    first_preact_gradient, first_batchnorm_gradients = batch_normalize_backward(first_block_gradient, first_normalized_input, first_inverse_deviation, first_norm_gain)
    latent_grad, first_weight_grad = adjoint(first_preact_gradient, latent, first_weight, H0, W0)
    return (features, latent_grad, first_weight_grad, second_weight_grad, first_batchnorm_gradients, second_batchnorm_gradients)
```

```python
import jax
import jax.numpy as jnp
from jax import lax
from jax.sharding import PartitionSpec as P

H0 = 4
W0 = 64


norm_epsilon = 1e-05
PHASE_TAPS = (((1, 1), (3, 0)), ((0, 2), (2, 1)))


GROUP = ("space", "rep")


def group_size():
    return lax.axis_size("space") * lax.axis_size("rep")


def group_sum(values):
    count = group_size()
    copies = jnp.broadcast_to(values[None], (count,) + values.shape)
    return jnp.sum(lax.all_to_all(copies, GROUP, 0, 0), axis=0)


def exchange_steps():
    steps = []
    for axis in ("rep", "space"):
        bit = 1
        while bit < lax.axis_size(axis):
            steps.append((axis, bit))
            bit *= 2
    return steps


def swap(block, axis, bit):
    return lax.ppermute(block, axis, [(i, i ^ bit) for i in range(lax.axis_size(axis))])


def halving_sum(values):
    steps = exchange_steps()
    part = values
    for axis, bit in steps:
        upper = (lax.axis_index(axis) // bit) % 2
        half = part.shape[0] // 2
        kept = lax.dynamic_slice_in_dim(part, upper * half, half)
        sent = lax.dynamic_slice_in_dim(part, (1 - upper) * half, half).astype(jnp.bfloat16)
        part = kept + swap(sent, axis, bit).astype(jnp.float32)
    part = part.astype(jnp.bfloat16)
    for axis, bit in reversed(steps):
        upper = (lax.axis_index(axis) // bit) % 2
        other = swap(part, axis, bit)
        part = jnp.where(
            upper == 0,
            jnp.concatenate([part, other]),
            jnp.concatenate([other, part]),
        )
    return part.astype(jnp.float32)


def shifted(block, axis, distance):
    devices = range(lax.axis_size(axis))
    route = [(i - distance, i) for i in devices if i - distance in devices]
    return lax.ppermute(block, axis, route)


def with_halo(cells, sides, width):
    for axis, dim in sides:
        count = lax.axis_size(axis)
        ends = count - 1
        head = lax.slice_in_dim(cells, 0, width, axis=dim)
        tail = lax.slice_in_dim(cells, cells.shape[dim] - width, cells.shape[dim], axis=dim)
        cells = jnp.concatenate(
            [
                lax.ppermute(tail, axis, [(i, (i + 1) % count) for i in range(ends)]),
                cells,
                lax.ppermute(head, axis, [((i + 1) % count, i) for i in range(ends)]),
            ],
            axis=dim,
        )
    return cells


def activate(values):
    return values * jax.nn.sigmoid(values)


def activate_slope(values):
    gate = jax.nn.sigmoid(values)
    return gate * (1.0 + values * (1.0 - gate))


def shift_flat(values, row_step, col_step, plane_width):
    offset = row_step * plane_width + col_step
    length = values.shape[-1]
    if offset > 0:
        moved = jnp.concatenate(
            [values[..., offset:], jnp.zeros(values.shape[:-1] + (offset,), values.dtype)], axis=-1
        )
    elif offset < 0:
        moved = jnp.concatenate(
            [
                jnp.zeros(values.shape[:-1] + (-offset,), values.dtype),
                values[..., : length + offset],
            ],
            axis=-1,
        )
    else:
        moved = values
    if col_step != 0:
        column = jnp.arange(length) % plane_width
        inside = (column + col_step >= 0) & (column + col_step < plane_width)
        moved = jnp.where(inside, moved, jnp.zeros((), values.dtype))
    return moved


def assemble(summed, height, plane_width):
    samples, cout = (summed.shape[0], summed.shape[2])
    phase_rows = []
    for row_phase in range(2):
        phase_cols = []
        for col_phase in range(2):
            accum = None
            for row_tap, row_start in PHASE_TAPS[row_phase]:
                for col_tap, col_start in PHASE_TAPS[col_phase]:
                    term = shift_flat(
                        summed[:, 4 * row_tap + col_tap], row_start - 1, col_start - 1, plane_width
                    )
                    accum = term if accum is None else accum + term
            phase_cols.append(accum)
        phase_rows.append(jnp.stack(phase_cols, axis=2))
    stacked = jnp.stack(phase_rows, axis=2)
    stacked = stacked.reshape(samples, cout, 2, 2, height, plane_width).transpose(0, 1, 4, 2, 5, 3)
    return stacked.reshape(samples, cout, 4 * height * plane_width)


def expand_local(padded, weight, first, plane_count, height, plane_width):
    cout, cin = (weight.shape[1], weight.shape[2])
    kernel = weight.reshape(4, 16, cout, cin)
    planes = []
    for offset in range(first, first + plane_count):
        half = offset // 2
        summed = None
        for depth_tap, depth_start in PHASE_TAPS[offset % 2]:
            source = padded[:, :, half + depth_start, :]
            term = jnp.einsum(
                "tok,skh->stoh", kernel[depth_tap], source, preferred_element_type=jnp.float32
            )
            summed = term if summed is None else summed + term
        planes.append(assemble(summed, height, plane_width))
    return jnp.stack(planes, axis=2)


def expand_layer(field, weight, height, plane_width):
    planes = field.shape[2]
    padded = jnp.pad(field, ((0, 0), (0, 0), (1, 1), (0, 0)))
    full = expand_local(padded, weight, -1, 2 * planes + 2, height, plane_width)
    from_below = shifted(full[:, :, -1], "space", 1)
    from_above = shifted(full[:, :, 0], "space", -1)
    inner = full[:, :, 1:-1]
    inner = inner.at[:, :, 0].add(from_below)
    inner = inner.at[:, :, -1].add(from_above)
    return inner


def entry_count(field):
    return (
        field.shape[0]
        * lax.axis_size("rep")
        * field.shape[2]
        * lax.axis_size("space")
        * field.shape[3]
    )


def batch_normalize(pre, norm_gain, norm_shift):
    element_count = entry_count(pre)
    summed = group_sum(jnp.sum(pre, axis=(0, 2, 3)))
    mean = summed / element_count
    centred_input = pre - mean[None, :, None, None]
    variance = (
        group_sum(jnp.sum(centred_input * centred_input, axis=(0, 2, 3)))
        / element_count
    )
    inverse_deviation = lax.rsqrt(variance + norm_epsilon)
    normalized_input = centred_input * inverse_deviation[None, :, None, None]
    return (
        normalized_input,
        inverse_deviation,
        norm_gain[None, :, None, None] * normalized_input + norm_shift[None, :, None, None],
    )


def batch_normalize_backward(upstream_gradient, normalized_input, inverse_deviation, norm_gain):
    element_count = entry_count(upstream_gradient)
    gain_gradient, shift_gradient = group_sum(
        jnp.stack(
            [
                jnp.sum(upstream_gradient * normalized_input, axis=(0, 2, 3)),
                jnp.sum(upstream_gradient, axis=(0, 2, 3)),
            ]
        )
    )
    scale_factor = (norm_gain * inverse_deviation)[None, :, None, None]
    preact_gradient = scale_factor * (
        upstream_gradient
        - shift_gradient[None, :, None, None] / element_count
        - normalized_input * gain_gradient[None, :, None, None] / element_count
    )
    return (preact_gradient.astype(jnp.bfloat16), jnp.stack([gain_gradient, shift_gradient]))


def shrink_layer(upstream_gradient, field, weight, height, plane_width):
    padded = with_halo(upstream_gradient, (("space", 2),), 1)
    samples, cout, depth_padded = (padded.shape[0], padded.shape[1], padded.shape[2])
    cin = field.shape[1]
    kernel = weight.reshape(4, 16, cout, cin)
    phases = padded.reshape(samples, cout, depth_padded, height, 2, plane_width, 2)
    phases = phases.transpose(0, 1, 2, 4, 6, 3, 5).reshape(
        samples, cout, depth_padded, 2, 2, height * plane_width
    )
    kernel_parts = [None, None, None, None]
    field_planes = []
    for plane_index in range(field.shape[2]):
        source = field[:, :, plane_index, :]
        plane_grad = None
        for depth_tap in range(4):
            grad_phases = phases[:, :, 2 * plane_index + depth_tap]
            windows = []
            for row_tap in range(4):
                for col_tap in range(4):
                    windows.append(
                        shift_flat(
                            grad_phases[:, :, (row_tap + 1) % 2, (col_tap + 1) % 2],
                            (row_tap - 1) // 2,
                            (col_tap - 1) // 2,
                            plane_width,
                        )
                    )
            stacked = jnp.stack(windows, axis=1)
            term = jnp.einsum(
                "tok,stoh->skh", kernel[depth_tap], stacked, preferred_element_type=jnp.float32
            )
            part_kernel = jnp.einsum(
                "stoh,skh->tok", stacked, source, preferred_element_type=jnp.float32
            )
            plane_grad = term if plane_grad is None else plane_grad + term
            kernel_parts[depth_tap] = (
                part_kernel
                if kernel_parts[depth_tap] is None
                else kernel_parts[depth_tap] + part_kernel
            )
        field_planes.append(plane_grad)
    return (jnp.stack(field_planes, axis=2), jnp.stack(kernel_parts).reshape(64, cout, cin))


def local(
    latent,
    first_weight,
    first_norm_gain,
    first_norm_shift,
    second_weight,
    second_norm_gain,
    second_norm_shift,
    cotangent,
):
    first_preactivation = expand_layer(latent, first_weight, H0, W0)
    first_normalized_input, first_inverse_deviation, first_norm_output = batch_normalize(
        first_preactivation, first_norm_gain, first_norm_shift
    )
    act_one = activate(first_norm_output).astype(jnp.bfloat16)
    second_preactivation = expand_layer(act_one, second_weight, 2 * H0, 2 * W0)
    second_normalized_input, second_inverse_deviation, second_norm_output = batch_normalize(
        second_preactivation, second_norm_gain, second_norm_shift
    )
    features = activate(second_norm_output).astype(jnp.bfloat16)
    second_block_gradient = cotangent.astype(jnp.float32) * activate_slope(second_norm_output)
    second_preact_gradient, second_batchnorm_gradients = batch_normalize_backward(
        second_block_gradient, second_normalized_input, second_inverse_deviation, second_norm_gain
    )
    act_grad, second_local = shrink_layer(
        second_preact_gradient, act_one, second_weight, 2 * H0, 2 * W0
    )
    first_block_gradient = act_grad * activate_slope(first_norm_output)
    first_preact_gradient, first_batchnorm_gradients = batch_normalize_backward(
        first_block_gradient, first_normalized_input, first_inverse_deviation, first_norm_gain
    )
    latent_grad, first_local = shrink_layer(first_preact_gradient, latent, first_weight, H0, W0)
    second_weight_grad = halving_sum(second_local.reshape(-1, 128)).reshape(second_local.shape)
    first_weight_grad = halving_sum(first_local.reshape(-1, 128)).reshape(first_local.shape)
    return (
        features,
        latent_grad,
        first_weight_grad,
        second_weight_grad,
        first_batchnorm_gradients,
        second_batchnorm_gradients,
    )


def solution(mesh):
    in_specs = (
        P(("group", "rep"), None, "space", None),
        P(),
        P(),
        P(),
        P(),
        P(),
        P(),
        P(("group", "rep"), None, "space", None),
    )
    out_specs = (
        P(("group", "rep"), None, "space", None),
        P(("group", "rep"), None, "space", None),
        P("group", None, None),
        P("group", None, None),
        P("group", None),
        P("group", None),
    )
    return jax.shard_map(local, mesh=mesh, in_specs=in_specs, out_specs=out_specs, check_vma=False)
```

```python
import jax
import jax.numpy as jnp
from jax import lax
from jax.experimental import pallas as pl
from jax.experimental.pallas import tpu as pltpu
from jax.sharding import PartitionSpec as P

H0 = 4
W0 = 64
CELLS = H0 * W0
C0 = 128
C1 = 64
C2 = 32
EPSILON = 1e-05

F32 = jnp.float32
BF16 = jnp.bfloat16
GROUP = ("space", "rep")

PHASE_TAPS = (((1, 0), (3, -1)), ((2, 0), (0, 1)))
TAP_PHASES = ((1, -1), (0, 0), (1, 0), (0, 1))
FINE_STEPS = {
    (0, -1): (1, -1),
    (0, 0): (0, 0),
    (0, 1): (1, 0),
    (1, -1): (0, 0),
    (1, 0): (1, 0),
    (1, 1): (0, 1),
}


def group_size():
    return lax.axis_size("space") * lax.axis_size("rep")


def exchange_steps():
    steps = []
    for axis in ("rep", "space"):
        bit = 1
        while bit < lax.axis_size(axis):
            steps.append((axis, bit))
            bit *= 2
    return steps


def swap(block, axis, bit):
    return lax.ppermute(block, axis, [(i, i ^ bit) for i in range(lax.axis_size(axis))])


def halving_sum(values):
    steps = exchange_steps()
    part = values
    for axis, bit in steps:
        upper = (lax.axis_index(axis) // bit) % 2
        half = part.shape[0] // 2
        kept = lax.dynamic_slice_in_dim(part, upper * half, half)
        sent = lax.dynamic_slice_in_dim(part, (1 - upper) * half, half).astype(BF16)
        part = kept + swap(sent, axis, bit).astype(F32)
    part = part.astype(BF16)
    for axis, bit in reversed(steps):
        upper = (lax.axis_index(axis) // bit) % 2
        other = swap(part, axis, bit)
        part = jnp.where(
            upper == 0,
            jnp.concatenate([part, other]),
            jnp.concatenate([other, part]),
        )
    return part.astype(F32)


def exchange(copies):
    return lax.all_to_all(copies, GROUP, 0, 0)


def to_above(block):
    count = lax.axis_size("space")
    return lax.ppermute(block, "space", [(i, i + 1) for i in range(count - 1)])


def to_below(block):
    count = lax.axis_size("space")
    return lax.ppermute(block, "space", [(i + 1, i) for i in range(count - 1)])


def call(kernel, outs, args, scratch=()):
    return pl.pallas_call(
        kernel,
        out_shape=[jax.ShapeDtypeStruct(shape, dtype) for shape, dtype in outs],
        in_specs=[pl.BlockSpec(memory_space=pltpu.VMEM)] * len(args),
        out_specs=[pl.BlockSpec(memory_space=pltpu.VMEM)] * len(outs),
        scratch_shapes=list(scratch),
        compiler_params=pltpu.CompilerParams(vmem_limit_bytes=48 * 2**20),
        cost_estimate=pl.CostEstimate(flops=10**9, bytes_accessed=4 * 10**6, transcendentals=0),
    )(*args)


def matmul(a, b):
    return jnp.dot(a, b, preferred_element_type=F32)


def matmul_nt(a, b):
    return lax.dot_general(a, b, (((1,), (1,)), ((), ())), preferred_element_type=F32)


def shift_matrix(dj, dl):
    src = lax.broadcasted_iota(jnp.int32, (CELLS, CELLS), 0)
    dst = lax.broadcasted_iota(jnp.int32, (CELLS, CELLS), 1)
    col = dst % W0 + dl
    hit = (src == dst + dj * W0 + dl) & (col >= 0) & (col < W0)
    return jnp.where(hit, 1.0, 0.0).astype(BF16)


def shift_slot(dj, dl):
    return slice(((dj + 1) * 3 + dl + 1) * CELLS, ((dj + 1) * 3 + dl + 2) * CELLS)


def spread_matrix():
    src = lax.broadcasted_iota(jnp.int32, (512, 512), 0)
    dst = lax.broadcasted_iota(jnp.int32, (512, 512), 1)
    cp2, cp, jj, l = dst // 256, (dst // 128) % 2, (dst // 64) % 2, dst % 64
    return jnp.where(src == jj * 256 + 4 * l + 2 * cp + cp2, 1.0, 0.0).astype(BF16)


def columns(rows):
    return jnp.transpose(jnp.concatenate([rows, jnp.zeros((120, 128), F32)], axis=0))


def emit_rows(ref, first, second):
    lane = lax.broadcasted_iota(jnp.int32, (first.shape[0], 128), 1)
    tile = jnp.where(lane == 0, first, jnp.where(lane == 1, second, 0.0))
    tile = jnp.concatenate([tile] * (128 // first.shape[0]), axis=0)
    rows = jnp.transpose(tile)[0:8, :]
    for k in range(ref.shape[0]):
        ref[k] = rows


def fold(rows, channels):
    total = rows[0:channels]
    for k in range(1, rows.shape[0] // channels):
        total = total + rows[k * channels : (k + 1) * channels]
    return total


def moments(copies, local_count):
    count = copies.shape[0]
    sums = jnp.sum(copies, axis=0)
    mean = sums[0:1] / count
    away = copies - mean[None]
    spread = jnp.sum(away * away, axis=0)[0:1]
    variance = (sums[1:2] + local_count * spread) / (count * local_count)
    return mean, lax.rsqrt(variance + EPSILON)


def sigmoid(values):
    return 1.0 / (1.0 + jnp.exp(-values))


def prepare_kernel(w1_ref, w2_ref, a1_ref, a2_ref, b1_ref, b2_ref, sh_ref):
    for dj in (-1, 0, 1):
        for dl in (-1, 0, 1):
            sh_ref[:, shift_slot(dj, dl)] = shift_matrix(dj, dl)
    a1_ref[...] = jnp.zeros(a1_ref.shape, BF16)
    for par in range(2):
        for rp in range(2):
            for cp in range(2):
                row2 = par * 4 * C2 + (2 * rp + cp) * C2
                pieces = [jnp.zeros((C2, C1), BF16)] * 18
                for p, dp in PHASE_TAPS[par]:
                    dt = dp + 1 - par
                    for q, dr in PHASE_TAPS[rp]:
                        for r, dc in PHASE_TAPS[cp]:
                            tap = 16 * p + 4 * q + r
                            slot = dt * 9 + (dr + 1) * 3 + dc + 1
                            row = par * 4 * C1 + (2 * rp + cp) * C1
                            a1_ref[row : row + C1, slot * C0 : (slot + 1) * C0] = w1_ref[
                                tap * C1 : (tap + 1) * C1, :
                            ]
                            pieces[slot] = w2_ref[tap * C2 : (tap + 1) * C2, :]
                a2_ref[row2 : row2 + C2, :] = jnp.concatenate(pieces, axis=1)
    eye = jnp.where(
        lax.broadcasted_iota(jnp.int32, (128, 128), 0)
        == lax.broadcasted_iota(jnp.int32, (128, 128), 1),
        1.0,
        0.0,
    ).astype(BF16)

    @pl.loop(0, 8)
    def _(k):
        at = pl.multiple_of(k * 512, 512)
        b1_ref[:, pl.ds(at, 512)] = matmul_nt(eye, w1_ref[pl.ds(at, 512), :]).astype(BF16)

    @pl.loop(0, 4)
    def _(k):
        at = pl.multiple_of(k * 512, 512)
        b2_ref[:, pl.ds(at, 512)] = matmul_nt(eye[0:C1, 0:C1], w2_ref[pl.ds(at, 512), :]).astype(
            BF16
        )


def first_kernel(lat_ref, below_ref, above_ref, a1_ref, sh_ref, pre_ref, out_ref, x_ref):
    planes = jnp.concatenate([below_ref[...], lat_ref[...], above_ref[...]], axis=0)
    for k in range(9):
        moved = matmul(planes, sh_ref[:, k * CELLS : (k + 1) * CELLS]).astype(BF16)
        for z in range(3):
            at = (z * 9 + k) * C0
            x_ref[at : at + C0, :] = moved[z * C0 : (z + 1) * C0]
    for m in range(2):
        both = matmul(a1_ref[...], x_ref[m * 9 * C0 : (m + 2) * 9 * C0, :])
        pre_ref[2 * m + 1] = both[0 : 4 * C1]
        pre_ref[2 * m] = both[4 * C1 : 8 * C1]
    lower, upper = pre_ref[1], pre_ref[2]
    sums = fold(jnp.sum(lower + upper, axis=1, keepdims=True), C1)
    mean = sums / (8 * CELLS)
    wide = jnp.concatenate([mean] * 4, axis=0)
    lower, upper = lower - wide, upper - wide
    squares = fold(jnp.sum(lower * lower + upper * upper, axis=1, keepdims=True), C1)
    emit_rows(out_ref, mean, squares)


def second_kernel(got_ref, pre1_ref, p1_ref, a2_ref, sh_ref, pre_ref, act_ref, st_ref, out_ref, x_ref):
    mean, scale = moments(got_ref[...], 8 * CELLS)
    st = jnp.concatenate([mean, scale, p1_ref[0:6]], axis=0)
    st_ref[...] = st
    cols = columns(st)
    mean, scale, gain, shift = (cols[0:C1, k : k + 1] for k in range(4))
    keeps = (cols[0:C1, 4:5], None, None, cols[0:C1, 5:6])
    for q in range(4):
        for block in range(4):
            rp, cp = block // 2, block % 2
            norm = gain * ((pre1_ref[q, block * C1 : (block + 1) * C1, :] - mean) * scale) + shift
            act = norm * sigmoid(norm)
            if keeps[q] is not None:
                act = act * keeps[q]
            act = act.astype(BF16)
            if q in (1, 2):
                act_ref[q - 1, :, block * CELLS : (block + 1) * CELLS] = act
            sj, sl = 1 - 2 * rp, 1 - 2 * cp
            moved = {(0, 0): act}
            for dj, dl in ((sj, 0), (0, sl), (sj, sl)):
                moved[dj, dl] = matmul(act, sh_ref[:, shift_slot(dj, dl)]).astype(BF16)
            for (trp, dr), (srp, dj) in FINE_STEPS.items():
                if srp != rp:
                    continue
                for (tcp, dc), (scp, dl) in FINE_STEPS.items():
                    if scp != cp:
                        continue
                    at = q * 9 * C1 + ((dr + 1) * 3 + dc + 1) * C1
                    lane = (2 * trp + tcp) * CELLS
                    x_ref[at : at + C1, lane : lane + CELLS] = moved[dj, dl]

    for m in range(3):

        @pl.loop(0, 4)
        def _(block):
            lane = pl.multiple_of(block * CELLS, CELLS)
            both = matmul(a2_ref[...], x_ref[m * 9 * C1 : (m + 2) * 9 * C1, pl.ds(lane, CELLS)])
            pre_ref[2 * m + 1, :, pl.ds(lane, CELLS)] = both[0 : 4 * C2]
            pre_ref[2 * m, :, pl.ds(lane, CELLS)] = both[4 * C2 : 8 * C2]

    total = pre_ref[1] + pre_ref[2] + pre_ref[3] + pre_ref[4]
    sums = fold(jnp.sum(total, axis=1, keepdims=True), C2)
    mean = sums / (64 * CELLS)
    wide = jnp.concatenate([mean] * 4, axis=0)
    squares = jnp.zeros((4 * C2, CELLS), F32)
    for t in range(1, 5):
        for block in range(4):
            away = pre_ref[t, :, block * CELLS : (block + 1) * CELLS] - wide
            squares = squares + away * away
    emit_rows(out_ref, mean, fold(jnp.sum(squares, axis=1, keepdims=True), C2))


def spread_kernel(cot_ref, out_ref):
    matrix = spread_matrix()
    count = cot_ref.shape[0] // C2
    for rp in range(2):
        for rp2 in range(2):
            for h in range(2):
                lanes = [(4 * (2 * h + jj) + 2 * rp + rp2) * 256 for jj in range(2)]
                rows = jnp.concatenate([cot_ref[:, at : at + 256] for at in lanes], axis=1)
                moved = matmul(rows, matrix).astype(BF16)
                for cp2 in range(2):
                    for cp in range(2):
                        row = (2 * rp2 + cp2) * C2
                        lane = (2 * rp + cp) * CELLS + h * 128
                        piece = moved[:, cp2 * 256 + cp * 128 : cp2 * 256 + cp * 128 + 128]
                        for t in range(count):
                            out_ref[t, row : row + C2, lane : lane + 128] = piece[
                                t * C2 : (t + 1) * C2
                            ]


def gather_kernel(feat_ref, out_ref):
    matrix = spread_matrix()
    count = feat_ref.shape[0]
    for rp in range(2):
        for rp2 in range(2):
            for h in range(2):
                pieces = []
                for cp2 in range(2):
                    for cp in range(2):
                        row = (2 * rp2 + cp2) * C2
                        lane = (2 * rp + cp) * CELLS + h * 128
                        pieces.append(
                            jnp.concatenate(
                                [
                                    feat_ref[t, row : row + C2, lane : lane + 128]
                                    for t in range(count)
                                ],
                                axis=0,
                            )
                        )
                moved = matmul_nt(jnp.concatenate(pieces, axis=1), matrix).astype(BF16)
                for jj in range(2):
                    at = (4 * (2 * h + jj) + 2 * rp + rp2) * 256
                    out_ref[:, at : at + 256] = moved[:, jj * 256 : (jj + 1) * 256]


def third_kernel(got_ref, pre_ref, cot_ref, p2_ref, grad_ref, feat_ref, st_ref, out_ref):
    mean, scale = moments(got_ref[...], 64 * CELLS)
    st = jnp.concatenate([mean, scale, p2_ref[0:6]], axis=0)
    st_ref[...] = st
    cols = columns(st)
    mean, scale, gain, shift = (cols[:, k : k + 1] for k in range(4))

    def slope(t, lane):
        hat = (pre_ref[t, :, pl.ds(lane, CELLS)] - mean) * scale
        norm = gain * hat + shift
        gate = sigmoid(norm)
        cot = cot_ref[t, :, pl.ds(lane, CELLS)].astype(F32)
        grad = cot * (gate * (1.0 + norm * (1.0 - gate)))
        grad_ref[t, :, pl.ds(lane, CELLS)] = grad
        return hat, norm, gate, grad

    for t in (0, 5):

        @pl.loop(0, 4)
        def _(block):
            slope(t, pl.multiple_of(block * CELLS, CELLS))

    def body(k, carry):
        t = k // 4 + 1
        lane = pl.multiple_of((k % 4) * CELLS, CELLS)
        hat, norm, gate, grad = slope(t, lane)
        feat_ref[t - 1, :, pl.ds(lane, CELLS)] = (norm * gate).astype(BF16)
        return carry[0] + grad * hat, carry[1] + grad

    zero = jnp.zeros((4 * C2, CELLS), F32)
    first, second = lax.fori_loop(0, 16, body, (zero, zero))
    emit_rows(
        out_ref,
        fold(jnp.sum(first, axis=1, keepdims=True), C2),
        fold(jnp.sum(second, axis=1, keepdims=True), C2),
    )


def fourth_kernel(
    got_ref, pre_ref, grad_ref, st2_ref, b2_ref, sh_ref, act_ref, pre1_ref, st1_ref,
    g1_ref, dw_ref, sum_ref, out_ref, x_ref,
):
    sums = jnp.sum(got_ref[...], axis=0)
    sum_ref[...] = sums
    total = got_ref.shape[0] * 64 * CELLS
    cols = columns(jnp.concatenate([st2_ref[0:6], sums[0:2] / total], axis=0))
    mean, scale, gain = (cols[:, k : k + 1] for k in range(3))
    hat_part, part = cols[:, 6:7], cols[:, 7:8]
    keeps = {0: cols[:, 4:5], 5: cols[:, 5:6]}
    for t in range(6):
        factor = gain * scale
        if t in keeps:
            factor = factor * keeps[t]
        for block in range(4):
            rp, cp = block // 2, block % 2
            lanes = slice(block * CELLS, (block + 1) * CELLS)
            hat = (pre_ref[t, :, lanes] - mean) * scale
            dpre = (factor * (grad_ref[t, :, lanes] - part - hat * hat_part)).astype(BF16)
            sj, sl = 1 - 2 * rp, 1 - 2 * cp
            moved = {(0, 0): dpre}
            for dj, dl in ((sj, 0), (0, sl), (sj, sl)):
                moved[dj, dl] = matmul(dpre, sh_ref[:, shift_slot(dj, dl)]).astype(BF16)
            for q, (rp2, dr) in enumerate(TAP_PHASES):
                for r, (cp2, dc) in enumerate(TAP_PHASES):
                    row = (2 * rp2 + cp2) * C2
                    for trp in range(2):
                        for tcp in range(2):
                            srp, dj = FINE_STEPS[trp, dr]
                            scp, dl = FINE_STEPS[tcp, dc]
                            if (srp, scp) != (rp, cp):
                                continue
                            at = t * 16 * C2 + (4 * q + r) * C2
                            lane = (2 * trp + tcp) * CELLS
                            x_ref[at : at + C2, lane : lane + CELLS] = moved[dj, dl][row : row + C2]

    cols = columns(st1_ref[...])
    mean, scale, gain, shift = (cols[0:C1, k : k + 1] for k in range(4))
    first = jnp.zeros((C1, CELLS), F32)
    second = jnp.zeros((C1, CELLS), F32)
    for j in range(2):
        for block in range(4):
            lanes = slice(block * CELLS, (block + 1) * CELLS)
            act_grad = matmul(b2_ref[...], x_ref[j * 32 * C2 : (j + 2) * 32 * C2, lanes])
            hat = (pre1_ref[j + 1, block * C1 : (block + 1) * C1, :] - mean) * scale
            norm = gain * hat + shift
            gate = sigmoid(norm)
            grad = act_grad * (gate * (1.0 + norm * (1.0 - gate)))
            g1_ref[j, block * C1 : (block + 1) * C1, :] = grad
            first = first + grad * hat
            second = second + grad
    emit_rows(
        out_ref,
        jnp.sum(first, axis=1, keepdims=True),
        jnp.sum(second, axis=1, keepdims=True),
    )
    for p in range(4):
        part = matmul_nt(x_ref[p * 16 * C2 : (p + 1) * 16 * C2, :], act_ref[0])
        part = part + matmul_nt(x_ref[(p + 2) * 16 * C2 : (p + 3) * 16 * C2, :], act_ref[1])
        dw_ref[p * 16 * C2 : (p + 1) * 16 * C2, :] = part


def first_dpre(grad, pre, cols, keep):
    mean, scale, gain = (cols[0:C1, k : k + 1] for k in range(3))
    hat_part, part = cols[0:C1, 6:7], cols[0:C1, 7:8]
    factor = gain * scale
    if keep is not None:
        factor = factor * keep
    return (factor * (grad - part - (pre - mean) * scale * hat_part)).astype(BF16)


def first_windows(x_ref, base, grad_ref, pre_ref, cols, keep, sh_ref):
    for block in range(4):
        rp, cp = block // 2, block % 2
        rows = slice(block * C1, (block + 1) * C1)
        dpre = first_dpre(grad_ref[rows, :].astype(F32), pre_ref[rows, :], cols, keep)
        for q, (trp, dj) in enumerate(TAP_PHASES):
            for r, (tcp, dl) in enumerate(TAP_PHASES):
                if (trp, tcp) != (rp, cp):
                    continue
                moved = dpre
                if (dj, dl) != (0, 0):
                    moved = matmul(dpre, sh_ref[:, shift_slot(dj, dl)]).astype(BF16)
                at = base + (4 * q + r) * C1
                x_ref[at : at + C1, :] = moved


def fifth_kernel(
    got_ref, g1_ref, pre1_ref, st1_ref, sh_ref, lat_ref, below_ref, above_ref, dw_ref, sum_ref, x_ref
):
    sums = jnp.sum(got_ref[...], axis=0)
    sum_ref[...] = sums
    total = got_ref.shape[0] * 8 * CELLS
    cols = columns(jnp.concatenate([st1_ref[0:6], sums[0:2] / total], axis=0))
    for j in range(2):
        first_windows(
            x_ref, j * 16 * C1, g1_ref.at[j], pre1_ref.at[j + 1], cols, None, sh_ref
        )
    for p, j, field in ((0, 1, above_ref), (1, 0, lat_ref), (2, 1, lat_ref), (3, 0, below_ref)):
        for half in range(2):
            at = p * 16 * C1 + half * 8 * C1
            src = j * 16 * C1 + half * 8 * C1
            dw_ref[at : at + 8 * C1, :] = matmul_nt(x_ref[src : src + 8 * C1, :], field[...])


def sixth_kernel(
    sum_ref, low_ref, high_ref, pre1_ref, st1_ref, sh_ref, b1_ref, own_ref, count_ref, out_ref, x_ref
):
    total = count_ref.shape[0] * 8 * CELLS
    cols = columns(jnp.concatenate([st1_ref[0:6], sum_ref[0:2] / total], axis=0))
    keeps = (cols[0:C1, 4:5], cols[0:C1, 5:6])
    first_windows(x_ref, 0, low_ref, pre1_ref.at[0], cols, keeps[0], sh_ref)
    first_windows(x_ref, 16 * C1, high_ref, pre1_ref.at[3], cols, keeps[1], sh_ref)
    grad = matmul(b1_ref[:, 0 : 16 * C1], x_ref[0 : 16 * C1, :])
    grad = grad + matmul(b1_ref[:, 16 * C1 : 48 * C1], own_ref[...])
    out_ref[...] = grad + matmul(b1_ref[:, 48 * C1 : 64 * C1], x_ref[16 * C1 : 32 * C1, :])


def local(
    latent,
    first_weight,
    first_norm_gain,
    first_norm_shift,
    second_weight,
    second_norm_gain,
    second_norm_shift,
    cotangent,
):
    count = group_size()
    place = lax.axis_index("space")
    below_is = jnp.full((128,), place > 0, F32)
    above_is = jnp.full((128,), place < lax.axis_size("space") - 1, F32)
    blank = jnp.zeros((128,), F32)
    p1 = jnp.stack(
        [jnp.tile(first_norm_gain, 2), jnp.tile(first_norm_shift, 2), below_is, above_is]
        + [blank] * 4
    )
    p2 = jnp.stack(
        [jnp.tile(second_norm_gain, 4), jnp.tile(second_norm_shift, 4), below_is, above_is]
        + [blank] * 4
    )
    lat = latent.reshape(C0, CELLS)
    lat_below = to_above(lat)
    lat_above = to_below(lat)
    cot = cotangent.reshape(C2, 4, 16 * CELLS).transpose(1, 0, 2)
    cot_below = to_above(cot[3])
    cot_above = to_below(cot[0])
    w1 = first_weight.reshape(64 * C1, C0)
    w2 = second_weight.reshape(64 * C2, C1)
    a1, a2, b1, b2, sh = call(
        prepare_kernel,
        [
            ((8 * C1, 18 * C0), BF16),
            ((8 * C2, 18 * C1), BF16),
            ((C0, 64 * C1), BF16),
            ((C1, 64 * C2), BF16),
            ((CELLS, 9 * CELLS), BF16),
        ],
        [w1, w2],
    )
    stats = ((count, 8, 128), F32)
    pre1, out = call(
        first_kernel,
        [((4, 4 * C1, CELLS), F32), stats],
        [lat, lat_below, lat_above, a1, sh],
        [pltpu.VMEM((27 * C0, CELLS), BF16)],
    )
    (spread,) = call(
        spread_kernel,
        [((6, 4 * C2, 4 * CELLS), BF16)],
        [jnp.concatenate([cot_below[None], cot, cot_above[None]]).reshape(6 * C2, 16 * CELLS)],
    )
    got = exchange(out)
    pre2, act, st1, out = call(
        second_kernel,
        [((6, 4 * C2, 4 * CELLS), F32), ((2, C1, 4 * CELLS), BF16), ((8, 128), F32), stats],
        [got, pre1, p1, a2, sh],
        [pltpu.VMEM((36 * C1, 4 * CELLS), BF16)],
    )
    got = exchange(out)
    grad2, feat, st2, out = call(
        third_kernel,
        [
            ((6, 4 * C2, 4 * CELLS), F32),
            ((4, 4 * C2, 4 * CELLS), BF16),
            ((8, 128), F32),
            stats,
        ],
        [got, pre2, spread, p2],
    )
    got = exchange(out)
    grad1, dw2, sum2, out = call(
        fourth_kernel,
        [((2, 4 * C1, CELLS), F32), ((64 * C2, C1), F32), ((8, 128), F32), stats],
        [got, pre2, grad2, st2, b2, sh, act, pre1, st1],
        [pltpu.VMEM((96 * C2, 4 * CELLS), BF16)],
    )
    grad_below = to_above(grad1[1])
    grad_above = to_below(grad1[0])
    got = exchange(out)
    dw1, sum1, windows = call(
        fifth_kernel,
        [((64 * C1, C0), F32), ((8, 128), F32), ((32 * C1, CELLS), BF16)],
        [got, grad1, pre1, st1, sh, lat, lat_below, lat_above],
    )
    (latent_grad,) = call(
        sixth_kernel,
        [((C0, CELLS), F32)],
        [sum1, grad_below, grad_above, pre1, st1, sh, b1, windows, got],
        [pltpu.VMEM((32 * C1, CELLS), BF16)],
    )
    (features,) = call(gather_kernel, [((4 * C2, 16 * CELLS), BF16)], [feat])
    features = features.reshape(4, C2, 16 * CELLS).transpose(1, 0, 2)
    second_weight_grad = halving_sum(dw2.reshape(-1, 128)).reshape(64, C2, C1)
    first_weight_grad = halving_sum(dw1).reshape(64, C1, C0)
    return (
        features[None],
        latent_grad.reshape(1, C0, 1, CELLS),
        first_weight_grad,
        second_weight_grad,
        sum1[0:2, 0:C1],
        sum2[0:2, 0:C2],
    )


def solution(mesh):
    volume = P(("group", "rep"), None, "space", None)
    in_specs = (volume, P(), P(), P(), P(), P(), P(), volume)
    out_specs = (
        volume,
        volume,
        P("group", None, None),
        P("group", None, None),
        P("group", None),
        P("group", None),
    )
    return jax.shard_map(local, mesh=mesh, in_specs=in_specs, out_specs=out_specs, check_vma=False)
```

```python
import jax
import jax.numpy as jnp
from jax import lax
from jax.experimental import pallas as pl
from jax.experimental.pallas import tpu as pltpu
from jax.sharding import PartitionSpec as P

H0 = 4
W0 = 64
CELLS = H0 * W0
C0 = 128
C1 = 64
C2 = 32
EPSILON = 1e-05

F32 = jnp.float32
BF16 = jnp.bfloat16
GROUP = ("space", "rep")

PHASE_TAPS = (((1, 0), (3, -1)), ((2, 0), (0, 1)))
TAP_PHASES = ((1, -1), (0, 0), (1, 0), (0, 1))
FINE_STEPS = {
    (0, -1): (1, -1),
    (0, 0): (0, 0),
    (0, 1): (1, 0),
    (1, -1): (0, 0),
    (1, 0): (1, 0),
    (1, 1): (0, 1),
}


def group_size():
    return lax.axis_size("space") * lax.axis_size("rep")


def swap(block, axis, bit):
    return lax.ppermute(block, axis, [(i, i ^ bit) for i in range(lax.axis_size(axis))])


def chunk_steps():
    bits = []
    bit = 1
    while bit < lax.axis_size("space"):
        bits.append(("space", bit))
        bit *= 2
    return bits, bits[1:2] + bits[0:1] + bits[2:]


def halve(part, axis, bit):
    upper = (lax.axis_index(axis) // bit) % 2
    half = part.shape[0] // 2
    kept = lax.dynamic_slice_in_dim(part, upper * half, half)
    sent = lax.dynamic_slice_in_dim(part, (1 - upper) * half, half).astype(BF16)
    return kept + swap(sent, axis, bit).astype(F32)


def double(part, axis, bit):
    upper = (lax.axis_index(axis) // bit) % 2
    other = swap(part, axis, bit)
    return jnp.where(
        upper == 0, jnp.concatenate([part, other]), jnp.concatenate([other, part])
    )


def space_sums(parts):
    orders = chunk_steps()
    for step in range(len(orders[0])):
        parts = [halve(part, *order[step]) for part, order in zip(parts, orders)]
    parts = [part.astype(BF16) for part in parts]
    for step in reversed(range(len(orders[0]))):
        parts = [double(part, *order[step]) for part, order in zip(parts, orders)]
    return parts


def exchange(copies):
    return lax.all_to_all(copies, GROUP, 0, 0)


def to_above(block):
    count = lax.axis_size("space")
    return lax.ppermute(block, "space", [(i, i + 1) for i in range(count - 1)])


def to_below(block):
    count = lax.axis_size("space")
    return lax.ppermute(block, "space", [(i + 1, i) for i in range(count - 1)])


def call(kernel, outs, args, scratch=()):
    return pl.pallas_call(
        kernel,
        out_shape=[jax.ShapeDtypeStruct(shape, dtype) for shape, dtype in outs],
        in_specs=[pl.BlockSpec(memory_space=pltpu.VMEM)] * len(args),
        out_specs=[pl.BlockSpec(memory_space=pltpu.VMEM)] * len(outs),
        scratch_shapes=list(scratch),
        compiler_params=pltpu.CompilerParams(vmem_limit_bytes=24 * 2**20),
        cost_estimate=pl.CostEstimate(flops=10**9, bytes_accessed=4 * 10**6, transcendentals=0),
    )(*args)


def matmul(a, b):
    return jnp.dot(a, b, preferred_element_type=F32)


def matmul_nt(a, b):
    return lax.dot_general(a, b, (((1,), (1,)), ((), ())), preferred_element_type=F32)


def shift_matrix(dj, dl):
    src = lax.broadcasted_iota(jnp.int32, (CELLS, CELLS), 0)
    dst = lax.broadcasted_iota(jnp.int32, (CELLS, CELLS), 1)
    col = dst % W0 + dl
    hit = (src == dst + dj * W0 + dl) & (col >= 0) & (col < W0)
    return jnp.where(hit, 1.0, 0.0).astype(BF16)


def shift_slot(dj, dl):
    return slice(((dj + 1) * 3 + dl + 1) * CELLS, ((dj + 1) * 3 + dl + 2) * CELLS)


def spread_matrix():
    src = lax.broadcasted_iota(jnp.int32, (512, 512), 0)
    dst = lax.broadcasted_iota(jnp.int32, (512, 512), 1)
    cp2, cp, jj, l = dst // 256, (dst // 128) % 2, (dst // 64) % 2, dst % 64
    return jnp.where(src == jj * 256 + 4 * l + 2 * cp + cp2, 1.0, 0.0).astype(BF16)


def columns(rows):
    return jnp.transpose(jnp.concatenate([rows, jnp.zeros((120, 128), F32)], axis=0))


def emit_rows(ref, first, second):
    lane = lax.broadcasted_iota(jnp.int32, (first.shape[0], 128), 1)
    tile = jnp.where(lane == 0, first, jnp.where(lane == 1, second, 0.0))
    tile = jnp.concatenate([tile] * (128 // first.shape[0]), axis=0)
    rows = jnp.transpose(tile)[0:8, :]
    for k in range(ref.shape[0]):
        ref[k] = rows


def fold(rows, channels):
    total = rows[0:channels]
    for k in range(1, rows.shape[0] // channels):
        total = total + rows[k * channels : (k + 1) * channels]
    return total


def moments(copies, local_count):
    count = copies.shape[0]
    sums = jnp.sum(copies, axis=0)
    mean = sums[0:1] / count
    away = copies - mean[None]
    spread = jnp.sum(away * away, axis=0)[0:1]
    variance = (sums[1:2] + local_count * spread) / (count * local_count)
    return mean, lax.rsqrt(variance + EPSILON)


def sigmoid(values):
    return 1.0 / (1.0 + jnp.exp(-values))


def spread_planes(cot_ref, out_ref, planes):
    matrix = spread_matrix()
    for rp in range(2):
        for rp2 in range(2):
            for h in range(2):
                lanes = [(4 * (2 * h + jj) + 2 * rp + rp2) * 256 for jj in range(2)]
                rows = jnp.concatenate(
                    [cot_ref[0 : len(planes) * C2, at : at + 256] for at in lanes], axis=1
                )
                moved = matmul(rows, matrix).astype(BF16)
                for cp2 in range(2):
                    for cp in range(2):
                        row = (2 * rp2 + cp2) * C2
                        lane = (2 * rp + cp) * CELLS + h * 128
                        piece = moved[:, cp2 * 256 + cp * 128 : cp2 * 256 + cp * 128 + 128]
                        for k, t in enumerate(planes):
                            out_ref[t, row : row + C2, lane : lane + 128] = piece[
                                k * C2 : (k + 1) * C2
                            ]


def prepare_kernel(
    w1_ref, w2_ref, gain1_ref, shift1_ref, gain2_ref, shift2_ref, cot_ref,
    a1_ref, a2_ref, b1_ref, b2_ref, sh_ref, p1_ref, p2_ref, spread_ref,
):
    place = lax.axis_index("space")
    below = jnp.where(place > 0, 1.0, 0.0)
    above = jnp.where(place < lax.axis_size("space") - 1, 1.0, 0.0)
    edges = [jnp.full((1, 128), below, F32), jnp.full((1, 128), above, F32)]
    blank = [jnp.zeros((4, 128), F32)]
    p1_ref[...] = jnp.concatenate(
        [jnp.concatenate([ref[...]] * 2, axis=1) for ref in (gain1_ref, shift1_ref)] + edges + blank
    )
    p2_ref[...] = jnp.concatenate(
        [jnp.concatenate([ref[...]] * 4, axis=1) for ref in (gain2_ref, shift2_ref)] + edges + blank
    )
    spread_planes(cot_ref, spread_ref, range(4))
    for dj in (-1, 0, 1):
        for dl in (-1, 0, 1):
            sh_ref[:, shift_slot(dj, dl)] = shift_matrix(dj, dl)
    a1_ref[...] = jnp.zeros(a1_ref.shape, BF16)
    for par in range(2):
        for rp in range(2):
            for cp in range(2):
                row2 = par * 4 * C2 + (2 * rp + cp) * C2
                pieces = [jnp.zeros((C2, C1), BF16)] * 18
                for p, dp in PHASE_TAPS[par]:
                    dt = dp + 1 - par
                    for q, dr in PHASE_TAPS[rp]:
                        for r, dc in PHASE_TAPS[cp]:
                            tap = 16 * p + 4 * q + r
                            slot = dt * 9 + (dr + 1) * 3 + dc + 1
                            row = par * 4 * C1 + (2 * rp + cp) * C1
                            a1_ref[row : row + C1, slot * C0 : (slot + 1) * C0] = w1_ref[
                                tap * C1 : (tap + 1) * C1, :
                            ]
                            pieces[slot] = w2_ref[tap * C2 : (tap + 1) * C2, :]
                a2_ref[row2 : row2 + C2, :] = jnp.concatenate(pieces, axis=1)
    eye = jnp.where(
        lax.broadcasted_iota(jnp.int32, (128, 128), 0)
        == lax.broadcasted_iota(jnp.int32, (128, 128), 1),
        1.0,
        0.0,
    ).astype(BF16)

    @pl.loop(0, 8)
    def _(k):
        at = pl.multiple_of(k * 512, 512)
        b1_ref[:, pl.ds(at, 512)] = matmul_nt(eye, w1_ref[pl.ds(at, 512), :]).astype(BF16)

    @pl.loop(0, 4)
    def _(k):
        at = pl.multiple_of(k * 512, 512)
        b2_ref[:, pl.ds(at, 512)] = matmul_nt(eye[0:C1, 0:C1], w2_ref[pl.ds(at, 512), :]).astype(
            BF16
        )


def halo_latent(halo_ref):
    rows = halo_ref[C2 : C2 + 8, :].astype(F32)
    return jnp.concatenate(
        [rows[:, m * CELLS : (m + 1) * CELLS] for m in range(C0 // 8)], axis=0
    ).astype(BF16)


def first_kernel(
    lat_ref, below_ref, above_ref, a1_ref, sh_ref,
    pre_ref, out_ref, spread_ref, near_ref, x_ref,
):
    near_ref[0] = halo_latent(below_ref)
    near_ref[1] = halo_latent(above_ref)
    planes = jnp.concatenate([near_ref[0], lat_ref[...], near_ref[1]], axis=0)
    for k in range(9):
        moved = matmul(planes, sh_ref[:, k * CELLS : (k + 1) * CELLS]).astype(BF16)
        for z in range(3):
            at = (z * 9 + k) * C0
            x_ref[at : at + C0, :] = moved[z * C0 : (z + 1) * C0]
    for m in range(2):
        both = matmul(a1_ref[...], x_ref[m * 9 * C0 : (m + 2) * 9 * C0, :])
        pre_ref[2 * m + 1] = both[0 : 4 * C1]
        pre_ref[2 * m] = both[4 * C1 : 8 * C1]
    lower, upper = pre_ref[1], pre_ref[2]
    sums = fold(jnp.sum(lower + upper, axis=1, keepdims=True), C1)
    mean = sums / (8 * CELLS)
    wide = jnp.concatenate([mean] * 4, axis=0)
    lower, upper = lower - wide, upper - wide
    squares = fold(jnp.sum(lower * lower + upper * upper, axis=1, keepdims=True), C1)
    emit_rows(out_ref, mean, squares)
    spread_planes(below_ref, spread_ref, (0,))
    spread_planes(above_ref, spread_ref, (1,))


def second_kernel(got_ref, pre1_ref, p1_ref, a2_ref, sh_ref, pre_ref, act_ref, st_ref, out_ref, x_ref):
    mean, scale = moments(got_ref[...], 8 * CELLS)
    st = jnp.concatenate([mean, scale, p1_ref[0:6]], axis=0)
    st_ref[...] = st
    cols = columns(st)
    mean, scale, gain, shift = (cols[0:C1, k : k + 1] for k in range(4))
    keeps = (cols[0:C1, 4:5], None, None, cols[0:C1, 5:6])
    for q in range(4):
        for block in range(4):
            rp, cp = block // 2, block % 2
            norm = gain * ((pre1_ref[q, block * C1 : (block + 1) * C1, :] - mean) * scale) + shift
            act = norm * sigmoid(norm)
            if keeps[q] is not None:
                act = act * keeps[q]
            act = act.astype(BF16)
            if q in (1, 2):
                act_ref[q - 1, :, block * CELLS : (block + 1) * CELLS] = act
            sj, sl = 1 - 2 * rp, 1 - 2 * cp
            moved = {(0, 0): act}
            for dj, dl in ((sj, 0), (0, sl), (sj, sl)):
                moved[dj, dl] = matmul(act, sh_ref[:, shift_slot(dj, dl)]).astype(BF16)
            for (trp, dr), (srp, dj) in FINE_STEPS.items():
                if srp != rp:
                    continue
                for (tcp, dc), (scp, dl) in FINE_STEPS.items():
                    if scp != cp:
                        continue
                    at = q * 9 * C1 + ((dr + 1) * 3 + dc + 1) * C1
                    lane = (2 * trp + tcp) * CELLS
                    x_ref[at : at + C1, lane : lane + CELLS] = moved[dj, dl]

    for m in range(3):

        @pl.loop(0, 4)
        def _(block):
            lane = pl.multiple_of(block * CELLS, CELLS)
            both = matmul(a2_ref[...], x_ref[m * 9 * C1 : (m + 2) * 9 * C1, pl.ds(lane, CELLS)])
            pre_ref[2 * m + 1, :, pl.ds(lane, CELLS)] = both[0 : 4 * C2]
            pre_ref[2 * m, :, pl.ds(lane, CELLS)] = both[4 * C2 : 8 * C2]

    total = pre_ref[1] + pre_ref[2] + pre_ref[3] + pre_ref[4]
    sums = fold(jnp.sum(total, axis=1, keepdims=True), C2)
    mean = sums / (64 * CELLS)
    wide = jnp.concatenate([mean] * 4, axis=0)
    squares = jnp.zeros((4 * C2, CELLS), F32)
    for t in range(1, 5):
        for block in range(4):
            away = pre_ref[t, :, block * CELLS : (block + 1) * CELLS] - wide
            squares = squares + away * away
    emit_rows(out_ref, mean, fold(jnp.sum(squares, axis=1, keepdims=True), C2))


def gather_kernel(feat_ref, out_ref):
    matrix = spread_matrix()
    count = feat_ref.shape[0]
    for rp in range(2):
        for rp2 in range(2):
            for h in range(2):
                pieces = []
                for cp2 in range(2):
                    for cp in range(2):
                        row = (2 * rp2 + cp2) * C2
                        lane = (2 * rp + cp) * CELLS + h * 128
                        pieces.append(
                            jnp.concatenate(
                                [
                                    feat_ref[t, row : row + C2, lane : lane + 128]
                                    for t in range(count)
                                ],
                                axis=0,
                            )
                        )
                moved = matmul_nt(jnp.concatenate(pieces, axis=1), matrix).astype(BF16)
                for jj in range(2):
                    at = (4 * (2 * h + jj) + 2 * rp + rp2) * 256
                    out_ref[:, at : at + 256] = moved[:, jj * 256 : (jj + 1) * 256]


def third_kernel(got_ref, pre_ref, cot_ref, edge_ref, p2_ref, grad_ref, feat_ref, st_ref, out_ref):
    mean, scale = moments(got_ref[...], 64 * CELLS)
    st = jnp.concatenate([mean, scale, p2_ref[0:6]], axis=0)
    st_ref[...] = st
    cols = columns(st)
    mean, scale, gain, shift = (cols[:, k : k + 1] for k in range(4))

    def slope(t, lane, cot):
        hat = (pre_ref[t, :, pl.ds(lane, CELLS)] - mean) * scale
        norm = gain * hat + shift
        gate = sigmoid(norm)
        grad = cot.astype(F32) * (gate * (1.0 + norm * (1.0 - gate)))
        grad_ref[t, :, pl.ds(lane, CELLS)] = grad
        return hat, norm, gate, grad

    for k in range(2):

        @pl.loop(0, 4)
        def _(block):
            lane = pl.multiple_of(block * CELLS, CELLS)
            slope(5 * k, lane, edge_ref[k, :, pl.ds(lane, CELLS)])

    def body(k, carry):
        t = k // 4 + 1
        lane = pl.multiple_of((k % 4) * CELLS, CELLS)
        hat, norm, gate, grad = slope(t, lane, cot_ref[t - 1, :, pl.ds(lane, CELLS)])
        feat_ref[t - 1, :, pl.ds(lane, CELLS)] = (norm * gate).astype(BF16)
        return carry[0] + grad * hat, carry[1] + grad

    zero = jnp.zeros((4 * C2, CELLS), F32)
    first, second = lax.fori_loop(0, 16, body, (zero, zero))
    emit_rows(
        out_ref,
        fold(jnp.sum(first, axis=1, keepdims=True), C2),
        fold(jnp.sum(second, axis=1, keepdims=True), C2),
    )


def fourth_kernel(
    got_ref, pre_ref, grad_ref, st2_ref, b2_ref, sh_ref, act_ref, pre1_ref, st1_ref,
    g1_ref, dw_ref, sum_ref, out_ref, x_ref,
):
    sums = jnp.sum(got_ref[...], axis=0)
    sum_ref[...] = sums
    total = got_ref.shape[0] * 64 * CELLS
    cols = columns(jnp.concatenate([st2_ref[0:6], sums[0:2] / total], axis=0))
    mean, scale, gain = (cols[:, k : k + 1] for k in range(3))
    hat_part, part = cols[:, 6:7], cols[:, 7:8]
    keeps = {0: cols[:, 4:5], 5: cols[:, 5:6]}
    for t in range(6):
        factor = gain * scale
        if t in keeps:
            factor = factor * keeps[t]
        for block in range(4):
            rp, cp = block // 2, block % 2
            lanes = slice(block * CELLS, (block + 1) * CELLS)
            hat = (pre_ref[t, :, lanes] - mean) * scale
            dpre = (factor * (grad_ref[t, :, lanes] - part - hat * hat_part)).astype(BF16)
            sj, sl = 1 - 2 * rp, 1 - 2 * cp
            moved = {(0, 0): dpre}
            for dj, dl in ((sj, 0), (0, sl), (sj, sl)):
                moved[dj, dl] = matmul(dpre, sh_ref[:, shift_slot(dj, dl)]).astype(BF16)
            for q, (rp2, dr) in enumerate(TAP_PHASES):
                for r, (cp2, dc) in enumerate(TAP_PHASES):
                    row = (2 * rp2 + cp2) * C2
                    for trp in range(2):
                        for tcp in range(2):
                            srp, dj = FINE_STEPS[trp, dr]
                            scp, dl = FINE_STEPS[tcp, dc]
                            if (srp, scp) != (rp, cp):
                                continue
                            at = t * 16 * C2 + (4 * q + r) * C2
                            lane = (2 * trp + tcp) * CELLS
                            x_ref[at : at + C2, lane : lane + CELLS] = moved[dj, dl][row : row + C2]

    cols = columns(st1_ref[...])
    mean, scale, gain, shift = (cols[0:C1, k : k + 1] for k in range(4))
    first = jnp.zeros((C1, CELLS), F32)
    second = jnp.zeros((C1, CELLS), F32)
    for j in range(2):
        for block in range(4):
            lanes = slice(block * CELLS, (block + 1) * CELLS)
            act_grad = matmul(b2_ref[...], x_ref[j * 32 * C2 : (j + 2) * 32 * C2, lanes])
            hat = (pre1_ref[j + 1, block * C1 : (block + 1) * C1, :] - mean) * scale
            norm = gain * hat + shift
            gate = sigmoid(norm)
            grad = act_grad * (gate * (1.0 + norm * (1.0 - gate)))
            g1_ref[j, block * C1 : (block + 1) * C1, :] = grad
            first = first + grad * hat
            second = second + grad
    emit_rows(
        out_ref,
        jnp.sum(first, axis=1, keepdims=True),
        jnp.sum(second, axis=1, keepdims=True),
    )
    parts = []
    for p in range(4):
        part = matmul_nt(x_ref[p * 16 * C2 : (p + 1) * 16 * C2, :], act_ref[0])
        parts.append(part + matmul_nt(x_ref[(p + 2) * 16 * C2 : (p + 3) * 16 * C2, :], act_ref[1]))
    for p in range(2):
        dw_ref[p * 16 * C2 : (p + 1) * 16 * C2, :] = jnp.concatenate(
            [parts[p], parts[p + 2]], axis=1
        )


def first_dpre(grad, pre, cols, keep):
    mean, scale, gain = (cols[0:C1, k : k + 1] for k in range(3))
    hat_part, part = cols[0:C1, 6:7], cols[0:C1, 7:8]
    factor = gain * scale
    if keep is not None:
        factor = factor * keep
    return (factor * (grad - part - (pre - mean) * scale * hat_part)).astype(BF16)


def first_windows(x_ref, base, grad_ref, pre_ref, cols, keep, sh_ref):
    for block in range(4):
        rp, cp = block // 2, block % 2
        rows = slice(block * C1, (block + 1) * C1)
        dpre = first_dpre(grad_ref[rows, :].astype(F32), pre_ref[rows, :], cols, keep)
        for q, (trp, dj) in enumerate(TAP_PHASES):
            for r, (tcp, dl) in enumerate(TAP_PHASES):
                if (trp, tcp) != (rp, cp):
                    continue
                moved = dpre
                if (dj, dl) != (0, 0):
                    moved = matmul(dpre, sh_ref[:, shift_slot(dj, dl)]).astype(BF16)
                at = base + (4 * q + r) * C1
                x_ref[at : at + C1, :] = moved


def fifth_kernel(
    got_ref, g1_ref, pre1_ref, st1_ref, sh_ref, lat_ref, near_ref, dw2_ref,
    keep_a_ref, keep_b_ref, send_a_ref, send_b_ref, sum_ref, x_ref, dw_ref,
):
    sums = jnp.sum(got_ref[...], axis=0)
    sum_ref[...] = sums
    total = got_ref.shape[0] * 8 * CELLS
    cols = columns(jnp.concatenate([st1_ref[0:6], sums[0:2] / total], axis=0))
    for j in range(2):
        first_windows(
            x_ref, j * 16 * C1, g1_ref.at[j], pre1_ref.at[j + 1], cols, None, sh_ref
        )
    fields = (near_ref[1], lat_ref[...], lat_ref[...], near_ref[0])
    for p, j, field in ((0, 1, fields[0]), (1, 0, fields[1]), (2, 1, fields[2]), (3, 0, fields[3])):
        for half in range(2):
            at = p * 16 * C1 + half * 8 * C1
            src = j * 16 * C1 + half * 8 * C1
            dw_ref[at : at + 8 * C1, :] = matmul_nt(x_ref[src : src + 8 * C1, :], field)
    dw_ref[64 * C1 :, :] = dw2_ref[...]
    chunk = dw_ref.shape[0] // 4
    core = lax.axis_index("rep")
    mine = pl.multiple_of(core * (2 * chunk), 2 * chunk)
    theirs = pl.multiple_of((1 - core) * (2 * chunk), 2 * chunk)
    keep_a_ref[...] = dw_ref[pl.ds(mine, chunk), :]
    keep_b_ref[...] = dw_ref[pl.ds(mine + chunk, chunk), :]
    send_a_ref[...] = dw_ref[pl.ds(theirs, chunk), :].astype(BF16)
    send_b_ref[...] = dw_ref[pl.ds(theirs + chunk, chunk), :].astype(BF16)


def last_kernel(own_a_ref, own_b_ref, other_a_ref, other_b_ref, dw1_ref, dw2_ref, x_ref):
    core = lax.axis_index("rep")
    chunk = own_a_ref.shape[0]
    mine = pl.multiple_of(core * (2 * chunk), 2 * chunk)
    theirs = pl.multiple_of((1 - core) * (2 * chunk), 2 * chunk)
    x_ref[pl.ds(mine, chunk), :] = own_a_ref[...].astype(F32)
    x_ref[pl.ds(mine + chunk, chunk), :] = own_b_ref[...].astype(F32)
    x_ref[pl.ds(theirs, chunk), :] = other_a_ref[...].astype(F32)
    x_ref[pl.ds(theirs + chunk, chunk), :] = other_b_ref[...].astype(F32)
    dw1_ref[...] = x_ref[0 : 64 * C1, :]
    dw2_ref[0 : 32 * C2, :] = x_ref[64 * C1 :, 0:C1]
    dw2_ref[32 * C2 :, :] = x_ref[64 * C1 :, C1:]


def sixth_kernel(
    sum_ref, low_ref, high_ref, pre1_ref, st1_ref, sh_ref, b1_ref, own_ref, count_ref, out_ref, x_ref
):
    total = count_ref.shape[0] * 8 * CELLS
    cols = columns(jnp.concatenate([st1_ref[0:6], sum_ref[0:2] / total], axis=0))
    keeps = (cols[0:C1, 4:5], cols[0:C1, 5:6])
    first_windows(x_ref, 0, low_ref, pre1_ref.at[0], cols, keeps[0], sh_ref)
    first_windows(x_ref, 16 * C1, high_ref, pre1_ref.at[3], cols, keeps[1], sh_ref)
    grad = matmul(b1_ref[:, 0 : 16 * C1], x_ref[0 : 16 * C1, :])
    grad = grad + matmul(b1_ref[:, 16 * C1 : 48 * C1], own_ref[...])
    out_ref[...] = grad + matmul(b1_ref[:, 48 * C1 : 64 * C1], x_ref[16 * C1 : 32 * C1, :])


def local(
    latent,
    first_weight,
    first_norm_gain,
    first_norm_shift,
    second_weight,
    second_norm_gain,
    second_norm_shift,
    cotangent,
):
    count = group_size()
    lat = latent.reshape(C0, CELLS)
    cot = cotangent.reshape(C2, 4, 16 * CELLS)
    low = lat.reshape(C0 // 8, 8, CELLS).transpose(1, 0, 2).reshape(8, 16 * CELLS)
    below = to_above(jnp.concatenate([cot[:, 3], low]))
    above = to_below(jnp.concatenate([cot[:, 0], low]))
    planes = cot.transpose(1, 0, 2).reshape(4 * C2, 16 * CELLS)
    w1 = first_weight.reshape(64 * C1, C0)
    w2 = second_weight.reshape(64 * C2, C1)
    a1, a2, b1, b2, sh, p1, p2, spread = call(
        prepare_kernel,
        [
            ((8 * C1, 18 * C0), BF16),
            ((8 * C2, 18 * C1), BF16),
            ((C0, 64 * C1), BF16),
            ((C1, 64 * C2), BF16),
            ((CELLS, 9 * CELLS), BF16),
            ((8, 128), F32),
            ((8, 128), F32),
            ((4, 4 * C2, 4 * CELLS), BF16),
        ],
        [
            w1,
            w2,
            first_norm_gain.reshape(1, C1),
            first_norm_shift.reshape(1, C1),
            second_norm_gain.reshape(1, C2),
            second_norm_shift.reshape(1, C2),
            planes,
        ],
    )
    stats = ((count, 8, 128), F32)
    pre1, out, edge, near = call(
        first_kernel,
        [
            ((4, 4 * C1, CELLS), F32),
            stats,
            ((2, 4 * C2, 4 * CELLS), BF16),
            ((2, C0, CELLS), BF16),
        ],
        [lat, below, above, a1, sh],
        [pltpu.VMEM((27 * C0, CELLS), BF16)],
    )
    got = exchange(out)
    pre2, act, st1, out = call(
        second_kernel,
        [((6, 4 * C2, 4 * CELLS), F32), ((2, C1, 4 * CELLS), BF16), ((8, 128), F32), stats],
        [got, pre1, p1, a2, sh],
        [pltpu.VMEM((36 * C1, 4 * CELLS), BF16)],
    )
    got = exchange(out)
    grad2, feat, st2, out = call(
        third_kernel,
        [
            ((6, 4 * C2, 4 * CELLS), F32),
            ((4, 4 * C2, 4 * CELLS), BF16),
            ((8, 128), F32),
            stats,
        ],
        [got, pre2, spread, edge, p2],
    )
    got = exchange(out)
    grad1, dw2, sum2, out = call(
        fourth_kernel,
        [((2, 4 * C1, CELLS), F32), ((32 * C2, 2 * C1), F32), ((8, 128), F32), stats],
        [got, pre2, grad2, st2, b2, sh, act, pre1, st1],
        [pltpu.VMEM((96 * C2, 4 * CELLS), BF16)],
    )
    grad_below = to_above(grad1[1])
    grad_above = to_below(grad1[0])
    got = exchange(out)
    rows = (64 * C1 + 32 * C2) // 4
    keep_a, keep_b, send_a, send_b, sum1, windows = call(
        fifth_kernel,
        [
            ((rows, C0), F32),
            ((rows, C0), F32),
            ((rows, C0), BF16),
            ((rows, C0), BF16),
            ((8, 128), F32),
            ((32 * C1, CELLS), BF16),
        ],
        [got, grad1, pre1, st1, sh, lat, near, dw2],
        [pltpu.VMEM((4 * rows, C0), F32)],
    )
    (latent_grad,) = call(
        sixth_kernel,
        [((C0, CELLS), F32)],
        [sum1, grad_below, grad_above, pre1, st1, sh, b1, windows, got],
        [pltpu.VMEM((32 * C1, CELLS), BF16)],
    )
    (features,) = call(gather_kernel, [((4 * C2, 16 * CELLS), BF16)], [feat])
    features = features.reshape(4, C2, 16 * CELLS).transpose(1, 0, 2)
    part_a, part_b = space_sums(
        [
            keep_a + swap(send_a, "rep", 1).astype(F32),
            keep_b + swap(send_b, "rep", 1).astype(F32),
        ]
    )
    first_weight_grad, second_weight_grad = call(
        last_kernel,
        [((64 * C1, C0), F32), ((64 * C2, C1), F32)],
        [part_a, part_b, swap(part_a, "rep", 1), swap(part_b, "rep", 1)],
        [pltpu.VMEM((4 * rows, C0), F32)],
    )
    return (
        features[None],
        latent_grad.reshape(1, C0, 1, CELLS),
        first_weight_grad.reshape(64, C1, C0),
        second_weight_grad.reshape(64, C2, C1),
        sum1[0:2, 0:C1],
        sum2[0:2, 0:C2],
    )


def solution(mesh):
    volume = P(("group", "rep"), None, "space", None)
    in_specs = (volume, P(), P(), P(), P(), P(), P(), volume)
    out_specs = (
        volume,
        volume,
        P("group", None, None),
        P("group", None, None),
        P("group", None),
        P("group", None),
    )
    return jax.shard_map(local, mesh=mesh, in_specs=in_specs, out_specs=out_specs, check_vma=False)
```

```python
import jax
import jax.numpy as jnp
from jax import lax
from jax.experimental import pallas as pl
from jax.experimental.pallas import tpu as pltpu
from jax.sharding import PartitionSpec as P

H0 = 4
W0 = 64
CELLS = H0 * W0
C0 = 128
C1 = 64
C2 = 32
EPSILON = 1e-05

F32 = jnp.float32
BF16 = jnp.bfloat16
GROUP = ("space", "rep")

PHASE_TAPS = (((1, 0), (3, -1)), ((2, 0), (0, 1)))
TAP_PHASES = ((1, -1), (0, 0), (1, 0), (0, 1))
FINE_STEPS = {
    (0, -1): (1, -1),
    (0, 0): (0, 0),
    (0, 1): (1, 0),
    (1, -1): (0, 0),
    (1, 0): (1, 0),
    (1, 1): (0, 1),
}


def group_size():
    return lax.axis_size("space") * lax.axis_size("rep")


def swap(block, axis, bit):
    return lax.ppermute(block, axis, [(i, i ^ bit) for i in range(lax.axis_size(axis))])


def chunk_steps():
    bits = []
    bit = 1
    while bit < lax.axis_size("space"):
        bits.append(("space", bit))
        bit *= 2
    return bits, bits[1:2] + bits[0:1] + bits[2:]


def halve(part, axis, bit):
    upper = (lax.axis_index(axis) // bit) % 2
    half = part.shape[0] // 2
    kept = lax.dynamic_slice_in_dim(part, upper * half, half)
    sent = lax.dynamic_slice_in_dim(part, (1 - upper) * half, half).astype(BF16)
    return kept + swap(sent, axis, bit).astype(F32)


def double(part, axis, bit):
    upper = (lax.axis_index(axis) // bit) % 2
    other = swap(part, axis, bit)
    return jnp.where(
        upper == 0, jnp.concatenate([part, other]), jnp.concatenate([other, part])
    )


def exchange(copies):
    return lax.all_to_all(copies, GROUP, 0, 0)


def is_even():
    return lax.axis_index("space") % 2 == 0


def swap_inner(block):
    return swap(block, "space", 1)


def swap_outer(block):
    count = lax.axis_size("space")
    pairs = [(i, i + 1) for i in range(1, count - 1, 2)]
    return lax.ppermute(block, "space", pairs + [(j, i) for i, j in pairs])


def hold(*values):
    return lax.optimization_barrier(values)


def call(kernel, outs, args, scratch=(), far=(), far_args=()):
    def spec(away):
        return pl.BlockSpec(memory_space=pl.ANY if away else pltpu.VMEM)

    return pl.pallas_call(
        kernel,
        out_shape=[jax.ShapeDtypeStruct(shape, dtype) for shape, dtype in outs],
        in_specs=[spec(k in far_args) for k in range(len(args))],
        out_specs=[spec(k in far) for k in range(len(outs))],
        scratch_shapes=list(scratch),
        compiler_params=pltpu.CompilerParams(vmem_limit_bytes=24 * 2**20),
        cost_estimate=pl.CostEstimate(flops=10**9, bytes_accessed=4 * 10**6, transcendentals=0),
    )(*args)


def matmul(a, b):
    return jnp.dot(a, b, preferred_element_type=F32)


def matmul_nt(a, b):
    return lax.dot_general(a, b, (((1,), (1,)), ((), ())), preferred_element_type=F32)


def shift_matrix(dj, dl):
    src = lax.broadcasted_iota(jnp.int32, (CELLS, CELLS), 0)
    dst = lax.broadcasted_iota(jnp.int32, (CELLS, CELLS), 1)
    col = dst % W0 + dl
    hit = (src == dst + dj * W0 + dl) & (col >= 0) & (col < W0)
    return jnp.where(hit, 1.0, 0.0).astype(BF16)


def shift_slot(dj, dl):
    return slice(((dj + 1) * 3 + dl + 1) * CELLS, ((dj + 1) * 3 + dl + 2) * CELLS)


def spread_matrix():
    src = lax.broadcasted_iota(jnp.int32, (512, 512), 0)
    dst = lax.broadcasted_iota(jnp.int32, (512, 512), 1)
    cp2, cp, jj, l = dst // 256, (dst // 128) % 2, (dst // 64) % 2, dst % 64
    return jnp.where(src == jj * 256 + 4 * l + 2 * cp + cp2, 1.0, 0.0).astype(BF16)


def columns(rows):
    return jnp.transpose(jnp.concatenate([rows, jnp.zeros((120, 128), F32)], axis=0))


def emit_rows(ref, first, second):
    lane = lax.broadcasted_iota(jnp.int32, (first.shape[0], 128), 1)
    tile = jnp.where(lane == 0, first, jnp.where(lane == 1, second, 0.0))
    tile = jnp.concatenate([tile] * (128 // first.shape[0]), axis=0)
    rows = jnp.transpose(tile)[0:8, :]
    for k in range(ref.shape[0]):
        ref[k] = rows


def fold(rows, channels):
    total = rows[0:channels]
    for k in range(1, rows.shape[0] // channels):
        total = total + rows[k * channels : (k + 1) * channels]
    return total


def moments(copies, local_count):
    count = copies.shape[0]
    sums = jnp.sum(copies, axis=0)
    mean = sums[0:1] / count
    away = copies - mean[None]
    spread = jnp.sum(away * away, axis=0)[0:1]
    variance = (sums[1:2] + local_count * spread) / (count * local_count)
    return mean, lax.rsqrt(variance + EPSILON)


def sigmoid(values):
    return 1.0 / (1.0 + jnp.exp(-values))


def spread_planes(cot_ref, out_ref, planes, matrix):
    for rp in range(2):
        for rp2 in range(2):
            for h in range(2):
                lanes = [(4 * (2 * h + jj) + 2 * rp + rp2) * 256 for jj in range(2)]
                rows = jnp.concatenate(
                    [cot_ref[0 : len(planes) * C2, at : at + 256] for at in lanes], axis=1
                )
                moved = matmul(rows, matrix).astype(BF16)
                for cp2 in range(2):
                    for cp in range(2):
                        row = (2 * rp2 + cp2) * C2
                        lane = (2 * rp + cp) * CELLS + h * 128
                        piece = moved[:, cp2 * 256 + cp * 128 : cp2 * 256 + cp * 128 + 128]
                        for k, t in enumerate(planes):
                            out_ref[t, row : row + C2, lane : lane + 128] = piece[
                                k * C2 : (k + 1) * C2
                            ]


def prepare_kernel(
    w1_far, w2_far, gain1_far, shift1_far, gain2_far, shift2_far, cot_ref,
    a1_ref, a2_ref, b1_ref, b2_ref, sh_ref, p1_ref, p2_ref, spread_ref, matrix_ref,
    w1_ref, w2_ref, gain1_ref, shift1_ref, gain2_ref, shift2_ref, sem,
):
    copies = [
        pltpu.make_async_copy(far, near, sem.at[k])
        for k, (far, near) in enumerate(
            (
                (w1_far, w1_ref),
                (w2_far, w2_ref),
                (gain1_far, gain1_ref),
                (shift1_far, shift1_ref),
                (gain2_far, gain2_ref),
                (shift2_far, shift2_ref),
            )
        )
    ]
    for copy in copies:
        copy.start()
    matrix_ref[...] = spread_matrix()
    spread_planes(cot_ref, spread_ref, range(4), matrix_ref[...])
    for dj in (-1, 0, 1):
        for dl in (-1, 0, 1):
            sh_ref[:, shift_slot(dj, dl)] = shift_matrix(dj, dl)
    for copy in copies:
        copy.wait()
    place = lax.axis_index("space")
    below = jnp.where(place > 0, 1.0, 0.0)
    above = jnp.where(place < lax.axis_size("space") - 1, 1.0, 0.0)
    edges = [jnp.full((1, 128), below, F32), jnp.full((1, 128), above, F32)]
    blank = [jnp.zeros((4, 128), F32)]
    p1_ref[...] = jnp.concatenate(
        [jnp.concatenate([ref[...]] * 2, axis=1) for ref in (gain1_ref, shift1_ref)] + edges + blank
    )
    p2_ref[...] = jnp.concatenate(
        [jnp.concatenate([ref[...]] * 4, axis=1) for ref in (gain2_ref, shift2_ref)] + edges + blank
    )
    a1_ref[...] = jnp.zeros(a1_ref.shape, BF16)
    for par in range(2):
        for rp in range(2):
            for cp in range(2):
                row2 = par * 4 * C2 + (2 * rp + cp) * C2
                pieces = [jnp.zeros((C2, C1), BF16)] * 18
                for p, dp in PHASE_TAPS[par]:
                    dt = dp + 1 - par
                    for q, dr in PHASE_TAPS[rp]:
                        for r, dc in PHASE_TAPS[cp]:
                            tap = 16 * p + 4 * q + r
                            slot = dt * 9 + (dr + 1) * 3 + dc + 1
                            row = par * 4 * C1 + (2 * rp + cp) * C1
                            a1_ref[row : row + C1, slot * C0 : (slot + 1) * C0] = w1_ref[
                                tap * C1 : (tap + 1) * C1, :
                            ]
                            pieces[slot] = w2_ref[tap * C2 : (tap + 1) * C2, :]
                a2_ref[row2 : row2 + C2, :] = jnp.concatenate(pieces, axis=1)
    eye = jnp.where(
        lax.broadcasted_iota(jnp.int32, (128, 128), 0)
        == lax.broadcasted_iota(jnp.int32, (128, 128), 1),
        1.0,
        0.0,
    ).astype(BF16)

    @pl.loop(0, 8)
    def _(k):
        at = pl.multiple_of(k * 512, 512)
        b1_ref[:, pl.ds(at, 512)] = matmul_nt(eye, w1_ref[pl.ds(at, 512), :]).astype(BF16)

    @pl.loop(0, 4)
    def _(k):
        at = pl.multiple_of(k * 512, 512)
        b2_ref[:, pl.ds(at, 512)] = matmul_nt(eye[0:C1, 0:C1], w2_ref[pl.ds(at, 512), :]).astype(
            BF16
        )


def first_kernel(
    lat_ref, inner_ref, outer_ref, a1_ref, sh_ref, pre_ref, out_ref, near_ref, x_ref
):
    even = is_even()
    near_ref[0] = jnp.where(even, outer_ref[...], inner_ref[...])
    near_ref[1] = jnp.where(even, inner_ref[...], outer_ref[...])
    planes = jnp.concatenate([near_ref[0], lat_ref[...], near_ref[1]], axis=0)
    for k in range(9):
        moved = matmul(planes, sh_ref[:, k * CELLS : (k + 1) * CELLS]).astype(BF16)
        for z in range(3):
            at = (z * 9 + k) * C0
            x_ref[at : at + C0, :] = moved[z * C0 : (z + 1) * C0]
    for m in range(2):
        both = matmul(a1_ref[...], x_ref[m * 9 * C0 : (m + 2) * 9 * C0, :])
        pre_ref[2 * m + 1] = both[0 : 4 * C1]
        pre_ref[2 * m] = both[4 * C1 : 8 * C1]
    lower, upper = pre_ref[1], pre_ref[2]
    sums = fold(jnp.sum(lower + upper, axis=1, keepdims=True), C1)
    mean = sums / (8 * CELLS)
    wide = jnp.concatenate([mean] * 4, axis=0)
    lower, upper = lower - wide, upper - wide
    squares = fold(jnp.sum(lower * lower + upper * upper, axis=1, keepdims=True), C1)
    emit_rows(out_ref, mean, squares)


def second_kernel(got_ref, pre1_ref, p1_ref, a2_ref, sh_ref, pre_ref, act_ref, st_ref, out_ref, x_ref):
    mean, scale = moments(got_ref[...], 8 * CELLS)
    st = jnp.concatenate([mean, scale, p1_ref[0:6]], axis=0)
    st_ref[...] = st
    cols = columns(st)
    mean, scale, gain, shift = (cols[0:C1, k : k + 1] for k in range(4))
    keeps = (cols[0:C1, 4:5], None, None, cols[0:C1, 5:6])
    for q in range(4):
        for block in range(4):
            rp, cp = block // 2, block % 2
            norm = gain * ((pre1_ref[q, block * C1 : (block + 1) * C1, :] - mean) * scale) + shift
            act = norm * sigmoid(norm)
            if keeps[q] is not None:
                act = act * keeps[q]
            act = act.astype(BF16)
            if q in (1, 2):
                act_ref[q - 1, :, block * CELLS : (block + 1) * CELLS] = act
            sj, sl = 1 - 2 * rp, 1 - 2 * cp
            moved = {(0, 0): act}
            for dj, dl in ((sj, 0), (0, sl), (sj, sl)):
                moved[dj, dl] = matmul(act, sh_ref[:, shift_slot(dj, dl)]).astype(BF16)
            for (trp, dr), (srp, dj) in FINE_STEPS.items():
                if srp != rp:
                    continue
                for (tcp, dc), (scp, dl) in FINE_STEPS.items():
                    if scp != cp:
                        continue
                    at = q * 9 * C1 + ((dr + 1) * 3 + dc + 1) * C1
                    lane = (2 * trp + tcp) * CELLS
                    x_ref[at : at + C1, lane : lane + CELLS] = moved[dj, dl]

    for m in range(3):

        @pl.loop(0, 4)
        def _(block):
            lane = pl.multiple_of(block * CELLS, CELLS)
            both = matmul(a2_ref[...], x_ref[m * 9 * C1 : (m + 2) * 9 * C1, pl.ds(lane, CELLS)])
            pre_ref[2 * m + 1, :, pl.ds(lane, CELLS)] = both[0 : 4 * C2]
            pre_ref[2 * m, :, pl.ds(lane, CELLS)] = both[4 * C2 : 8 * C2]

    total = pre_ref[1] + pre_ref[2] + pre_ref[3] + pre_ref[4]
    sums = fold(jnp.sum(total, axis=1, keepdims=True), C2)
    mean = sums / (64 * CELLS)
    wide = jnp.concatenate([mean] * 4, axis=0)
    squares = jnp.zeros((4 * C2, CELLS), F32)
    for t in range(1, 5):
        for block in range(4):
            away = pre_ref[t, :, block * CELLS : (block + 1) * CELLS] - wide
            squares = squares + away * away
    emit_rows(out_ref, mean, fold(jnp.sum(squares, axis=1, keepdims=True), C2))


def gather_kernel(feat_ref, out_ref):
    matrix = spread_matrix()
    count = feat_ref.shape[0]
    for rp in range(2):
        for rp2 in range(2):
            for h in range(2):
                pieces = []
                for cp2 in range(2):
                    for cp in range(2):
                        row = (2 * rp2 + cp2) * C2
                        lane = (2 * rp + cp) * CELLS + h * 128
                        pieces.append(
                            jnp.concatenate(
                                [
                                    feat_ref[t, row : row + C2, lane : lane + 128]
                                    for t in range(count)
                                ],
                                axis=0,
                            )
                        )
                moved = matmul_nt(jnp.concatenate(pieces, axis=1), matrix).astype(BF16)
                for jj in range(2):
                    at = (4 * (2 * h + jj) + 2 * rp + rp2) * 256
                    out_ref[:, at : at + 256] = moved[:, jj * 256 : (jj + 1) * 256]


def third_kernel(
    got_ref, pre_ref, cot_ref, inner_ref, outer_ref, matrix_ref, p2_ref,
    grad_ref, feat_far, st_ref, out_ref, rows_ref, edge_ref, feat_ref, sem,
):
    even = is_even()
    rows_ref[0:C2] = jnp.where(even, outer_ref[...], inner_ref[...])
    rows_ref[C2:] = jnp.where(even, inner_ref[...], outer_ref[...])
    spread_planes(rows_ref, edge_ref, range(2), matrix_ref[...])
    mean, scale = moments(got_ref[...], 64 * CELLS)
    st = jnp.concatenate([mean, scale, p2_ref[0:6]], axis=0)
    st_ref[...] = st
    cols = columns(st)
    mean, scale, gain, shift = (cols[:, k : k + 1] for k in range(4))

    def slope(t, lane, cot):
        hat = (pre_ref[t, :, pl.ds(lane, CELLS)] - mean) * scale
        norm = gain * hat + shift
        gate = sigmoid(norm)
        grad = cot.astype(F32) * (gate * (1.0 + norm * (1.0 - gate)))
        grad_ref[t, :, pl.ds(lane, CELLS)] = grad
        return hat, norm, gate, grad

    first = jnp.zeros((4 * C2, CELLS), F32)
    second = jnp.zeros((4 * C2, CELLS), F32)
    copies = []
    for t in range(1, 5):

        def body(block, carry):
            lane = pl.multiple_of(block * CELLS, CELLS)
            hat, norm, gate, grad = slope(t, lane, cot_ref[t - 1, :, pl.ds(lane, CELLS)])
            feat_ref[t - 1, :, pl.ds(lane, CELLS)] = (norm * gate).astype(BF16)
            return carry[0] + grad * hat, carry[1] + grad

        first, second = lax.fori_loop(0, 4, body, (first, second))
        copies.append(
            pltpu.make_async_copy(feat_ref.at[t - 1], feat_far.at[t - 1], sem.at[t - 1])
        )
        copies[-1].start()
    for k in range(2):

        @pl.loop(0, 4)
        def _(block):
            lane = pl.multiple_of(block * CELLS, CELLS)
            slope(5 * k, lane, edge_ref[k, :, pl.ds(lane, CELLS)])

    emit_rows(
        out_ref,
        fold(jnp.sum(first, axis=1, keepdims=True), C2),
        fold(jnp.sum(second, axis=1, keepdims=True), C2),
    )
    for copy in copies:
        copy.wait()


def fourth_kernel(
    got_ref, pre_ref, grad_ref, st2_ref, b2_ref, sh_ref, act_ref, pre1_ref, st1_ref,
    g1_ref, dw_ref, sum_ref, out_ref, x_ref,
):
    sums = jnp.sum(got_ref[...], axis=0)
    sum_ref[...] = sums
    total = got_ref.shape[0] * 64 * CELLS
    cols = columns(jnp.concatenate([st2_ref[0:6], sums[0:2] / total], axis=0))
    mean, scale, gain = (cols[:, k : k + 1] for k in range(3))
    hat_part, part = cols[:, 6:7], cols[:, 7:8]
    keeps = {0: cols[:, 4:5], 5: cols[:, 5:6]}
    for t in range(6):
        factor = gain * scale
        if t in keeps:
            factor = factor * keeps[t]
        for block in range(4):
            rp, cp = block // 2, block % 2
            lanes = slice(block * CELLS, (block + 1) * CELLS)
            hat = (pre_ref[t, :, lanes] - mean) * scale
            dpre = (factor * (grad_ref[t, :, lanes] - part - hat * hat_part)).astype(BF16)
            sj, sl = 1 - 2 * rp, 1 - 2 * cp
            moved = {(0, 0): dpre}
            for dj, dl in ((sj, 0), (0, sl), (sj, sl)):
                moved[dj, dl] = matmul(dpre, sh_ref[:, shift_slot(dj, dl)]).astype(BF16)
            for q, (rp2, dr) in enumerate(TAP_PHASES):
                for r, (cp2, dc) in enumerate(TAP_PHASES):
                    row = (2 * rp2 + cp2) * C2
                    for trp in range(2):
                        for tcp in range(2):
                            srp, dj = FINE_STEPS[trp, dr]
                            scp, dl = FINE_STEPS[tcp, dc]
                            if (srp, scp) != (rp, cp):
                                continue
                            at = t * 16 * C2 + (4 * q + r) * C2
                            lane = (2 * trp + tcp) * CELLS
                            x_ref[at : at + C2, lane : lane + CELLS] = moved[dj, dl][row : row + C2]

    cols = columns(st1_ref[...])
    mean, scale, gain, shift = (cols[0:C1, k : k + 1] for k in range(4))
    first = jnp.zeros((C1, CELLS), F32)
    second = jnp.zeros((C1, CELLS), F32)
    for j in range(2):
        for block in range(4):
            lanes = slice(block * CELLS, (block + 1) * CELLS)
            act_grad = matmul(b2_ref[...], x_ref[j * 32 * C2 : (j + 2) * 32 * C2, lanes])
            hat = (pre1_ref[j + 1, block * C1 : (block + 1) * C1, :] - mean) * scale
            norm = gain * hat + shift
            gate = sigmoid(norm)
            grad = act_grad * (gate * (1.0 + norm * (1.0 - gate)))
            g1_ref[j, block * C1 : (block + 1) * C1, :] = grad
            first = first + grad * hat
            second = second + grad
    emit_rows(
        out_ref,
        jnp.sum(first, axis=1, keepdims=True),
        jnp.sum(second, axis=1, keepdims=True),
    )
    parts = []
    for p in range(4):
        part = matmul_nt(x_ref[p * 16 * C2 : (p + 1) * 16 * C2, :], act_ref[0])
        parts.append(part + matmul_nt(x_ref[(p + 2) * 16 * C2 : (p + 3) * 16 * C2, :], act_ref[1]))
    for p in range(2):
        dw_ref[p * 16 * C2 : (p + 1) * 16 * C2, :] = jnp.concatenate(
            [parts[p], parts[p + 2]], axis=1
        )


def first_dpre(grad, pre, cols):
    mean, scale, gain = (cols[0:C1, k : k + 1] for k in range(3))
    hat_part, part = cols[0:C1, 6:7], cols[0:C1, 7:8]
    return (gain * scale * (grad - part - (pre - mean) * scale * hat_part)).astype(BF16)


def first_windows(x_ref, base, grad_ref, pre_ref, cols, sh_ref):
    for block in range(4):
        rp, cp = block // 2, block % 2
        rows = slice(block * C1, (block + 1) * C1)
        dpre = first_dpre(grad_ref[rows, :], pre_ref[rows, :], cols)
        for q, (trp, dj) in enumerate(TAP_PHASES):
            for r, (tcp, dl) in enumerate(TAP_PHASES):
                if (trp, tcp) != (rp, cp):
                    continue
                moved = dpre
                if (dj, dl) != (0, 0):
                    moved = matmul(dpre, sh_ref[:, shift_slot(dj, dl)]).astype(BF16)
                at = base + (4 * q + r) * C1
                x_ref[at : at + C1, :] = moved


def fifth_kernel(
    got_ref, g1_ref, pre1_ref, st1_ref, sh_ref, lat_ref, near_ref, dw2_ref, b1_ref,
    keep_a_ref, keep_b_ref, send_a_ref, send_b_ref, sum_ref, mid_ref, inner_ref, outer_ref,
    x_ref, dw_ref, out_ref, sem,
):
    sums = jnp.sum(got_ref[...], axis=0)
    sum_ref[...] = sums
    total = got_ref.shape[0] * 8 * CELLS
    cols = columns(jnp.concatenate([st1_ref[0:6], sums[0:2] / total], axis=0))
    for j in range(2):
        first_windows(x_ref, j * 16 * C1, g1_ref.at[j], pre1_ref.at[j + 1], cols, sh_ref)
    fields = (near_ref[1], lat_ref[...], lat_ref[...], near_ref[0])
    for p, j, field in ((0, 1, fields[0]), (1, 0, fields[1]), (2, 1, fields[2]), (3, 0, fields[3])):
        for half in range(2):
            at = p * 16 * C1 + half * 8 * C1
            src = j * 16 * C1 + half * 8 * C1
            dw_ref[at : at + 8 * C1, :] = matmul_nt(x_ref[src : src + 8 * C1, :], field)
    dw_ref[64 * C1 :, :] = dw2_ref[...]
    chunk = dw_ref.shape[0] // 4
    core = lax.axis_index("rep")
    mine = pl.multiple_of(core * (2 * chunk), 2 * chunk)
    theirs = pl.multiple_of((1 - core) * (2 * chunk), 2 * chunk)
    out_ref[...] = dw_ref[pl.ds(theirs, 2 * chunk), :].astype(BF16)
    copies = [
        pltpu.make_async_copy(out_ref.at[0:chunk], send_a_ref, sem.at[0]),
        pltpu.make_async_copy(out_ref.at[chunk:], send_b_ref, sem.at[1]),
        pltpu.make_async_copy(dw_ref.at[pl.ds(mine, chunk)], keep_a_ref, sem.at[2]),
        pltpu.make_async_copy(dw_ref.at[pl.ds(mine + chunk, chunk)], keep_b_ref, sem.at[3]),
    ]
    for copy in copies:
        copy.start()
    pieces = [
        matmul(b1_ref[:, p * 16 * C1 : (p + 1) * 16 * C1], x_ref[j * 16 * C1 : (j + 1) * 16 * C1, :])
        for p, j in ((0, 1), (1, 0), (2, 1), (3, 0))
    ]
    mid_ref[...] = pieces[1] + pieces[2]
    up, down = pieces[0].astype(BF16), pieces[3].astype(BF16)
    even = is_even()
    inner_ref[...] = jnp.where(even, up, down)
    outer_ref[...] = jnp.where(even, down, up)
    for copy in copies:
        copy.wait()


def last_kernel(own_a_ref, own_b_ref, other_a_ref, other_b_ref, dw1_ref, dw2_ref, x_ref):
    core = lax.axis_index("rep")
    chunk = own_a_ref.shape[0]
    mine = pl.multiple_of(core * (2 * chunk), 2 * chunk)
    theirs = pl.multiple_of((1 - core) * (2 * chunk), 2 * chunk)
    x_ref[pl.ds(mine, chunk), :] = own_a_ref[...].astype(F32)
    x_ref[pl.ds(mine + chunk, chunk), :] = own_b_ref[...].astype(F32)
    x_ref[pl.ds(theirs, chunk), :] = other_a_ref[...].astype(F32)
    x_ref[pl.ds(theirs + chunk, chunk), :] = other_b_ref[...].astype(F32)
    dw1_ref[...] = x_ref[0 : 64 * C1, :]
    dw2_ref[0 : 32 * C2, :] = x_ref[64 * C1 :, 0:C1]
    dw2_ref[32 * C2 :, :] = x_ref[64 * C1 :, C1:]


def local(
    latent,
    first_weight,
    first_norm_gain,
    first_norm_shift,
    second_weight,
    second_norm_gain,
    second_norm_shift,
    cotangent,
):
    count = group_size()
    lat = latent.reshape(C0, CELLS)
    cot = cotangent.reshape(C2, 4, 16 * CELLS)
    top, bottom = cot[:, 3], cot[:, 0]
    lat_inner = swap_inner(lat)
    lat_outer = swap_outer(lat)
    cot_inner = swap_inner(jnp.where(is_even(), top, bottom))
    cot_outer = swap_outer(jnp.where(is_even(), bottom, top))
    planes = cot.transpose(1, 0, 2).reshape(4 * C2, 16 * CELLS)
    w1 = first_weight.reshape(64 * C1, C0)
    w2 = second_weight.reshape(64 * C2, C1)
    a1, a2, b1, b2, sh, p1, p2, spread, matrix = call(
        prepare_kernel,
        [
            ((8 * C1, 18 * C0), BF16),
            ((8 * C2, 18 * C1), BF16),
            ((C0, 64 * C1), BF16),
            ((C1, 64 * C2), BF16),
            ((CELLS, 9 * CELLS), BF16),
            ((8, 128), F32),
            ((8, 128), F32),
            ((4, 4 * C2, 4 * CELLS), BF16),
            ((512, 512), BF16),
        ],
        [
            w1,
            w2,
            first_norm_gain.reshape(1, C1),
            first_norm_shift.reshape(1, C1),
            second_norm_gain.reshape(1, C2),
            second_norm_shift.reshape(1, C2),
            planes,
        ],
        [
            pltpu.VMEM((64 * C1, C0), BF16),
            pltpu.VMEM((64 * C2, C1), BF16),
            pltpu.VMEM((1, C1), F32),
            pltpu.VMEM((1, C1), F32),
            pltpu.VMEM((1, C2), F32),
            pltpu.VMEM((1, C2), F32),
            pltpu.SemaphoreType.DMA((6,)),
        ],
        far_args=range(6),
    )
    stats = ((count, 8, 128), F32)
    pre1, out, near = call(
        first_kernel,
        [
            ((4, 4 * C1, CELLS), F32),
            stats,
            ((2, C0, CELLS), BF16),
        ],
        [lat, lat_inner, lat_outer, a1, sh],
        [pltpu.VMEM((27 * C0, CELLS), BF16)],
    )
    got = exchange(out)
    pre2, act, st1, out = call(
        second_kernel,
        [((6, 4 * C2, 4 * CELLS), F32), ((2, C1, 4 * CELLS), BF16), ((8, 128), F32), stats],
        [got, pre1, p1, a2, sh],
        [pltpu.VMEM((36 * C1, 4 * CELLS), BF16)],
    )
    out, cot_inner, cot_outer = hold(out, cot_inner, cot_outer)
    got = exchange(out)
    grad2, feat, st2, out = call(
        third_kernel,
        [
            ((6, 4 * C2, 4 * CELLS), F32),
            ((4, 4 * C2, 4 * CELLS), BF16),
            ((8, 128), F32),
            stats,
        ],
        [got, pre2, spread, cot_inner, cot_outer, matrix, p2],
        [
            pltpu.VMEM((2 * C2, 16 * CELLS), BF16),
            pltpu.VMEM((2, 4 * C2, 4 * CELLS), BF16),
            pltpu.VMEM((4, 4 * C2, 4 * CELLS), BF16),
            pltpu.SemaphoreType.DMA((4,)),
        ],
        far=(1,),
    )
    got = exchange(out)
    grad1, dw2, sum2, out = call(
        fourth_kernel,
        [((2, 4 * C1, CELLS), F32), ((32 * C2, 2 * C1), F32), ((8, 128), F32), stats],
        [got, pre2, grad2, st2, b2, sh, act, pre1, st1],
        [pltpu.VMEM((96 * C2, 4 * CELLS), BF16)],
    )
    got = exchange(out)
    rows = (64 * C1 + 32 * C2) // 4
    keep_a, keep_b, send_a, send_b, sum1, mid, lat_in, lat_out = call(
        fifth_kernel,
        [
            ((rows, C0), F32),
            ((rows, C0), F32),
            ((rows, C0), BF16),
            ((rows, C0), BF16),
            ((8, 128), F32),
            ((C0, CELLS), F32),
            ((C0, CELLS), BF16),
            ((C0, CELLS), BF16),
        ],
        [got, grad1, pre1, st1, sh, lat, near, dw2, b1],
        [
            pltpu.VMEM((32 * C1, CELLS), BF16),
            pltpu.VMEM((4 * rows, C0), F32),
            pltpu.VMEM((2 * rows, C0), BF16),
            pltpu.SemaphoreType.DMA((4,)),
        ],
        far=range(4),
    )
    parts = [
        keep_a + swap(send_a, "rep", 1).astype(F32),
        keep_b + swap(send_b, "rep", 1).astype(F32),
    ]
    orders = chunk_steps()
    steps = len(orders[0])
    latent_grad = mid + swap_inner(lat_in).astype(F32) + swap_outer(lat_out).astype(F32)
    for step in range(steps):
        parts = [halve(part, *order[step]) for part, order in zip(parts, orders)]
    parts = [part.astype(BF16) for part in parts]
    for step in reversed(range(steps)):
        if step == 0:
            feat, *parts = hold(feat, *parts)
            (features,) = call(gather_kernel, [((4 * C2, 16 * CELLS), BF16)], [feat])
            features = features.reshape(4, C2, 16 * CELLS).transpose(1, 0, 2)
        parts = [double(part, *order[step]) for part, order in zip(parts, orders)]
    features, latent_grad, part_a, part_b = hold(features, latent_grad, *parts)
    first_weight_grad, second_weight_grad = call(
        last_kernel,
        [((64 * C1, C0), F32), ((64 * C2, C1), F32)],
        [part_a, part_b, swap(part_a, "rep", 1), swap(part_b, "rep", 1)],
        [pltpu.VMEM((4 * rows, C0), F32)],
    )
    return (
        features[None],
        latent_grad.reshape(1, C0, 1, CELLS),
        first_weight_grad.reshape(64, C1, C0),
        second_weight_grad.reshape(64, C2, C1),
        sum1[0:2, 0:C1],
        sum2[0:2, 0:C2],
    )


def solution(mesh):
    volume = P(("group", "rep"), None, "space", None)
    in_specs = (volume, P(), P(), P(), P(), P(), P(), volume)
    out_specs = (
        volume,
        volume,
        P("group", None, None),
        P("group", None, None),
        P("group", None),
        P("group", None),
    )
    return jax.shard_map(local, mesh=mesh, in_specs=in_specs, out_specs=out_specs, check_vma=False)
```

```python
import jax
import jax.numpy as jnp
from jax import lax
from jax.experimental import pallas as pl
from jax.experimental.pallas import tpu as pltpu
from jax.sharding import PartitionSpec as P

H0 = 4
W0 = 64
CELLS = H0 * W0
C0 = 128
C1 = 64
C2 = 32
EPSILON = 1e-05

F32 = jnp.float32
BF16 = jnp.bfloat16
GROUP = ("space", "rep")

PHASE_TAPS = (((1, 0), (3, -1)), ((2, 0), (0, 1)))
TAP_PHASES = ((1, -1), (0, 0), (1, 0), (0, 1))
FINE_STEPS = {
    (0, -1): (1, -1),
    (0, 0): (0, 0),
    (0, 1): (1, 0),
    (1, -1): (0, 0),
    (1, 0): (1, 0),
    (1, 1): (0, 1),
}


def group_size():
    return lax.axis_size("space") * lax.axis_size("rep")


def swap(block, axis, bit):
    return lax.ppermute(block, axis, [(i, i ^ bit) for i in range(lax.axis_size(axis))])


def chunk_steps():
    bits = []
    bit = 1
    while bit < lax.axis_size("space"):
        bits.append(("space", bit))
        bit *= 2
    return bits, bits[1:2] + bits[0:1] + bits[2:]


def halve(part, axis, bit):
    upper = (lax.axis_index(axis) // bit) % 2
    half = part.shape[0] // 2
    kept = lax.dynamic_slice_in_dim(part, upper * half, half)
    sent = lax.dynamic_slice_in_dim(part, (1 - upper) * half, half).astype(BF16)
    return kept + swap(sent, axis, bit).astype(F32)


def double(part, axis, bit):
    upper = (lax.axis_index(axis) // bit) % 2
    other = swap(part, axis, bit)
    return jnp.where(
        upper == 0, jnp.concatenate([part, other]), jnp.concatenate([other, part])
    )


def exchange(copies):
    return lax.all_to_all(copies, GROUP, 0, 0)


def is_even():
    return lax.axis_index("space") % 2 == 0


def swap_inner(block):
    return swap(block, "space", 1)


def swap_outer(block):
    count = lax.axis_size("space")
    pairs = [(i, i + 1) for i in range(1, count - 1, 2)]
    return lax.ppermute(block, "space", pairs + [(j, i) for i, j in pairs])


def hold(*values):
    return lax.optimization_barrier(values)


def call(kernel, outs, args, scratch=(), far=(), far_args=()):
    def spec(away):
        return pl.BlockSpec(memory_space=pl.ANY if away else pltpu.VMEM)

    return pl.pallas_call(
        kernel,
        out_shape=[jax.ShapeDtypeStruct(shape, dtype) for shape, dtype in outs],
        in_specs=[spec(k in far_args) for k in range(len(args))],
        out_specs=[spec(k in far) for k in range(len(outs))],
        scratch_shapes=list(scratch),
        compiler_params=pltpu.CompilerParams(vmem_limit_bytes=24 * 2**20),
        cost_estimate=pl.CostEstimate(flops=10**9, bytes_accessed=4 * 10**6, transcendentals=0),
    )(*args)


def matmul(a, b):
    return jnp.dot(a, b, preferred_element_type=F32)


def matmul_nt(a, b):
    return lax.dot_general(a, b, (((1,), (1,)), ((), ())), preferred_element_type=F32)


def shift_matrix(dj, dl):
    src = lax.broadcasted_iota(jnp.int32, (CELLS, CELLS), 0)
    dst = lax.broadcasted_iota(jnp.int32, (CELLS, CELLS), 1)
    col = dst % W0 + dl
    hit = (src == dst + dj * W0 + dl) & (col >= 0) & (col < W0)
    return jnp.where(hit, 1.0, 0.0).astype(BF16)


def shift_slot(dj, dl):
    return slice(((dj + 1) * 3 + dl + 1) * CELLS, ((dj + 1) * 3 + dl + 2) * CELLS)


def spread_matrix():
    src = lax.broadcasted_iota(jnp.int32, (512, 512), 0)
    dst = lax.broadcasted_iota(jnp.int32, (512, 512), 1)
    cp2, cp, jj, l = dst // 256, (dst // 128) % 2, (dst // 64) % 2, dst % 64
    return jnp.where(src == jj * 256 + 4 * l + 2 * cp + cp2, 1.0, 0.0).astype(BF16)


def columns(rows):
    return jnp.transpose(jnp.concatenate([rows, jnp.zeros((120, 128), F32)], axis=0))


def emit_rows(ref, first, second):
    lane = lax.broadcasted_iota(jnp.int32, (first.shape[0], 128), 1)
    tile = jnp.where(lane == 0, first, jnp.where(lane == 1, second, 0.0))
    tile = jnp.concatenate([tile] * (128 // first.shape[0]), axis=0)
    rows = jnp.transpose(tile)[0:8, :]
    for k in range(ref.shape[0]):
        ref[k] = rows


def fold(rows, channels):
    total = rows[0:channels]
    for k in range(1, rows.shape[0] // channels):
        total = total + rows[k * channels : (k + 1) * channels]
    return total


def moments(copies, local_count):
    count = copies.shape[0]
    sums = jnp.sum(copies, axis=0)
    mean = sums[0:1] / count
    away = copies - mean[None]
    spread = jnp.sum(away * away, axis=0)[0:1]
    variance = (sums[1:2] + local_count * spread) / (count * local_count)
    return mean, lax.rsqrt(variance + EPSILON)


def sigmoid(values):
    return 0.5 * jnp.tanh(0.5 * values) + 0.5


def spread_planes(cot_ref, out_ref, planes, matrix):
    for rp in range(2):
        for rp2 in range(2):
            for h in range(2):
                lanes = [(4 * (2 * h + jj) + 2 * rp + rp2) * 256 for jj in range(2)]
                rows = jnp.concatenate(
                    [cot_ref[0 : len(planes) * C2, at : at + 256] for at in lanes], axis=1
                )
                moved = matmul(rows, matrix).astype(BF16)
                for cp2 in range(2):
                    for cp in range(2):
                        row = (2 * rp2 + cp2) * C2
                        lane = (2 * rp + cp) * CELLS + h * 128
                        piece = moved[:, cp2 * 256 + cp * 128 : cp2 * 256 + cp * 128 + 128]
                        for k, t in enumerate(planes):
                            out_ref[t, row : row + C2, lane : lane + 128] = piece[
                                k * C2 : (k + 1) * C2
                            ]


def prepare_kernel(
    w1_far, w2_far, gain1_far, shift1_far, gain2_far, shift2_far, cot_ref,
    a1_ref, a2_ref, b1_ref, b2_ref, sh_ref, p1_ref, p2_ref, spread_ref, matrix_ref,
    w1_ref, w2_ref, gain1_ref, shift1_ref, gain2_ref, shift2_ref, sem,
):
    copies = [
        pltpu.make_async_copy(far, near, sem.at[k])
        for k, (far, near) in enumerate(
            (
                (w1_far, w1_ref),
                (w2_far, w2_ref),
                (gain1_far, gain1_ref),
                (shift1_far, shift1_ref),
                (gain2_far, gain2_ref),
                (shift2_far, shift2_ref),
            )
        )
    ]
    for copy in copies:
        copy.start()
    matrix_ref[...] = spread_matrix()
    spread_planes(cot_ref, spread_ref, range(4), matrix_ref[...])
    for dj in (-1, 0, 1):
        for dl in (-1, 0, 1):
            sh_ref[:, shift_slot(dj, dl)] = shift_matrix(dj, dl)
    for copy in copies:
        copy.wait()
    place = lax.axis_index("space")
    below = jnp.where(place > 0, 1.0, 0.0)
    above = jnp.where(place < lax.axis_size("space") - 1, 1.0, 0.0)
    edges = [jnp.full((1, 128), below, F32), jnp.full((1, 128), above, F32)]
    blank = [jnp.zeros((4, 128), F32)]
    p1_ref[...] = jnp.concatenate(
        [jnp.concatenate([ref[...]] * 2, axis=1) for ref in (gain1_ref, shift1_ref)] + edges + blank
    )
    p2_ref[...] = jnp.concatenate(
        [jnp.concatenate([ref[...]] * 4, axis=1) for ref in (gain2_ref, shift2_ref)] + edges + blank
    )
    a1_ref[...] = jnp.zeros(a1_ref.shape, BF16)
    for par in range(2):
        for rp in range(2):
            for cp in range(2):
                row2 = par * 4 * C2 + (2 * rp + cp) * C2
                pieces = [jnp.zeros((C2, C1), BF16)] * 18
                for p, dp in PHASE_TAPS[par]:
                    dt = dp + 1 - par
                    for q, dr in PHASE_TAPS[rp]:
                        for r, dc in PHASE_TAPS[cp]:
                            tap = 16 * p + 4 * q + r
                            slot = dt * 9 + (dr + 1) * 3 + dc + 1
                            row = par * 4 * C1 + (2 * rp + cp) * C1
                            a1_ref[row : row + C1, slot * C0 : (slot + 1) * C0] = w1_ref[
                                tap * C1 : (tap + 1) * C1, :
                            ]
                            pieces[slot] = w2_ref[tap * C2 : (tap + 1) * C2, :]
                a2_ref[row2 : row2 + C2, :] = jnp.concatenate(pieces, axis=1)
    for k in range(32):
        b1_ref[:, k * 128 : (k + 1) * 128] = jnp.transpose(w1_ref[k * 128 : (k + 1) * 128, :])
    for k in range(16):
        b2_ref[:, k * 128 : (k + 1) * 128] = jnp.transpose(w2_ref[k * 128 : (k + 1) * 128, :])


def first_kernel(
    lat_ref, inner_ref, outer_ref, a1_ref, sh_ref, pre_ref, out_ref, near_ref, x_ref
):
    even = is_even()
    near_ref[0] = jnp.where(even, outer_ref[...], inner_ref[...])
    near_ref[1] = jnp.where(even, inner_ref[...], outer_ref[...])
    planes = jnp.concatenate([near_ref[0], lat_ref[...], near_ref[1]], axis=0)
    for k in range(9):
        moved = matmul(planes, sh_ref[:, k * CELLS : (k + 1) * CELLS]).astype(BF16)
        for z in range(3):
            at = (z * 9 + k) * C0
            x_ref[at : at + C0, :] = moved[z * C0 : (z + 1) * C0]
    for m in range(2):
        both = matmul(a1_ref[...], x_ref[m * 9 * C0 : (m + 2) * 9 * C0, :])
        pre_ref[2 * m + 1] = both[0 : 4 * C1]
        pre_ref[2 * m] = both[4 * C1 : 8 * C1]
    lower, upper = pre_ref[1], pre_ref[2]
    sums = fold(jnp.sum(lower + upper, axis=1, keepdims=True), C1)
    mean = sums / (8 * CELLS)
    wide = jnp.concatenate([mean] * 4, axis=0)
    lower, upper = lower - wide, upper - wide
    squares = fold(jnp.sum(lower * lower + upper * upper, axis=1, keepdims=True), C1)
    emit_rows(out_ref, mean, squares)


def second_kernel(got_ref, pre1_ref, p1_ref, a2_ref, sh_ref, pre_ref, act_ref, st_ref, out_ref, x_ref, all_ref):
    mean, scale = moments(got_ref[...], 8 * CELLS)
    st = jnp.concatenate([mean, scale, p1_ref[0:6]], axis=0)
    st_ref[...] = st
    cols = columns(st)
    mean, scale, gain, shift = (cols[0:C1, k : k + 1] for k in range(4))
    keeps = (cols[0:C1, 4:5], None, None, cols[0:C1, 5:6])
    for block in range(4):
        rp, cp = block // 2, block % 2
        for q in range(4):
            norm = gain * ((pre1_ref[q, block * C1 : (block + 1) * C1, :] - mean) * scale) + shift
            act = norm * sigmoid(norm)
            if keeps[q] is not None:
                act = act * keeps[q]
            act = act.astype(BF16)
            all_ref[block, q * C1 : (q + 1) * C1, :] = act
            if q in (1, 2):
                act_ref[(q - 1) * C1 : q * C1, block * CELLS : (block + 1) * CELLS] = act
        sj, sl = 1 - 2 * rp, 1 - 2 * cp
        for dj, dl in ((0, 0), (sj, 0), (0, sl), (sj, sl)):
            moved = all_ref[block]
            if (dj, dl) != (0, 0):
                moved = matmul(moved, sh_ref[:, shift_slot(dj, dl)]).astype(BF16)
            for (trp, dr), source in FINE_STEPS.items():
                if source != (rp, dj):
                    continue
                for (tcp, dc), source in FINE_STEPS.items():
                    if source != (cp, dl):
                        continue
                    lane = (2 * trp + tcp) * CELLS
                    for q in range(4):
                        at = q * 9 * C1 + ((dr + 1) * 3 + dc + 1) * C1
                        x_ref[at : at + C1, lane : lane + CELLS] = moved[q * C1 : (q + 1) * C1]

    for m in range(3):
        for block in range(4):
            lanes = slice(block * CELLS, (block + 1) * CELLS)
            both = matmul(a2_ref[...], x_ref[m * 9 * C1 : (m + 2) * 9 * C1, lanes])
            pre_ref[2 * m + 1, :, lanes] = both[0 : 4 * C2]
            pre_ref[2 * m, :, lanes] = both[4 * C2 : 8 * C2]

    partial = jnp.zeros((C2, CELLS), F32)
    for phase in range(4):
        for t in range(1, 5):
            for block in range(4):
                partial = partial + pre_ref[
                    t, phase * C2 : (phase + 1) * C2, block * CELLS : (block + 1) * CELLS
                ]
    mean = jnp.sum(partial, axis=1, keepdims=True) / (64 * CELLS)
    wide = jnp.broadcast_to(mean, (C2, CELLS))
    squares = jnp.zeros((C2, CELLS), F32)
    for phase in range(4):
        for t in range(1, 5):
            for block in range(4):
                away = (
                    pre_ref[
                        t, phase * C2 : (phase + 1) * C2, block * CELLS : (block + 1) * CELLS
                    ]
                    - wide
                )
                squares = squares + away * away
    emit_rows(out_ref, mean, jnp.sum(squares, axis=1, keepdims=True))


def gather_kernel(feat_ref, out_ref):
    matrix = spread_matrix()
    count = feat_ref.shape[0]
    for rp in range(2):
        for rp2 in range(2):
            for h in range(2):
                pieces = []
                for cp2 in range(2):
                    for cp in range(2):
                        row = (2 * rp2 + cp2) * C2
                        lane = (2 * rp + cp) * CELLS + h * 128
                        pieces.append(
                            jnp.concatenate(
                                [
                                    feat_ref[t, row : row + C2, lane : lane + 128]
                                    for t in range(count)
                                ],
                                axis=0,
                            )
                        )
                moved = matmul_nt(jnp.concatenate(pieces, axis=1), matrix).astype(BF16)
                for jj in range(2):
                    at = (4 * (2 * h + jj) + 2 * rp + rp2) * 256
                    out_ref[:, at : at + 256] = moved[:, jj * 256 : (jj + 1) * 256]


def third_kernel(
    got_ref, pre_ref, cot_ref, inner_ref, outer_ref, matrix_ref, p2_ref,
    grad_ref, feat_far, st_ref, out_ref, rows_ref, edge_ref, feat_ref, sem,
):
    even = is_even()
    rows_ref[0:C2] = jnp.where(even, outer_ref[...], inner_ref[...])
    rows_ref[C2:] = jnp.where(even, inner_ref[...], outer_ref[...])
    spread_planes(rows_ref, edge_ref, range(2), matrix_ref[...])
    mean, scale = moments(got_ref[...], 64 * CELLS)
    st = jnp.concatenate([mean, scale, p2_ref[0:6]], axis=0)
    st_ref[...] = st
    cols = columns(st)
    sums = []
    for phase in range(4):
        rows = slice(phase * C2, (phase + 1) * C2)
        mean, scale, gain, shift = (
            jnp.broadcast_to(cols[rows, k : k + 1], (C2, CELLS)) for k in range(4)
        )

        def slope(t, lane, cot):
            hat = (pre_ref[t, rows, pl.ds(lane, CELLS)] - mean) * scale
            norm = gain * hat + shift
            gate = sigmoid(norm)
            grad = cot.astype(F32) * (gate * (1.0 + norm * (1.0 - gate)))
            grad_ref[t, rows, pl.ds(lane, CELLS)] = grad
            return hat, norm, gate, grad

        def body(step, carry):
            t = step // 4
            lane = pl.multiple_of((step % 4) * CELLS, CELLS)
            hat, norm, gate, grad = slope(t + 1, lane, cot_ref[t, rows, pl.ds(lane, CELLS)])
            feat_ref[t, rows, pl.ds(lane, CELLS)] = (norm * gate).astype(BF16)
            return carry[0] + grad * hat, carry[1] + grad

        zero = jnp.zeros((C2, CELLS), F32)
        sums.append(lax.fori_loop(0, 16, body, (zero, zero), unroll=16))

        for k in range(2):
            for lane in range(0, 4 * CELLS, CELLS):
                slope(5 * k, lane, edge_ref[k, rows, pl.ds(lane, CELLS)])

    copy = pltpu.make_async_copy(feat_ref, feat_far, sem)
    copy.start()
    first, second = (sum(part[k] for part in sums) for k in range(2))
    emit_rows(
        out_ref,
        jnp.sum(first, axis=1, keepdims=True),
        jnp.sum(second, axis=1, keepdims=True),
    )
    copy.wait()


def fourth_kernel(
    got_ref, pre_ref, grad_ref, st2_ref, b2_ref, sh_ref, act_ref, pre1_ref, st1_ref,
    g1_ref, dw_ref, sum_ref, out_ref, x_ref, all_ref,
):
    sums = jnp.sum(got_ref[...], axis=0)
    sum_ref[...] = sums
    total = got_ref.shape[0] * 64 * CELLS
    cols = columns(jnp.concatenate([st2_ref[0:6], sums[0:2] / total], axis=0))
    mean, scale, gain = (cols[:, k : k + 1] for k in range(3))
    factor = gain * scale
    slant, offset = factor * scale * cols[:, 6:7], factor * cols[:, 7:8]
    for block in range(4):
        rp, cp = block // 2, block % 2
        lanes = slice(block * CELLS, (block + 1) * CELLS)
        for phase in range(4):
            rows = slice(phase * C2, (phase + 1) * C2)
            for t in range(6):
                away = pre_ref[t, rows, lanes] - mean[rows]
                dpre = factor[rows] * grad_ref[t, rows, lanes] - offset[rows] - away * slant[rows]
                if t == 0:
                    dpre = dpre * cols[rows, 4:5]
                if t == 5:
                    dpre = dpre * cols[rows, 5:6]
                all_ref[block, phase, t * C2 : (t + 1) * C2, :] = dpre.astype(BF16)
        for q, (rp2, dr) in enumerate(TAP_PHASES):
            for r, (cp2, dc) in enumerate(TAP_PHASES):
                moves = {}
                for trp in range(2):
                    for tcp in range(2):
                        srp, dj = FINE_STEPS[trp, dr]
                        scp, dl = FINE_STEPS[tcp, dc]
                        if (srp, scp) == (rp, cp):
                            moves[trp, tcp] = (dj, dl)
                for (trp, tcp), (dj, dl) in moves.items():
                    moved = all_ref[block, 2 * rp2 + cp2]
                    if (dj, dl) != (0, 0):
                        moved = matmul(moved, sh_ref[:, shift_slot(dj, dl)]).astype(BF16)
                    lane = (2 * trp + tcp) * CELLS
                    for t in range(6):
                        at = t * 16 * C2 + (4 * q + r) * C2
                        x_ref[at : at + C2, lane : lane + CELLS] = moved[t * C2 : (t + 1) * C2]

    cols = columns(st1_ref[...])
    mean, scale, gain, shift = (cols[0:C1, k : k + 1] for k in range(4))
    first = jnp.zeros((C1, CELLS), F32)
    second = jnp.zeros((C1, CELLS), F32)
    for j in range(2):
        for block in range(4):
            lanes = slice(block * CELLS, (block + 1) * CELLS)
            act_grad = matmul(b2_ref[...], x_ref[j * 32 * C2 : (j + 2) * 32 * C2, lanes])
            hat = (pre1_ref[j + 1, block * C1 : (block + 1) * C1, :] - mean) * scale
            norm = gain * hat + shift
            gate = sigmoid(norm)
            grad = act_grad * (gate * (1.0 + norm * (1.0 - gate)))
            g1_ref[j, block * C1 : (block + 1) * C1, :] = grad
            first = first + grad * hat
            second = second + grad
    emit_rows(
        out_ref,
        jnp.sum(first, axis=1, keepdims=True),
        jnp.sum(second, axis=1, keepdims=True),
    )
    parts = [
        matmul_nt(x_ref[t * 16 * C2 : (t + 1) * 16 * C2, :], act_ref[...]) for t in range(6)
    ]
    for p in range(2):
        low = [parts[p + 2 * k][:, 0:C1] for k in range(2)]
        high = [parts[p + 2 + 2 * k][:, C1:] for k in range(2)]
        dw_ref[p * 16 * C2 : (p + 1) * 16 * C2, :] = jnp.concatenate(
            low, axis=1
        ) + jnp.concatenate(high, axis=1)


def first_dpre(grad, pre, cols):
    mean, scale, gain = (cols[0:C1, k : k + 1] for k in range(3))
    hat_part, part = cols[0:C1, 6:7], cols[0:C1, 7:8]
    return (gain * scale * (grad - part - (pre - mean) * scale * hat_part)).astype(BF16)


def first_windows(x_ref, base, grad_ref, pre_ref, cols, sh_ref):
    for block in range(4):
        rp, cp = block // 2, block % 2
        rows = slice(block * C1, (block + 1) * C1)
        dpre = first_dpre(grad_ref[rows, :], pre_ref[rows, :], cols)
        for q, (trp, dj) in enumerate(TAP_PHASES):
            for r, (tcp, dl) in enumerate(TAP_PHASES):
                if (trp, tcp) != (rp, cp):
                    continue
                moved = dpre
                if (dj, dl) != (0, 0):
                    moved = matmul(dpre, sh_ref[:, shift_slot(dj, dl)]).astype(BF16)
                at = base + (4 * q + r) * C1
                x_ref[at : at + C1, :] = moved


def fifth_kernel(
    got_ref, g1_ref, pre1_ref, st1_ref, sh_ref, lat_ref, near_ref, dw2_ref, b1_ref,
    keep_a_ref, keep_b_ref, send_a_ref, send_b_ref, sum_ref, mid_ref, inner_ref, outer_ref,
    x_ref, dw_ref, out_ref, sem,
):
    sums = jnp.sum(got_ref[...], axis=0)
    sum_ref[...] = sums
    total = got_ref.shape[0] * 8 * CELLS
    cols = columns(jnp.concatenate([st1_ref[0:6], sums[0:2] / total], axis=0))
    for j in range(2):
        first_windows(x_ref, j * 16 * C1, g1_ref.at[j], pre1_ref.at[j + 1], cols, sh_ref)
    fields = (near_ref[1], lat_ref[...], lat_ref[...], near_ref[0])
    for p, j, field in ((0, 1, fields[0]), (1, 0, fields[1]), (2, 1, fields[2]), (3, 0, fields[3])):
        for half in range(2):
            at = p * 16 * C1 + half * 8 * C1
            src = j * 16 * C1 + half * 8 * C1
            dw_ref[at : at + 8 * C1, :] = matmul_nt(x_ref[src : src + 8 * C1, :], field)
    dw_ref[64 * C1 :, :] = dw2_ref[...]
    chunk = dw_ref.shape[0] // 4
    core = lax.axis_index("rep")
    mine = pl.multiple_of(core * (2 * chunk), 2 * chunk)
    theirs = pl.multiple_of((1 - core) * (2 * chunk), 2 * chunk)
    out_ref[...] = dw_ref[pl.ds(theirs, 2 * chunk), :].astype(BF16)
    copies = [
        pltpu.make_async_copy(out_ref.at[0:chunk], send_a_ref, sem.at[0]),
        pltpu.make_async_copy(out_ref.at[chunk:], send_b_ref, sem.at[1]),
        pltpu.make_async_copy(dw_ref.at[pl.ds(mine, chunk)], keep_a_ref, sem.at[2]),
        pltpu.make_async_copy(dw_ref.at[pl.ds(mine + chunk, chunk)], keep_b_ref, sem.at[3]),
    ]
    for copy in copies:
        copy.start()
    pieces = [
        matmul(b1_ref[:, p * 16 * C1 : (p + 1) * 16 * C1], x_ref[j * 16 * C1 : (j + 1) * 16 * C1, :])
        for p, j in ((0, 1), (1, 0), (2, 1), (3, 0))
    ]
    mid_ref[...] = pieces[1] + pieces[2]
    up, down = pieces[0].astype(BF16), pieces[3].astype(BF16)
    even = is_even()
    inner_ref[...] = jnp.where(even, up, down)
    outer_ref[...] = jnp.where(even, down, up)
    for copy in copies:
        copy.wait()


def last_kernel(own_a_ref, own_b_ref, other_a_ref, other_b_ref, dw1_ref, dw2_ref, x_ref):
    core = lax.axis_index("rep")
    chunk = own_a_ref.shape[0]
    mine = pl.multiple_of(core * (2 * chunk), 2 * chunk)
    theirs = pl.multiple_of((1 - core) * (2 * chunk), 2 * chunk)
    x_ref[pl.ds(mine, chunk), :] = own_a_ref[...].astype(F32)
    x_ref[pl.ds(mine + chunk, chunk), :] = own_b_ref[...].astype(F32)
    x_ref[pl.ds(theirs, chunk), :] = other_a_ref[...].astype(F32)
    x_ref[pl.ds(theirs + chunk, chunk), :] = other_b_ref[...].astype(F32)
    dw1_ref[...] = x_ref[0 : 64 * C1, :]
    dw2_ref[0 : 32 * C2, :] = x_ref[64 * C1 :, 0:C1]
    dw2_ref[32 * C2 :, :] = x_ref[64 * C1 :, C1:]


def local(
    latent,
    first_weight,
    first_norm_gain,
    first_norm_shift,
    second_weight,
    second_norm_gain,
    second_norm_shift,
    cotangent,
):
    count = group_size()
    lat = latent.reshape(C0, CELLS)
    cot = cotangent.reshape(C2, 4, 16 * CELLS)
    top, bottom = cot[:, 3], cot[:, 0]
    lat_inner = swap_inner(lat)
    lat_outer = swap_outer(lat)
    cot_inner = swap_inner(jnp.where(is_even(), top, bottom))
    cot_outer = swap_outer(jnp.where(is_even(), bottom, top))
    planes = cot.transpose(1, 0, 2).reshape(4 * C2, 16 * CELLS)
    w1 = first_weight.reshape(64 * C1, C0)
    w2 = second_weight.reshape(64 * C2, C1)
    a1, a2, b1, b2, sh, p1, p2, spread, matrix = call(
        prepare_kernel,
        [
            ((8 * C1, 18 * C0), BF16),
            ((8 * C2, 18 * C1), BF16),
            ((C0, 64 * C1), BF16),
            ((C1, 64 * C2), BF16),
            ((CELLS, 9 * CELLS), BF16),
            ((8, 128), F32),
            ((8, 128), F32),
            ((4, 4 * C2, 4 * CELLS), BF16),
            ((512, 512), BF16),
        ],
        [
            w1,
            w2,
            first_norm_gain.reshape(1, C1),
            first_norm_shift.reshape(1, C1),
            second_norm_gain.reshape(1, C2),
            second_norm_shift.reshape(1, C2),
            planes,
        ],
        [
            pltpu.VMEM((64 * C1, C0), BF16),
            pltpu.VMEM((64 * C2, C1), BF16),
            pltpu.VMEM((1, C1), F32),
            pltpu.VMEM((1, C1), F32),
            pltpu.VMEM((1, C2), F32),
            pltpu.VMEM((1, C2), F32),
            pltpu.SemaphoreType.DMA((6,)),
        ],
        far_args=range(6),
    )
    stats = ((count, 8, 128), F32)
    pre1, out, near = call(
        first_kernel,
        [
            ((4, 4 * C1, CELLS), F32),
            stats,
            ((2, C0, CELLS), BF16),
        ],
        [lat, lat_inner, lat_outer, a1, sh],
        [pltpu.VMEM((27 * C0, CELLS), BF16)],
    )
    got = exchange(out)
    pre2, act, st1, out = call(
        second_kernel,
        [((6, 4 * C2, 4 * CELLS), F32), ((2 * C1, 4 * CELLS), BF16), ((8, 128), F32), stats],
        [got, pre1, p1, a2, sh],
        [pltpu.VMEM((36 * C1, 4 * CELLS), BF16), pltpu.VMEM((4, 4 * C1, CELLS), BF16)],
    )
    out, cot_inner, cot_outer = hold(out, cot_inner, cot_outer)
    got = exchange(out)
    grad2, feat, st2, out = call(
        third_kernel,
        [
            ((6, 4 * C2, 4 * CELLS), F32),
            ((4, 4 * C2, 4 * CELLS), BF16),
            ((8, 128), F32),
            stats,
        ],
        [got, pre2, spread, cot_inner, cot_outer, matrix, p2],
        [
            pltpu.VMEM((2 * C2, 16 * CELLS), BF16),
            pltpu.VMEM((2, 4 * C2, 4 * CELLS), BF16),
            pltpu.VMEM((4, 4 * C2, 4 * CELLS), BF16),
            pltpu.SemaphoreType.DMA,
        ],
        far=(1,),
    )
    got = exchange(out)
    grad1, dw2, sum2, out = call(
        fourth_kernel,
        [((2, 4 * C1, CELLS), F32), ((32 * C2, 2 * C1), F32), ((8, 128), F32), stats],
        [got, pre2, grad2, st2, b2, sh, act, pre1, st1],
        [pltpu.VMEM((96 * C2, 4 * CELLS), BF16), pltpu.VMEM((4, 4, 6 * C2, CELLS), BF16)],
    )
    got = exchange(out)
    rows = (64 * C1 + 32 * C2) // 4
    keep_a, keep_b, send_a, send_b, sum1, mid, lat_in, lat_out = call(
        fifth_kernel,
        [
            ((rows, C0), F32),
            ((rows, C0), F32),
            ((rows, C0), BF16),
            ((rows, C0), BF16),
            ((8, 128), F32),
            ((C0, CELLS), F32),
            ((C0, CELLS), BF16),
            ((C0, CELLS), BF16),
        ],
        [got, grad1, pre1, st1, sh, lat, near, dw2, b1],
        [
            pltpu.VMEM((32 * C1, CELLS), BF16),
            pltpu.VMEM((4 * rows, C0), F32),
            pltpu.VMEM((2 * rows, C0), BF16),
            pltpu.SemaphoreType.DMA((4,)),
        ],
        far=range(4),
    )
    parts = [
        keep_a + swap(send_a, "rep", 1).astype(F32),
        keep_b + swap(send_b, "rep", 1).astype(F32),
    ]
    orders = chunk_steps()
    steps = len(orders[0])
    for step in range(steps):
        parts = [halve(part, *order[step]) for part, order in zip(parts, orders)]
    parts = [part.astype(BF16) for part in parts]
    lat_in, lat_out, *parts = hold(lat_in, lat_out, *parts)
    latent_grad = mid + swap_inner(lat_in).astype(F32) + swap_outer(lat_out).astype(F32)
    for step in reversed(range(steps)):
        if step == 0:
            feat, *parts = hold(feat, *parts)
            (features,) = call(gather_kernel, [((4 * C2, 16 * CELLS), BF16)], [feat])
            features = features.reshape(4, C2, 16 * CELLS).transpose(1, 0, 2)
        parts = [double(part, *order[step]) for part, order in zip(parts, orders)]
    features, latent_grad, part_a, part_b = hold(features, latent_grad, *parts)
    first_weight_grad, second_weight_grad = call(
        last_kernel,
        [((64 * C1, C0), F32), ((64 * C2, C1), F32)],
        [part_a, part_b, swap(part_a, "rep", 1), swap(part_b, "rep", 1)],
        [pltpu.VMEM((4 * rows, C0), F32)],
    )
    return (
        features[None],
        latent_grad.reshape(1, C0, 1, CELLS),
        first_weight_grad.reshape(64, C1, C0),
        second_weight_grad.reshape(64, C2, C1),
        sum1[0:2, 0:C1],
        sum2[0:2, 0:C2],
    )


def solution(mesh):
    volume = P(("group", "rep"), None, "space", None)
    in_specs = (volume, P(), P(), P(), P(), P(), P(), volume)
    out_specs = (
        volume,
        volume,
        P("group", None, None),
        P("group", None, None),
        P("group", None),
        P("group", None),
    )
    return jax.shard_map(local, mesh=mesh, in_specs=in_specs, out_specs=out_specs, check_vma=False)
```

```python
import jax
import jax.numpy as jnp
from jax import lax
from jax.experimental import pallas as pl
from jax.experimental.pallas import tpu as pltpu
from jax.sharding import PartitionSpec as P

H0 = 4
W0 = 64
CELLS = H0 * W0
C0 = 128
C1 = 64
C2 = 32
EPSILON = 1e-05

F32 = jnp.float32
BF16 = jnp.bfloat16
GROUP = ("space", "rep")

PHASE_TAPS = (((1, 0), (3, -1)), ((2, 0), (0, 1)))
TAP_PHASES = ((1, -1), (0, 0), (1, 0), (0, 1))
FINE_STEPS = {
    (0, -1): (1, -1),
    (0, 0): (0, 0),
    (0, 1): (1, 0),
    (1, -1): (0, 0),
    (1, 0): (1, 0),
    (1, 1): (0, 1),
}


def group_size():
    return lax.axis_size("space") * lax.axis_size("rep")


def swap(block, axis, bit):
    return lax.ppermute(block, axis, [(i, i ^ bit) for i in range(lax.axis_size(axis))])


def chunk_steps():
    bits = []
    bit = 1
    while bit < lax.axis_size("space"):
        bits.append(("space", bit))
        bit *= 2
    return bits[1:2] + bits[0:1] + bits[2:], bits


def halve(part, axis, bit):
    upper = (lax.axis_index(axis) // bit) % 2
    half = part.shape[0] // 2
    kept = lax.dynamic_slice_in_dim(part, upper * half, half)
    sent = lax.dynamic_slice_in_dim(part, (1 - upper) * half, half).astype(BF16)
    return kept + swap(sent, axis, bit).astype(F32)


def double(part, axis, bit):
    upper = (lax.axis_index(axis) // bit) % 2
    other = swap(part, axis, bit)
    return jnp.where(
        upper == 0, jnp.concatenate([part, other]), jnp.concatenate([other, part])
    )


def exchange(copies):
    return lax.all_to_all(copies, GROUP, 0, 0)


def is_even():
    return lax.axis_index("space") % 2 == 0


def swap_inner(block):
    return swap(block, "space", 1)


def swap_outer(block):
    count = lax.axis_size("space")
    pairs = [(i, i + 1) for i in range(1, count - 1, 2)]
    return lax.ppermute(block, "space", pairs + [(j, i) for i, j in pairs])


def hold(*values):
    return lax.optimization_barrier(values)


def call(kernel, outs, args, scratch=(), far=(), far_args=()):
    def spec(away):
        return pl.BlockSpec(memory_space=pl.ANY if away else pltpu.VMEM)

    return pl.pallas_call(
        kernel,
        out_shape=[jax.ShapeDtypeStruct(shape, dtype) for shape, dtype in outs],
        in_specs=[spec(k in far_args) for k in range(len(args))],
        out_specs=[spec(k in far) for k in range(len(outs))],
        scratch_shapes=list(scratch),
        compiler_params=pltpu.CompilerParams(vmem_limit_bytes=24 * 2**20),
        cost_estimate=pl.CostEstimate(flops=10**9, bytes_accessed=4 * 10**6, transcendentals=0),
    )(*args)


def matmul(a, b):
    return jnp.dot(a, b, preferred_element_type=F32)


def matmul_nt(a, b):
    return lax.dot_general(a, b, (((1,), (1,)), ((), ())), preferred_element_type=F32)


def shift_matrix(dj, dl):
    src = lax.broadcasted_iota(jnp.int32, (CELLS, CELLS), 0)
    dst = lax.broadcasted_iota(jnp.int32, (CELLS, CELLS), 1)
    col = dst % W0 + dl
    hit = (src == dst + dj * W0 + dl) & (col >= 0) & (col < W0)
    return jnp.where(hit, 1.0, 0.0).astype(BF16)


def shift_slot(dj, dl):
    return slice(((dj + 1) * 3 + dl + 1) * CELLS, ((dj + 1) * 3 + dl + 2) * CELLS)


def spread_matrix():
    src = lax.broadcasted_iota(jnp.int32, (512, 512), 0)
    dst = lax.broadcasted_iota(jnp.int32, (512, 512), 1)
    cp2, cp, jj, l = dst // 256, (dst // 128) % 2, (dst // 64) % 2, dst % 64
    return jnp.where(src == jj * 256 + 4 * l + 2 * cp + cp2, 1.0, 0.0).astype(BF16)


def columns(rows):
    return jnp.transpose(jnp.concatenate([rows, jnp.zeros((120, 128), F32)], axis=0))


def emit_rows(ref, first, second):
    lane = lax.broadcasted_iota(jnp.int32, (first.shape[0], 128), 1)
    tile = jnp.where(lane == 0, first, jnp.where(lane == 1, second, 0.0))
    tile = jnp.concatenate([tile] * (128 // first.shape[0]), axis=0)
    rows = jnp.transpose(tile)[0:8, :]
    for k in range(ref.shape[0]):
        ref[k] = rows


def fold(rows, channels):
    total = rows[0:channels]
    for k in range(1, rows.shape[0] // channels):
        total = total + rows[k * channels : (k + 1) * channels]
    return total


def moments(copies, local_count):
    count = copies.shape[0]
    sums = jnp.sum(copies, axis=0)
    mean = sums[0:1] / count
    away = copies - mean[None]
    spread = jnp.sum(away * away, axis=0)[0:1]
    variance = (sums[1:2] + local_count * spread) / (count * local_count)
    return mean, lax.rsqrt(variance + EPSILON)


def sigmoid(values):
    return 0.5 * jnp.tanh(0.5 * values) + 0.5


def spread_planes(cot_ref, out_ref, planes, matrix):
    for rp in range(2):
        for rp2 in range(2):
            for h in range(2):
                lanes = [(4 * (2 * h + jj) + 2 * rp + rp2) * 256 for jj in range(2)]
                rows = jnp.concatenate(
                    [cot_ref[0 : len(planes) * C2, at : at + 256] for at in lanes], axis=1
                )
                moved = matmul(rows, matrix).astype(BF16)
                for cp2 in range(2):
                    for cp in range(2):
                        row = (2 * rp2 + cp2) * C2
                        lane = (2 * rp + cp) * CELLS + h * 128
                        piece = moved[:, cp2 * 256 + cp * 128 : cp2 * 256 + cp * 128 + 128]
                        for k, t in enumerate(planes):
                            out_ref[t, row : row + C2, lane : lane + 128] = piece[
                                k * C2 : (k + 1) * C2
                            ]


def prepare_kernel(
    w1_far, w2_far, gain1_far, shift1_far, gain2_far, shift2_far, cot_ref,
    a1_ref, a2_ref, b1_ref, b2_ref, sh_ref, p1_ref, p2_ref, spread_ref, matrix_ref,
    w1_ref, w2_ref, gain1_ref, shift1_ref, gain2_ref, shift2_ref, sem,
):
    copies = [
        pltpu.make_async_copy(far, near, sem.at[k])
        for k, (far, near) in enumerate(
            (
                (w1_far, w1_ref),
                (w2_far, w2_ref),
                (gain1_far, gain1_ref),
                (shift1_far, shift1_ref),
                (gain2_far, gain2_ref),
                (shift2_far, shift2_ref),
            )
        )
    ]
    for copy in copies:
        copy.start()
    matrix_ref[...] = spread_matrix()
    spread_planes(cot_ref, spread_ref, range(4), matrix_ref[...])
    for dj in (-1, 0, 1):
        for dl in (-1, 0, 1):
            sh_ref[:, shift_slot(dj, dl)] = shift_matrix(dj, dl)
    for copy in copies:
        copy.wait()
    place = lax.axis_index("space")
    below = jnp.where(place > 0, 1.0, 0.0)
    above = jnp.where(place < lax.axis_size("space") - 1, 1.0, 0.0)
    edges = [jnp.full((1, 128), below, F32), jnp.full((1, 128), above, F32)]
    blank = [jnp.zeros((4, 128), F32)]
    p1_ref[...] = jnp.concatenate(
        [jnp.concatenate([ref[...]] * 2, axis=1) for ref in (gain1_ref, shift1_ref)] + edges + blank
    )
    p2_ref[...] = jnp.concatenate(
        [jnp.concatenate([ref[...]] * 4, axis=1) for ref in (gain2_ref, shift2_ref)] + edges + blank
    )
    a1_ref[...] = jnp.zeros(a1_ref.shape, BF16)
    for par in range(2):
        for rp in range(2):
            for cp in range(2):
                row2 = par * 4 * C2 + (2 * rp + cp) * C2
                pieces = [jnp.zeros((C2, C1), BF16)] * 18
                for p, dp in PHASE_TAPS[par]:
                    dt = dp + 1 - par
                    for q, dr in PHASE_TAPS[rp]:
                        for r, dc in PHASE_TAPS[cp]:
                            tap = 16 * p + 4 * q + r
                            slot = dt * 9 + (dr + 1) * 3 + dc + 1
                            row = par * 4 * C1 + (2 * rp + cp) * C1
                            a1_ref[row : row + C1, slot * C0 : (slot + 1) * C0] = w1_ref[
                                tap * C1 : (tap + 1) * C1, :
                            ]
                            pieces[slot] = w2_ref[tap * C2 : (tap + 1) * C2, :]
                a2_ref[row2 : row2 + C2, :] = jnp.concatenate(pieces, axis=1)
    for k in range(32):
        b1_ref[:, k * 128 : (k + 1) * 128] = jnp.transpose(w1_ref[k * 128 : (k + 1) * 128, :])
    for k in range(16):
        b2_ref[:, k * 128 : (k + 1) * 128] = jnp.transpose(w2_ref[k * 128 : (k + 1) * 128, :])


def first_kernel(
    lat_ref, inner_ref, outer_ref, a1_ref, sh_ref, pre_ref, out_ref, near_ref, x_ref
):
    even = is_even()
    near_ref[0] = jnp.where(even, outer_ref[...], inner_ref[...])
    near_ref[1] = jnp.where(even, inner_ref[...], outer_ref[...])
    planes = jnp.concatenate([near_ref[0], lat_ref[...], near_ref[1]], axis=0)
    for k in range(9):
        moved = planes
        if k != 4:
            moved = matmul(planes, sh_ref[:, k * CELLS : (k + 1) * CELLS]).astype(BF16)
        for z in range(3):
            at = (z * 9 + k) * C0
            x_ref[at : at + C0, :] = moved[z * C0 : (z + 1) * C0]
    for m in range(2):
        both = matmul(a1_ref[...], x_ref[m * 9 * C0 : (m + 2) * 9 * C0, :])
        pre_ref[2 * m + 1] = both[0 : 4 * C1]
        pre_ref[2 * m] = both[4 * C1 : 8 * C1]
    lower, upper = pre_ref[1], pre_ref[2]
    sums = fold(jnp.sum(lower + upper, axis=1, keepdims=True), C1)
    mean = sums / (8 * CELLS)
    wide = jnp.concatenate([mean] * 4, axis=0)
    lower, upper = lower - wide, upper - wide
    squares = fold(jnp.sum(lower * lower + upper * upper, axis=1, keepdims=True), C1)
    emit_rows(out_ref, mean, squares)


def second_kernel(got_ref, pre1_ref, p1_ref, a2_ref, sh_ref, pre_ref, act_ref, st_ref, out_ref, x_ref, all_ref):
    mean, scale = moments(got_ref[...], 8 * CELLS)
    st = jnp.concatenate([mean, scale, p1_ref[0:6]], axis=0)
    st_ref[...] = st
    cols = columns(st)
    mean, scale, gain, shift = (cols[0:C1, k : k + 1] for k in range(4))
    keeps = (cols[0:C1, 4:5], None, None, cols[0:C1, 5:6])
    for block in range(4):
        rp, cp = block // 2, block % 2
        for q in range(4):
            norm = gain * ((pre1_ref[q, block * C1 : (block + 1) * C1, :] - mean) * scale) + shift
            act = norm * sigmoid(norm)
            if keeps[q] is not None:
                act = act * keeps[q]
            act = act.astype(BF16)
            all_ref[block, q * C1 : (q + 1) * C1, :] = act
            if q in (1, 2):
                act_ref[(q - 1) * C1 : q * C1, block * CELLS : (block + 1) * CELLS] = act
        sj, sl = 1 - 2 * rp, 1 - 2 * cp
        for dj, dl in ((0, 0), (sj, 0), (0, sl), (sj, sl)):
            moved = all_ref[block]
            if (dj, dl) != (0, 0):
                moved = matmul(moved, sh_ref[:, shift_slot(dj, dl)]).astype(BF16)
            for (trp, dr), source in FINE_STEPS.items():
                if source != (rp, dj):
                    continue
                for (tcp, dc), source in FINE_STEPS.items():
                    if source != (cp, dl):
                        continue
                    lane = (2 * trp + tcp) * CELLS
                    for q in range(4):
                        at = q * 9 * C1 + ((dr + 1) * 3 + dc + 1) * C1
                        x_ref[at : at + C1, lane : lane + CELLS] = moved[q * C1 : (q + 1) * C1]

    for m in range(3):
        for block in range(4):
            lanes = slice(block * CELLS, (block + 1) * CELLS)
            both = matmul(a2_ref[...], x_ref[m * 9 * C1 : (m + 2) * 9 * C1, lanes])
            pre_ref[2 * m + 1, :, lanes] = both[0 : 4 * C2]
            pre_ref[2 * m, :, lanes] = both[4 * C2 : 8 * C2]

    partial = jnp.zeros((C2, CELLS), F32)
    for phase in range(4):
        for t in range(1, 5):
            for block in range(4):
                partial = partial + pre_ref[
                    t, phase * C2 : (phase + 1) * C2, block * CELLS : (block + 1) * CELLS
                ]
    mean = jnp.sum(partial, axis=1, keepdims=True) / (64 * CELLS)
    wide = jnp.broadcast_to(mean, (C2, CELLS))
    squares = jnp.zeros((C2, CELLS), F32)
    for phase in range(4):
        for t in range(1, 5):
            for block in range(4):
                away = (
                    pre_ref[
                        t, phase * C2 : (phase + 1) * C2, block * CELLS : (block + 1) * CELLS
                    ]
                    - wide
                )
                squares = squares + away * away
    emit_rows(out_ref, mean, jnp.sum(squares, axis=1, keepdims=True))


def gather_kernel(feat_ref, out_ref):
    matrix = spread_matrix()
    count = feat_ref.shape[0]
    for rp in range(2):
        for rp2 in range(2):
            for h in range(2):
                pieces = []
                for cp2 in range(2):
                    for cp in range(2):
                        row = (2 * rp2 + cp2) * C2
                        lane = (2 * rp + cp) * CELLS + h * 128
                        pieces.append(
                            jnp.concatenate(
                                [
                                    feat_ref[t, row : row + C2, lane : lane + 128]
                                    for t in range(count)
                                ],
                                axis=0,
                            )
                        )
                moved = matmul_nt(jnp.concatenate(pieces, axis=1), matrix).astype(BF16)
                for jj in range(2):
                    at = (4 * (2 * h + jj) + 2 * rp + rp2) * 256
                    out_ref[:, at : at + 256] = moved[:, jj * 256 : (jj + 1) * 256]


def third_kernel(
    got_ref, pre_ref, cot_ref, inner_ref, outer_ref, matrix_ref, p2_ref,
    grad_ref, feat_far, st_ref, out_ref, rows_ref, edge_ref, feat_ref, sem,
):
    even = is_even()
    rows_ref[0:C2] = jnp.where(even, outer_ref[...], inner_ref[...])
    rows_ref[C2:] = jnp.where(even, inner_ref[...], outer_ref[...])
    spread_planes(rows_ref, edge_ref, range(2), matrix_ref[...])
    mean, scale = moments(got_ref[...], 64 * CELLS)
    st = jnp.concatenate([mean, scale, p2_ref[0:6]], axis=0)
    st_ref[...] = st
    cols = columns(st)
    sums = []
    for phase in range(4):
        rows = slice(phase * C2, (phase + 1) * C2)
        mean, scale, gain, shift = (
            jnp.broadcast_to(cols[rows, k : k + 1], (C2, CELLS)) for k in range(4)
        )

        def slope(t, lane, cot):
            hat = (pre_ref[t, rows, pl.ds(lane, CELLS)] - mean) * scale
            norm = gain * hat + shift
            gate = sigmoid(norm)
            grad = cot.astype(F32) * (gate * (1.0 + norm * (1.0 - gate)))
            grad_ref[t, rows, pl.ds(lane, CELLS)] = grad
            return hat, norm, gate, grad

        def body(step, carry):
            t = step // 4
            lane = pl.multiple_of((step % 4) * CELLS, CELLS)
            hat, norm, gate, grad = slope(t + 1, lane, cot_ref[t, rows, pl.ds(lane, CELLS)])
            feat_ref[t, rows, pl.ds(lane, CELLS)] = (norm * gate).astype(BF16)
            return carry[0] + grad * hat, carry[1] + grad

        zero = jnp.zeros((C2, CELLS), F32)
        sums.append(lax.fori_loop(0, 16, body, (zero, zero), unroll=16))

        for k in range(2):
            for lane in range(0, 4 * CELLS, CELLS):
                slope(5 * k, lane, edge_ref[k, rows, pl.ds(lane, CELLS)])

    copy = pltpu.make_async_copy(feat_ref, feat_far, sem)
    copy.start()
    first, second = (sum(part[k] for part in sums) for k in range(2))
    emit_rows(
        out_ref,
        jnp.sum(first, axis=1, keepdims=True),
        jnp.sum(second, axis=1, keepdims=True),
    )
    copy.wait()


def fourth_kernel(
    got_ref, pre_ref, grad_ref, st2_ref, b2_ref, sh_ref, act_ref, pre1_ref, st1_ref,
    g1_ref, dw_ref, sum_ref, out_ref, x_ref, all_ref,
):
    sums = jnp.sum(got_ref[...], axis=0)
    sum_ref[...] = sums
    total = got_ref.shape[0] * 64 * CELLS
    cols = columns(jnp.concatenate([st2_ref[0:6], sums[0:2] / total], axis=0))
    mean, scale, gain = (cols[:, k : k + 1] for k in range(3))
    factor = gain * scale
    slant, offset = factor * scale * cols[:, 6:7], factor * cols[:, 7:8]
    for block in range(4):
        rp, cp = block // 2, block % 2
        lanes = slice(block * CELLS, (block + 1) * CELLS)
        for phase in range(4):
            rows = slice(phase * C2, (phase + 1) * C2)
            for t in range(6):
                away = pre_ref[t, rows, lanes] - mean[rows]
                dpre = factor[rows] * grad_ref[t, rows, lanes] - offset[rows] - away * slant[rows]
                if t == 0:
                    dpre = dpre * cols[rows, 4:5]
                if t == 5:
                    dpre = dpre * cols[rows, 5:6]
                all_ref[block, phase, t * C2 : (t + 1) * C2, :] = dpre.astype(BF16)
        for q, (rp2, dr) in enumerate(TAP_PHASES):
            for r, (cp2, dc) in enumerate(TAP_PHASES):
                moves = {}
                for trp in range(2):
                    for tcp in range(2):
                        srp, dj = FINE_STEPS[trp, dr]
                        scp, dl = FINE_STEPS[tcp, dc]
                        if (srp, scp) == (rp, cp):
                            moves[trp, tcp] = (dj, dl)
                for (trp, tcp), (dj, dl) in moves.items():
                    moved = all_ref[block, 2 * rp2 + cp2]
                    if (dj, dl) != (0, 0):
                        moved = matmul(moved, sh_ref[:, shift_slot(dj, dl)]).astype(BF16)
                    lane = (2 * trp + tcp) * CELLS
                    for t in range(6):
                        at = t * 16 * C2 + (4 * q + r) * C2
                        x_ref[at : at + C2, lane : lane + CELLS] = moved[t * C2 : (t + 1) * C2]

    cols = columns(st1_ref[...])
    mean, scale, gain, shift = (cols[0:C1, k : k + 1] for k in range(4))
    first = jnp.zeros((C1, CELLS), F32)
    second = jnp.zeros((C1, CELLS), F32)
    for j in range(2):
        for block in range(4):
            lanes = slice(block * CELLS, (block + 1) * CELLS)
            act_grad = matmul(b2_ref[...], x_ref[j * 32 * C2 : (j + 2) * 32 * C2, lanes])
            hat = (pre1_ref[j + 1, block * C1 : (block + 1) * C1, :] - mean) * scale
            norm = gain * hat + shift
            gate = sigmoid(norm)
            grad = act_grad * (gate * (1.0 + norm * (1.0 - gate)))
            g1_ref[j, block * C1 : (block + 1) * C1, :] = grad
            first = first + grad * hat
            second = second + grad
    emit_rows(
        out_ref,
        jnp.sum(first, axis=1, keepdims=True),
        jnp.sum(second, axis=1, keepdims=True),
    )
    parts = [
        matmul_nt(x_ref[t * 16 * C2 : (t + 1) * 16 * C2, :], act_ref[...]) for t in range(6)
    ]
    for p in range(2):
        low = [parts[p + 2 * k][:, 0:C1] for k in range(2)]
        high = [parts[p + 2 + 2 * k][:, C1:] for k in range(2)]
        dw_ref[p * 16 * C2 : (p + 1) * 16 * C2, :] = jnp.concatenate(
            low, axis=1
        ) + jnp.concatenate(high, axis=1)


def first_windows(x_ref, grad_ref, pre_ref, cols, sh_ref):
    mean, scale, gain = (cols[0:C1, k : k + 1] for k in range(3))
    factor = gain * scale
    slant, offset = factor * scale * cols[0:C1, 6:7], factor * cols[0:C1, 7:8]
    for block in range(4):
        rp, cp = block // 2, block % 2
        rows = slice(block * C1, (block + 1) * C1)
        dpre = jnp.concatenate(
            [
                (
                    factor * grad_ref[j, rows, :]
                    - offset
                    - (pre_ref[j + 1, rows, :] - mean) * slant
                ).astype(BF16)
                for j in range(2)
            ],
            axis=0,
        )
        for q, (trp, dj) in enumerate(TAP_PHASES):
            for r, (tcp, dl) in enumerate(TAP_PHASES):
                if (trp, tcp) != (rp, cp):
                    continue
                moved = dpre
                if (dj, dl) != (0, 0):
                    moved = matmul(dpre, sh_ref[:, shift_slot(dj, dl)]).astype(BF16)
                for j in range(2):
                    at = (16 * j + 4 * q + r) * C1
                    x_ref[at : at + C1, :] = moved[j * C1 : (j + 1) * C1]


def weight_half(half, x_ref, lat_ref, near_ref, dw2_ref, a_ref, b_ref):
    taps = 16 * C1
    chunk = a_ref.shape[0]
    fields = (
        jnp.where(half == 0, near_ref[1], lat_ref[...]),
        jnp.where(half == 0, lat_ref[...], near_ref[0]),
    )
    a_ref[0:taps, :] = matmul_nt(x_ref[taps:, :], fields[0]).astype(a_ref.dtype)
    split = chunk - taps
    a_ref[taps:, :] = matmul_nt(x_ref[0:split, :], fields[1]).astype(a_ref.dtype)
    b_ref[0 : taps - split, :] = matmul_nt(x_ref[split:taps, :], fields[1]).astype(b_ref.dtype)
    rest = chunk - taps + split
    at = pl.multiple_of(half * rest, rest)
    b_ref[taps - split :, :] = dw2_ref[pl.ds(at, rest), :].astype(b_ref.dtype)


def fifth_kernel(
    got_ref, g1_ref, pre1_ref, st1_ref, sh_ref, lat_ref, near_ref, dw2_ref, b1_ref,
    send_a_ref, send_b_ref, keep_a_ref, keep_b_ref, sum_ref, mid_ref, inner_ref, outer_ref,
    x_ref,
):
    sums = jnp.sum(got_ref[...], axis=0)
    sum_ref[...] = sums
    total = got_ref.shape[0] * 8 * CELLS
    cols = columns(jnp.concatenate([st1_ref[0:6], sums[0:2] / total], axis=0))
    first_windows(x_ref, g1_ref, pre1_ref, cols, sh_ref)
    core = lax.axis_index("rep")
    weight_half(core, x_ref, lat_ref, near_ref, dw2_ref, keep_a_ref, keep_b_ref)
    weight_half(1 - core, x_ref, lat_ref, near_ref, dw2_ref, send_a_ref, send_b_ref)
    pieces = [
        matmul(b1_ref[:, p * 16 * C1 : (p + 1) * 16 * C1], x_ref[j * 16 * C1 : (j + 1) * 16 * C1, :])
        for p, j in ((0, 1), (1, 0), (2, 1), (3, 0))
    ]
    mid_ref[...] = pieces[1] + pieces[2]
    up, down = pieces[0].astype(BF16), pieces[3].astype(BF16)
    even = is_even()
    inner_ref[...] = jnp.where(even, up, down)
    outer_ref[...] = jnp.where(even, down, up)


def last_kernel(
    own_a_ref, own_b_ref, other_a_ref, other_b_ref, dw1_far, dw2_far, x_ref, y_ref, sem
):
    core = lax.axis_index("rep")
    chunk = own_a_ref.shape[0]
    rest = 16 * C2
    kept = chunk - rest
    copies = []

    def send(src, dst):
        copies.append(pltpu.make_async_copy(src, dst, sem.at[len(copies)]))
        copies[-1].start()

    for half in range(2):
        at = half * (chunk + kept)
        x_ref[at : at + chunk, :] = jnp.where(
            core == half, own_a_ref[...], other_a_ref[...]
        ).astype(F32)
        send(x_ref.at[at : at + chunk], dw1_far.at[at : at + chunk])
        last = jnp.where(core == half, own_b_ref[...], other_b_ref[...]).astype(F32)
        x_ref[at + chunk : at + chunk + kept, :] = last[0:kept]
        send(
            x_ref.at[at + chunk : at + chunk + kept], dw1_far.at[at + chunk : at + chunk + kept]
        )
        for k in range(2):
            row = half * rest + k * 2 * rest
            y_ref[row : row + rest, :] = last[kept:, k * C1 : (k + 1) * C1]
            send(y_ref.at[row : row + rest], dw2_far.at[row : row + rest])
    for copy in copies:
        copy.wait()


def local(
    latent,
    first_weight,
    first_norm_gain,
    first_norm_shift,
    second_weight,
    second_norm_gain,
    second_norm_shift,
    cotangent,
):
    count = group_size()
    lat = latent.reshape(C0, CELLS)
    cot = cotangent.reshape(C2, 4, 16 * CELLS)
    top, bottom = cot[:, 3], cot[:, 0]
    lat_inner = swap_inner(lat)
    lat_outer = swap_outer(lat)
    cot_inner = swap_inner(jnp.where(is_even(), top, bottom))
    cot_outer = swap_outer(jnp.where(is_even(), bottom, top))
    planes = cot.transpose(1, 0, 2).reshape(4 * C2, 16 * CELLS)
    w1 = first_weight.reshape(64 * C1, C0)
    w2 = second_weight.reshape(64 * C2, C1)
    a1, a2, b1, b2, sh, p1, p2, spread, matrix = call(
        prepare_kernel,
        [
            ((8 * C1, 18 * C0), BF16),
            ((8 * C2, 18 * C1), BF16),
            ((C0, 64 * C1), BF16),
            ((C1, 64 * C2), BF16),
            ((CELLS, 9 * CELLS), BF16),
            ((8, 128), F32),
            ((8, 128), F32),
            ((4, 4 * C2, 4 * CELLS), BF16),
            ((512, 512), BF16),
        ],
        [
            w1,
            w2,
            first_norm_gain.reshape(1, C1),
            first_norm_shift.reshape(1, C1),
            second_norm_gain.reshape(1, C2),
            second_norm_shift.reshape(1, C2),
            planes,
        ],
        [
            pltpu.VMEM((64 * C1, C0), BF16),
            pltpu.VMEM((64 * C2, C1), BF16),
            pltpu.VMEM((1, C1), F32),
            pltpu.VMEM((1, C1), F32),
            pltpu.VMEM((1, C2), F32),
            pltpu.VMEM((1, C2), F32),
            pltpu.SemaphoreType.DMA((6,)),
        ],
        far_args=range(6),
    )
    stats = ((count, 8, 128), F32)
    pre1, out, near = call(
        first_kernel,
        [
            ((4, 4 * C1, CELLS), F32),
            stats,
            ((2, C0, CELLS), BF16),
        ],
        [lat, lat_inner, lat_outer, a1, sh],
        [pltpu.VMEM((27 * C0, CELLS), BF16)],
    )
    got = exchange(out)
    pre2, act, st1, out = call(
        second_kernel,
        [((6, 4 * C2, 4 * CELLS), F32), ((2 * C1, 4 * CELLS), BF16), ((8, 128), F32), stats],
        [got, pre1, p1, a2, sh],
        [pltpu.VMEM((36 * C1, 4 * CELLS), BF16), pltpu.VMEM((4, 4 * C1, CELLS), BF16)],
    )
    out, cot_inner, cot_outer = hold(out, cot_inner, cot_outer)
    got = exchange(out)
    grad2, feat, st2, out = call(
        third_kernel,
        [
            ((6, 4 * C2, 4 * CELLS), F32),
            ((4, 4 * C2, 4 * CELLS), BF16),
            ((8, 128), F32),
            stats,
        ],
        [got, pre2, spread, cot_inner, cot_outer, matrix, p2],
        [
            pltpu.VMEM((2 * C2, 16 * CELLS), BF16),
            pltpu.VMEM((2, 4 * C2, 4 * CELLS), BF16),
            pltpu.VMEM((4, 4 * C2, 4 * CELLS), BF16),
            pltpu.SemaphoreType.DMA,
        ],
        far=(1,),
    )
    got = exchange(out)
    grad1, dw2, sum2, out = call(
        fourth_kernel,
        [((2, 4 * C1, CELLS), F32), ((32 * C2, 2 * C1), F32), ((8, 128), F32), stats],
        [got, pre2, grad2, st2, b2, sh, act, pre1, st1],
        [pltpu.VMEM((96 * C2, 4 * CELLS), BF16), pltpu.VMEM((4, 4, 6 * C2, CELLS), BF16)],
    )
    got = exchange(out)
    rows = (64 * C1 + 32 * C2) // 4
    send_a, send_b, keep_a, keep_b, sum1, mid, lat_in, lat_out = call(
        fifth_kernel,
        [
            ((rows, C0), BF16),
            ((rows, C0), BF16),
            ((rows, C0), F32),
            ((rows, C0), F32),
            ((8, 128), F32),
            ((C0, CELLS), F32),
            ((C0, CELLS), BF16),
            ((C0, CELLS), BF16),
        ],
        [got, grad1, pre1, st1, sh, lat, near, dw2, b1],
        [
            pltpu.VMEM((32 * C1, CELLS), BF16),
        ],
    )
    sent_a, sent_b = swap(send_a, "rep", 1), swap(send_b, "rep", 1)
    parts = [keep_a + sent_a.astype(F32), keep_b + sent_b.astype(F32)]
    orders = chunk_steps()
    steps = len(orders[0])
    for step in range(steps):
        parts = [halve(part, *order[step]) for part, order in zip(parts, orders)]
    parts = [part.astype(BF16) for part in parts]
    lat_in, lat_out, *parts = hold(lat_in, lat_out, *parts)
    latent_grad = mid + swap_inner(lat_in).astype(F32) + swap_outer(lat_out).astype(F32)
    for step in reversed(range(steps)):
        if step == 0:
            feat, *parts = hold(feat, *parts)
            (features,) = call(gather_kernel, [((4 * C2, 16 * CELLS), BF16)], [feat])
            features = features.reshape(4, C2, 16 * CELLS).transpose(1, 0, 2)
        parts = [double(part, *order[step]) for part, order in zip(parts, orders)]
    features, latent_grad, part_a, part_b = hold(features, latent_grad, *parts)
    first_weight_grad, second_weight_grad = call(
        last_kernel,
        [((64 * C1, C0), F32), ((64 * C2, C1), F32)],
        [part_a, part_b, swap(part_a, "rep", 1), swap(part_b, "rep", 1)],
        [
            pltpu.VMEM((64 * C1, C0), F32),
            pltpu.VMEM((64 * C2, C1), F32),
            pltpu.SemaphoreType.DMA((8,)),
        ],
        far=range(2),
    )
    return (
        features[None],
        latent_grad.reshape(1, C0, 1, CELLS),
        first_weight_grad.reshape(64, C1, C0),
        second_weight_grad.reshape(64, C2, C1),
        sum1[0:2, 0:C1],
        sum2[0:2, 0:C2],
    )


def solution(mesh):
    volume = P(("group", "rep"), None, "space", None)
    in_specs = (volume, P(), P(), P(), P(), P(), P(), volume)
    out_specs = (
        volume,
        volume,
        P("group", None, None),
        P("group", None, None),
        P("group", None),
        P("group", None),
    )
    return jax.shard_map(local, mesh=mesh, in_specs=in_specs, out_specs=out_specs, check_vma=False)
```

```python
import jax
import jax.numpy as jnp
from jax import lax
from jax.experimental import pallas as pl
from jax.experimental.pallas import tpu as pltpu
from jax.sharding import PartitionSpec as P

H0 = 4
W0 = 64
CELLS = H0 * W0
C0 = 128
C1 = 64
C2 = 32
EPSILON = 1e-05

F32 = jnp.float32
BF16 = jnp.bfloat16
GROUP = ("space", "rep")

PHASE_TAPS = (((1, 0), (3, -1)), ((2, 0), (0, 1)))
TAP_PHASES = ((1, -1), (0, 0), (1, 0), (0, 1))
FINE_STEPS = {
    (0, -1): (1, -1),
    (0, 0): (0, 0),
    (0, 1): (1, 0),
    (1, -1): (0, 0),
    (1, 0): (1, 0),
    (1, 1): (0, 1),
}


def group_size():
    return lax.axis_size("space") * lax.axis_size("rep")


def swap(block, axis, bit):
    return lax.ppermute(block, axis, [(i, i ^ bit) for i in range(lax.axis_size(axis))])


def chunk_steps():
    bits = []
    bit = 1
    while bit < lax.axis_size("space"):
        bits.append(("space", bit))
        bit *= 2
    return bits[1:2] + bits[0:1] + bits[2:], bits


def halve(part, axis, bit):
    upper = (lax.axis_index(axis) // bit) % 2
    half = part.shape[0] // 2
    kept = lax.dynamic_slice_in_dim(part, upper * half, half)
    sent = lax.dynamic_slice_in_dim(part, (1 - upper) * half, half).astype(BF16)
    return kept + swap(sent, axis, bit).astype(F32)


def double(part, axis, bit):
    upper = (lax.axis_index(axis) // bit) % 2
    other = swap(part, axis, bit)
    return jnp.where(
        upper == 0, jnp.concatenate([part, other]), jnp.concatenate([other, part])
    )


def exchange(copies):
    return lax.all_to_all(copies, GROUP, 0, 0)


def is_even():
    return lax.axis_index("space") % 2 == 0


def swap_inner(block):
    return swap(block, "space", 1)


def swap_outer(block):
    count = lax.axis_size("space")
    pairs = [(i, i + 1) for i in range(1, count - 1, 2)]
    return lax.ppermute(block, "space", pairs + [(j, i) for i, j in pairs])


def hold(*values):
    return lax.optimization_barrier(values)


def call(kernel, outs, args, scratch=(), far=(), far_args=()):
    def spec(away):
        return pl.BlockSpec(memory_space=pl.ANY if away else pltpu.VMEM)

    return pl.pallas_call(
        kernel,
        out_shape=[jax.ShapeDtypeStruct(shape, dtype) for shape, dtype in outs],
        in_specs=[spec(k in far_args) for k in range(len(args))],
        out_specs=[spec(k in far) for k in range(len(outs))],
        scratch_shapes=list(scratch),
        compiler_params=pltpu.CompilerParams(vmem_limit_bytes=24 * 2**20),
        cost_estimate=pl.CostEstimate(flops=10**9, bytes_accessed=4 * 10**6, transcendentals=0),
    )(*args)


def matmul(a, b):
    return jnp.dot(a, b, preferred_element_type=F32)


def matmul_nt(a, b):
    return lax.dot_general(a, b, (((1,), (1,)), ((), ())), preferred_element_type=F32)


def shift_matrix(dj, dl):
    src = lax.broadcasted_iota(jnp.int32, (CELLS, CELLS), 0)
    dst = lax.broadcasted_iota(jnp.int32, (CELLS, CELLS), 1)
    col = dst % W0 + dl
    hit = (src == dst + dj * W0 + dl) & (col >= 0) & (col < W0)
    return jnp.where(hit, 1.0, 0.0).astype(BF16)


def shift_slot(dj, dl):
    return slice(((dj + 1) * 3 + dl + 1) * CELLS, ((dj + 1) * 3 + dl + 2) * CELLS)


def spread_matrix():
    src = lax.broadcasted_iota(jnp.int32, (512, 512), 0)
    dst = lax.broadcasted_iota(jnp.int32, (512, 512), 1)
    cp2, cp, jj, l = dst // 256, (dst // 128) % 2, (dst // 64) % 2, dst % 64
    return jnp.where(src == jj * 256 + 4 * l + 2 * cp + cp2, 1.0, 0.0).astype(BF16)


def columns(rows):
    return jnp.transpose(jnp.concatenate([rows, jnp.zeros((120, 128), F32)], axis=0))


def emit_rows(ref, first, second):
    lane = lax.broadcasted_iota(jnp.int32, (first.shape[0], 128), 1)
    tile = jnp.where(lane == 0, first, jnp.where(lane == 1, second, 0.0))
    tile = jnp.concatenate([tile] * (128 // first.shape[0]), axis=0)
    rows = jnp.transpose(tile)[0:8, :]
    for k in range(ref.shape[0]):
        ref[k] = rows


def fold(rows, channels):
    total = rows[0:channels]
    for k in range(1, rows.shape[0] // channels):
        total = total + rows[k * channels : (k + 1) * channels]
    return total


def moments(copies, local_count):
    count = copies.shape[0]
    sums = jnp.sum(copies, axis=0)
    mean = sums[0:1] / count
    away = copies - mean[None]
    spread = jnp.sum(away * away, axis=0)[0:1]
    variance = (sums[1:2] + local_count * spread) / (count * local_count)
    return mean, lax.rsqrt(variance + EPSILON)


def sigmoid(values):
    return 0.5 * jnp.tanh(0.5 * values) + 0.5


def spread_planes(cot_ref, out_ref, planes, matrix):
    for rp in range(2):
        for rp2 in range(2):
            for h in range(2):
                lanes = [(4 * (2 * h + jj) + 2 * rp + rp2) * 256 for jj in range(2)]
                rows = jnp.concatenate(
                    [cot_ref[0 : len(planes) * C2, at : at + 256] for at in lanes], axis=1
                )
                moved = matmul(rows, matrix).astype(BF16)
                for cp2 in range(2):
                    for cp in range(2):
                        row = (2 * rp2 + cp2) * C2
                        lane = (2 * rp + cp) * CELLS + h * 128
                        piece = moved[:, cp2 * 256 + cp * 128 : cp2 * 256 + cp * 128 + 128]
                        for k, t in enumerate(planes):
                            out_ref[t, row : row + C2, lane : lane + 128] = piece[
                                k * C2 : (k + 1) * C2
                            ]


def prepare_kernel(
    w1_far, w2_far, gain1_far, shift1_far, gain2_far, shift2_far, cot_ref,
    a1_ref, a2_ref, b1_ref, b2_ref, sh_ref, p1_ref, p2_ref, spread_ref, matrix_ref,
    w1_ref, w2_ref, gain1_ref, shift1_ref, gain2_ref, shift2_ref, sem,
):
    copies = [
        pltpu.make_async_copy(far, near, sem.at[k])
        for k, (far, near) in enumerate(
            (
                (w1_far, w1_ref),
                (w2_far, w2_ref),
                (gain1_far, gain1_ref),
                (shift1_far, shift1_ref),
                (gain2_far, gain2_ref),
                (shift2_far, shift2_ref),
            )
        )
    ]
    for copy in copies:
        copy.start()
    matrix_ref[...] = spread_matrix()
    spread_planes(cot_ref, spread_ref, range(4), matrix_ref[...])
    for dj in (-1, 0, 1):
        for dl in (-1, 0, 1):
            sh_ref[:, shift_slot(dj, dl)] = shift_matrix(dj, dl)
    for copy in copies:
        copy.wait()
    place = lax.axis_index("space")
    below = jnp.where(place > 0, 1.0, 0.0)
    above = jnp.where(place < lax.axis_size("space") - 1, 1.0, 0.0)
    edges = [jnp.full((1, 128), below, F32), jnp.full((1, 128), above, F32)]
    blank = [jnp.zeros((4, 128), F32)]
    p1_ref[...] = jnp.concatenate(
        [jnp.concatenate([ref[...]] * 2, axis=1) for ref in (gain1_ref, shift1_ref)] + edges + blank
    )
    p2_ref[...] = jnp.concatenate(
        [jnp.concatenate([ref[...]] * 4, axis=1) for ref in (gain2_ref, shift2_ref)] + edges + blank
    )
    for par in range(2):
        for rp in range(2):
            for cp in range(2):
                row2 = ((2 * rp + par) * 2 + cp) * C2
                pieces = [jnp.zeros((C2, C1), BF16)] * 12
                for p, dp in PHASE_TAPS[par]:
                    dt = dp + 1 - par
                    for q, dr in PHASE_TAPS[rp]:
                        for r, dc in PHASE_TAPS[cp]:
                            tap = 16 * p + 4 * q + r
                            slot = 2 * ((dr + 1 - rp) * 2 + dc + 1 - cp) + dt
                            row = ((2 * rp + cp) * 2 + par) * C1
                            a1_ref[row : row + C1, slot * C0 : (slot + 1) * C0] = w1_ref[
                                tap * C1 : (tap + 1) * C1, :
                            ]
                            slot = 2 * ((dr + 1 - rp) * 3 + dc + 1) + dt
                            pieces[slot] = w2_ref[tap * C2 : (tap + 1) * C2, :]
                a2_ref[row2 : row2 + C2, :] = jnp.concatenate(pieces, axis=1)
    for k in range(32):
        b1_ref[:, k * 128 : (k + 1) * 128] = jnp.transpose(w1_ref[k * 128 : (k + 1) * 128, :])
    for k in range(16):
        b2_ref[:, k * 128 : (k + 1) * 128] = jnp.transpose(w2_ref[k * 128 : (k + 1) * 128, :])


def window_shifts(phase):
    rp, cp = phase // 2, phase % 2
    return [(rp + dr) * 3 + cp + dc for dr in range(2) for dc in range(2)]


def first_kernel(
    lat_ref, inner_ref, outer_ref, a1_ref, sh_ref, pre_ref, out_ref, near_ref, x_ref
):
    even = is_even()
    near_ref[0] = jnp.where(even, outer_ref[...], inner_ref[...])
    near_ref[1] = jnp.where(even, inner_ref[...], outer_ref[...])
    planes = jnp.concatenate([near_ref[0], lat_ref[...], near_ref[1]], axis=0)
    for k in range(9):
        moved = planes
        if k != 4:
            moved = matmul(planes, sh_ref[:, k * CELLS : (k + 1) * CELLS]).astype(BF16)
        for z in range(3):
            at = (k * 3 + z) * C0
            x_ref[at : at + C0, :] = moved[z * C0 : (z + 1) * C0]
    for m in range(2):
        for phase in range(4):
            cells = jnp.concatenate(
                [x_ref[(k * 3 + m) * C0 : (k * 3 + m + 2) * C0, :] for k in window_shifts(phase)],
                axis=0,
            )
            both = matmul(a1_ref[phase * 2 * C1 : (phase + 1) * 2 * C1, :], cells)
            rows = slice(phase * C1, (phase + 1) * C1)
            pre_ref[2 * m + 1, rows, :] = both[0:C1]
            pre_ref[2 * m, rows, :] = both[C1 : 2 * C1]
    lower, upper = pre_ref[1], pre_ref[2]
    sums = fold(jnp.sum(lower + upper, axis=1, keepdims=True), C1)
    mean = sums / (8 * CELLS)
    wide = jnp.concatenate([mean] * 4, axis=0)
    lower, upper = lower - wide, upper - wide
    squares = fold(jnp.sum(lower * lower + upper * upper, axis=1, keepdims=True), C1)
    emit_rows(out_ref, mean, squares)


def second_kernel(got_ref, pre1_ref, p1_ref, a2_ref, sh_ref, pre_ref, act_ref, st_ref, out_ref, x_ref, all_ref):
    mean, scale = moments(got_ref[...], 8 * CELLS)
    st = jnp.concatenate([mean, scale, p1_ref[0:6]], axis=0)
    st_ref[...] = st
    cols = columns(st)
    mean, scale, gain, shift = (cols[0:C1, k : k + 1] for k in range(4))
    keeps = (cols[0:C1, 4:5], None, None, cols[0:C1, 5:6])
    for block in range(4):
        rp, cp = block // 2, block % 2
        for q in range(4):
            norm = gain * ((pre1_ref[q, block * C1 : (block + 1) * C1, :] - mean) * scale) + shift
            act = norm * sigmoid(norm)
            if keeps[q] is not None:
                act = act * keeps[q]
            act = act.astype(BF16)
            all_ref[block, q * C1 : (q + 1) * C1, :] = act
            if q in (1, 2):
                act_ref[(q - 1) * C1 : q * C1, block * CELLS : (block + 1) * CELLS] = act
        sj, sl = 1 - 2 * rp, 1 - 2 * cp
        for dj, dl in ((0, 0), (sj, 0), (0, sl), (sj, sl)):
            moved = all_ref[block]
            if (dj, dl) != (0, 0):
                moved = matmul(moved, sh_ref[:, shift_slot(dj, dl)]).astype(BF16)
            for (trp, dr), source in FINE_STEPS.items():
                if source != (rp, dj):
                    continue
                for (tcp, dc), source in FINE_STEPS.items():
                    if source != (cp, dl):
                        continue
                    lane = (2 * trp + tcp) * CELLS
                    for q in range(4):
                        at = (((dr + 1) * 3 + dc + 1) * 4 + q) * C1
                        x_ref[at : at + C1, lane : lane + CELLS] = moved[q * C1 : (q + 1) * C1]

    for m in range(3):
        for block in range(4):
            lanes = slice(block * CELLS, (block + 1) * CELLS)
            for rp in range(2):
                cells = jnp.concatenate(
                    [
                        x_ref[(k * 4 + m) * C1 : (k * 4 + m + 2) * C1, lanes]
                        for k in range(3 * rp, 3 * rp + 6)
                    ],
                    axis=0,
                )
                both = matmul(a2_ref[rp * 4 * C2 : (rp + 1) * 4 * C2, :], cells)
                rows = slice(rp * 2 * C2, (rp + 1) * 2 * C2)
                pre_ref[2 * m + 1, rows, lanes] = both[0 : 2 * C2]
                pre_ref[2 * m, rows, lanes] = both[2 * C2 : 4 * C2]

    partial = jnp.zeros((C2, CELLS), F32)
    for phase in range(4):
        for t in range(1, 5):
            for block in range(4):
                partial = partial + pre_ref[
                    t, phase * C2 : (phase + 1) * C2, block * CELLS : (block + 1) * CELLS
                ]
    mean = jnp.sum(partial, axis=1, keepdims=True) / (64 * CELLS)
    wide = jnp.broadcast_to(mean, (C2, CELLS))
    squares = jnp.zeros((C2, CELLS), F32)
    for phase in range(4):
        for t in range(1, 5):
            for block in range(4):
                away = (
                    pre_ref[
                        t, phase * C2 : (phase + 1) * C2, block * CELLS : (block + 1) * CELLS
                    ]
                    - wide
                )
                squares = squares + away * away
    emit_rows(out_ref, mean, jnp.sum(squares, axis=1, keepdims=True))


def gather_kernel(feat_ref, out_ref):
    matrix = spread_matrix()
    count = feat_ref.shape[0]
    for rp in range(2):
        for rp2 in range(2):
            for h in range(2):
                pieces = []
                for cp2 in range(2):
                    for cp in range(2):
                        row = (2 * rp2 + cp2) * C2
                        lane = (2 * rp + cp) * CELLS + h * 128
                        pieces.append(
                            jnp.concatenate(
                                [
                                    feat_ref[t, row : row + C2, lane : lane + 128]
                                    for t in range(count)
                                ],
                                axis=0,
                            )
                        )
                moved = matmul_nt(jnp.concatenate(pieces, axis=1), matrix).astype(BF16)
                for jj in range(2):
                    at = (4 * (2 * h + jj) + 2 * rp + rp2) * 256
                    out_ref[:, at : at + 256] = moved[:, jj * 256 : (jj + 1) * 256]


def third_kernel(
    got_ref, pre_ref, cot_ref, inner_ref, outer_ref, matrix_ref, p2_ref,
    grad_ref, feat_far, st_ref, out_ref, rows_ref, edge_ref, feat_ref, sem,
):
    even = is_even()
    rows_ref[0:C2] = jnp.where(even, outer_ref[...], inner_ref[...])
    rows_ref[C2:] = jnp.where(even, inner_ref[...], outer_ref[...])
    spread_planes(rows_ref, edge_ref, range(2), matrix_ref[...])
    mean, scale = moments(got_ref[...], 64 * CELLS)
    st = jnp.concatenate([mean, scale, p2_ref[0:6]], axis=0)
    st_ref[...] = st
    cols = columns(st)
    sums = []
    for phase in range(4):
        rows = slice(phase * C2, (phase + 1) * C2)
        mean, scale, gain, shift = (
            jnp.broadcast_to(cols[rows, k : k + 1], (C2, CELLS)) for k in range(4)
        )

        def slope(t, lane, cot):
            hat = (pre_ref[t, rows, pl.ds(lane, CELLS)] - mean) * scale
            norm = gain * hat + shift
            gate = sigmoid(norm)
            grad = cot.astype(F32) * (gate * (1.0 + norm * (1.0 - gate)))
            grad_ref[t, rows, pl.ds(lane, CELLS)] = grad
            return hat, norm, gate, grad

        def body(step, carry):
            t = step // 4
            lane = pl.multiple_of((step % 4) * CELLS, CELLS)
            hat, norm, gate, grad = slope(t + 1, lane, cot_ref[t, rows, pl.ds(lane, CELLS)])
            feat_ref[t, rows, pl.ds(lane, CELLS)] = (norm * gate).astype(BF16)
            return carry[0] + grad * hat, carry[1] + grad

        zero = jnp.zeros((C2, CELLS), F32)
        sums.append(lax.fori_loop(0, 16, body, (zero, zero), unroll=16))

        for k in range(2):
            for lane in range(0, 4 * CELLS, CELLS):
                slope(5 * k, lane, edge_ref[k, rows, pl.ds(lane, CELLS)])

    copy = pltpu.make_async_copy(feat_ref, feat_far, sem)
    copy.start()
    first, second = (sum(part[k] for part in sums) for k in range(2))
    emit_rows(
        out_ref,
        jnp.sum(first, axis=1, keepdims=True),
        jnp.sum(second, axis=1, keepdims=True),
    )
    copy.wait()


def fourth_kernel(
    got_ref, pre_ref, grad_ref, st2_ref, b2_ref, sh_ref, act_ref, pre1_ref, st1_ref,
    g1_ref, dw_ref, sum_ref, out_ref, x_ref, all_ref,
):
    sums = jnp.sum(got_ref[...], axis=0)
    sum_ref[...] = sums
    total = got_ref.shape[0] * 64 * CELLS
    cols = columns(jnp.concatenate([st2_ref[0:6], sums[0:2] / total], axis=0))
    mean, scale, gain = (cols[:, k : k + 1] for k in range(3))
    factor = gain * scale
    slant, offset = factor * scale * cols[:, 6:7], factor * cols[:, 7:8]
    for block in range(4):
        rp, cp = block // 2, block % 2
        lanes = slice(block * CELLS, (block + 1) * CELLS)
        for phase in range(4):
            rows = slice(phase * C2, (phase + 1) * C2)
            for t in range(6):
                away = pre_ref[t, rows, lanes] - mean[rows]
                dpre = factor[rows] * grad_ref[t, rows, lanes] - offset[rows] - away * slant[rows]
                if t == 0:
                    dpre = dpre * cols[rows, 4:5]
                if t == 5:
                    dpre = dpre * cols[rows, 5:6]
                all_ref[block, phase, t * C2 : (t + 1) * C2, :] = dpre.astype(BF16)
        for q, (rp2, dr) in enumerate(TAP_PHASES):
            for r, (cp2, dc) in enumerate(TAP_PHASES):
                moves = {}
                for trp in range(2):
                    for tcp in range(2):
                        srp, dj = FINE_STEPS[trp, dr]
                        scp, dl = FINE_STEPS[tcp, dc]
                        if (srp, scp) == (rp, cp):
                            moves[trp, tcp] = (dj, dl)
                for (trp, tcp), (dj, dl) in moves.items():
                    moved = all_ref[block, 2 * rp2 + cp2]
                    if (dj, dl) != (0, 0):
                        moved = matmul(moved, sh_ref[:, shift_slot(dj, dl)]).astype(BF16)
                    lane = (2 * trp + tcp) * CELLS
                    for t in range(6):
                        at = t * 16 * C2 + (4 * q + r) * C2
                        x_ref[at : at + C2, lane : lane + CELLS] = moved[t * C2 : (t + 1) * C2]

    cols = columns(st1_ref[...])
    mean, scale, gain, shift = (cols[0:C1, k : k + 1] for k in range(4))
    first = jnp.zeros((C1, CELLS), F32)
    second = jnp.zeros((C1, CELLS), F32)
    for j in range(2):
        for block in range(4):
            lanes = slice(block * CELLS, (block + 1) * CELLS)
            act_grad = matmul(b2_ref[...], x_ref[j * 32 * C2 : (j + 2) * 32 * C2, lanes])
            hat = (pre1_ref[j + 1, block * C1 : (block + 1) * C1, :] - mean) * scale
            norm = gain * hat + shift
            gate = sigmoid(norm)
            grad = act_grad * (gate * (1.0 + norm * (1.0 - gate)))
            g1_ref[j, block * C1 : (block + 1) * C1, :] = grad
            first = first + grad * hat
            second = second + grad
    emit_rows(
        out_ref,
        jnp.sum(first, axis=1, keepdims=True),
        jnp.sum(second, axis=1, keepdims=True),
    )
    parts = [
        matmul_nt(x_ref[t * 16 * C2 : (t + 1) * 16 * C2, :], act_ref[...]) for t in range(6)
    ]
    for p in range(2):
        low = [parts[p + 2 * k][:, 0:C1] for k in range(2)]
        high = [parts[p + 2 + 2 * k][:, C1:] for k in range(2)]
        dw_ref[p * 16 * C2 : (p + 1) * 16 * C2, :] = jnp.concatenate(
            low, axis=1
        ) + jnp.concatenate(high, axis=1)


def first_windows(x_ref, grad_ref, pre_ref, cols, sh_ref):
    mean, scale, gain = (cols[0:C1, k : k + 1] for k in range(3))
    factor = gain * scale
    slant, offset = factor * scale * cols[0:C1, 6:7], factor * cols[0:C1, 7:8]
    for block in range(4):
        rp, cp = block // 2, block % 2
        rows = slice(block * C1, (block + 1) * C1)
        dpre = jnp.concatenate(
            [
                (
                    factor * grad_ref[j, rows, :]
                    - offset
                    - (pre_ref[j + 1, rows, :] - mean) * slant
                ).astype(BF16)
                for j in range(2)
            ],
            axis=0,
        )
        for q, (trp, dj) in enumerate(TAP_PHASES):
            for r, (tcp, dl) in enumerate(TAP_PHASES):
                if (trp, tcp) != (rp, cp):
                    continue
                moved = dpre
                if (dj, dl) != (0, 0):
                    moved = matmul(dpre, sh_ref[:, shift_slot(dj, dl)]).astype(BF16)
                for j in range(2):
                    at = (16 * j + 4 * q + r) * C1
                    x_ref[at : at + C1, :] = moved[j * C1 : (j + 1) * C1]


def weight_half(half, x_ref, lat_ref, near_ref, dw2_ref, a_ref, b_ref):
    taps = 16 * C1
    chunk = a_ref.shape[0]
    fields = (
        jnp.where(half == 0, near_ref[1], lat_ref[...]),
        jnp.where(half == 0, lat_ref[...], near_ref[0]),
    )
    a_ref[0:taps, :] = matmul_nt(x_ref[taps:, :], fields[0]).astype(a_ref.dtype)
    split = chunk - taps
    a_ref[taps:, :] = matmul_nt(x_ref[0:split, :], fields[1]).astype(a_ref.dtype)
    b_ref[0 : taps - split, :] = matmul_nt(x_ref[split:taps, :], fields[1]).astype(b_ref.dtype)
    rest = chunk - taps + split
    at = pl.multiple_of(half * rest, rest)
    b_ref[taps - split :, :] = dw2_ref[pl.ds(at, rest), :].astype(b_ref.dtype)


def fifth_kernel(
    got_ref, g1_ref, pre1_ref, st1_ref, sh_ref, lat_ref, near_ref, dw2_ref, b1_ref,
    send_a_ref, send_b_ref, keep_a_ref, keep_b_ref, sum_ref, mid_ref, inner_ref, outer_ref,
    x_ref,
):
    sums = jnp.sum(got_ref[...], axis=0)
    sum_ref[...] = sums
    total = got_ref.shape[0] * 8 * CELLS
    cols = columns(jnp.concatenate([st1_ref[0:6], sums[0:2] / total], axis=0))
    first_windows(x_ref, g1_ref, pre1_ref, cols, sh_ref)
    core = lax.axis_index("rep")
    weight_half(core, x_ref, lat_ref, near_ref, dw2_ref, keep_a_ref, keep_b_ref)
    weight_half(1 - core, x_ref, lat_ref, near_ref, dw2_ref, send_a_ref, send_b_ref)
    pieces = [
        matmul(b1_ref[:, p * 16 * C1 : (p + 1) * 16 * C1], x_ref[j * 16 * C1 : (j + 1) * 16 * C1, :])
        for p, j in ((0, 1), (1, 0), (2, 1), (3, 0))
    ]
    mid_ref[...] = pieces[1] + pieces[2]
    up, down = pieces[0].astype(BF16), pieces[3].astype(BF16)
    even = is_even()
    inner_ref[...] = jnp.where(even, up, down)
    outer_ref[...] = jnp.where(even, down, up)


def last_kernel(
    own_a_ref, own_b_ref, other_a_ref, other_b_ref, dw1_far, dw2_far, x_ref, y_ref, sem
):
    core = lax.axis_index("rep")
    chunk = own_a_ref.shape[0]
    rest = 16 * C2
    kept = chunk - rest
    copies = []

    def send(src, dst):
        copies.append(pltpu.make_async_copy(src, dst, sem.at[len(copies)]))
        copies[-1].start()

    for half in range(2):
        at = half * (chunk + kept)
        x_ref[at : at + chunk, :] = jnp.where(
            core == half, own_a_ref[...], other_a_ref[...]
        ).astype(F32)
        send(x_ref.at[at : at + chunk], dw1_far.at[at : at + chunk])
        last = jnp.where(core == half, own_b_ref[...], other_b_ref[...]).astype(F32)
        x_ref[at + chunk : at + chunk + kept, :] = last[0:kept]
        send(
            x_ref.at[at + chunk : at + chunk + kept], dw1_far.at[at + chunk : at + chunk + kept]
        )
        for k in range(2):
            row = half * rest + k * 2 * rest
            y_ref[row : row + rest, :] = last[kept:, k * C1 : (k + 1) * C1]
            send(y_ref.at[row : row + rest], dw2_far.at[row : row + rest])
    for copy in copies:
        copy.wait()


def local(
    latent,
    first_weight,
    first_norm_gain,
    first_norm_shift,
    second_weight,
    second_norm_gain,
    second_norm_shift,
    cotangent,
):
    count = group_size()
    lat = latent.reshape(C0, CELLS)
    cot = cotangent.reshape(C2, 4, 16 * CELLS)
    top, bottom = cot[:, 3], cot[:, 0]
    lat_inner = swap_inner(lat)
    lat_outer = swap_outer(lat)
    cot_inner = swap_inner(jnp.where(is_even(), top, bottom))
    cot_outer = swap_outer(jnp.where(is_even(), bottom, top))
    planes = cot.transpose(1, 0, 2).reshape(4 * C2, 16 * CELLS)
    w1 = first_weight.reshape(64 * C1, C0)
    w2 = second_weight.reshape(64 * C2, C1)
    a1, a2, b1, b2, sh, p1, p2, spread, matrix = call(
        prepare_kernel,
        [
            ((8 * C1, 8 * C0), BF16),
            ((8 * C2, 12 * C1), BF16),
            ((C0, 64 * C1), BF16),
            ((C1, 64 * C2), BF16),
            ((CELLS, 9 * CELLS), BF16),
            ((8, 128), F32),
            ((8, 128), F32),
            ((4, 4 * C2, 4 * CELLS), BF16),
            ((512, 512), BF16),
        ],
        [
            w1,
            w2,
            first_norm_gain.reshape(1, C1),
            first_norm_shift.reshape(1, C1),
            second_norm_gain.reshape(1, C2),
            second_norm_shift.reshape(1, C2),
            planes,
        ],
        [
            pltpu.VMEM((64 * C1, C0), BF16),
            pltpu.VMEM((64 * C2, C1), BF16),
            pltpu.VMEM((1, C1), F32),
            pltpu.VMEM((1, C1), F32),
            pltpu.VMEM((1, C2), F32),
            pltpu.VMEM((1, C2), F32),
            pltpu.SemaphoreType.DMA((6,)),
        ],
        far_args=range(6),
    )
    stats = ((count, 8, 128), F32)
    pre1, out, near = call(
        first_kernel,
        [
            ((4, 4 * C1, CELLS), F32),
            stats,
            ((2, C0, CELLS), BF16),
        ],
        [lat, lat_inner, lat_outer, a1, sh],
        [pltpu.VMEM((27 * C0, CELLS), BF16)],
    )
    got = exchange(out)
    pre2, act, st1, out = call(
        second_kernel,
        [((6, 4 * C2, 4 * CELLS), F32), ((2 * C1, 4 * CELLS), BF16), ((8, 128), F32), stats],
        [got, pre1, p1, a2, sh],
        [pltpu.VMEM((36 * C1, 4 * CELLS), BF16), pltpu.VMEM((4, 4 * C1, CELLS), BF16)],
    )
    out, cot_inner, cot_outer = hold(out, cot_inner, cot_outer)
    got = exchange(out)
    grad2, feat, st2, out = call(
        third_kernel,
        [
            ((6, 4 * C2, 4 * CELLS), F32),
            ((4, 4 * C2, 4 * CELLS), BF16),
            ((8, 128), F32),
            stats,
        ],
        [got, pre2, spread, cot_inner, cot_outer, matrix, p2],
        [
            pltpu.VMEM((2 * C2, 16 * CELLS), BF16),
            pltpu.VMEM((2, 4 * C2, 4 * CELLS), BF16),
            pltpu.VMEM((4, 4 * C2, 4 * CELLS), BF16),
            pltpu.SemaphoreType.DMA,
        ],
        far=(1,),
    )
    got = exchange(out)
    grad1, dw2, sum2, out = call(
        fourth_kernel,
        [((2, 4 * C1, CELLS), F32), ((32 * C2, 2 * C1), F32), ((8, 128), F32), stats],
        [got, pre2, grad2, st2, b2, sh, act, pre1, st1],
        [pltpu.VMEM((96 * C2, 4 * CELLS), BF16), pltpu.VMEM((4, 4, 6 * C2, CELLS), BF16)],
    )
    got = exchange(out)
    rows = (64 * C1 + 32 * C2) // 4
    send_a, send_b, keep_a, keep_b, sum1, mid, lat_in, lat_out = call(
        fifth_kernel,
        [
            ((rows, C0), BF16),
            ((rows, C0), BF16),
            ((rows, C0), F32),
            ((rows, C0), F32),
            ((8, 128), F32),
            ((C0, CELLS), F32),
            ((C0, CELLS), BF16),
            ((C0, CELLS), BF16),
        ],
        [got, grad1, pre1, st1, sh, lat, near, dw2, b1],
        [
            pltpu.VMEM((32 * C1, CELLS), BF16),
        ],
    )
    sent_a, sent_b = swap(send_a, "rep", 1), swap(send_b, "rep", 1)
    parts = [keep_a + sent_a.astype(F32), keep_b + sent_b.astype(F32)]
    orders = chunk_steps()
    steps = len(orders[0])
    for step in range(steps):
        parts = [halve(part, *order[step]) for part, order in zip(parts, orders)]
    parts = [part.astype(BF16) for part in parts]
    lat_in, lat_out, *parts = hold(lat_in, lat_out, *parts)
    latent_grad = mid + swap_inner(lat_in).astype(F32) + swap_outer(lat_out).astype(F32)
    for step in reversed(range(steps)):
        if step == 0:
            feat, *parts = hold(feat, *parts)
            (features,) = call(gather_kernel, [((4 * C2, 16 * CELLS), BF16)], [feat])
            features = features.reshape(4, C2, 16 * CELLS).transpose(1, 0, 2)
        parts = [double(part, *order[step]) for part, order in zip(parts, orders)]
    features, latent_grad, part_a, part_b = hold(features, latent_grad, *parts)
    first_weight_grad, second_weight_grad = call(
        last_kernel,
        [((64 * C1, C0), F32), ((64 * C2, C1), F32)],
        [part_a, part_b, swap(part_a, "rep", 1), swap(part_b, "rep", 1)],
        [
            pltpu.VMEM((64 * C1, C0), F32),
            pltpu.VMEM((64 * C2, C1), F32),
            pltpu.SemaphoreType.DMA((8,)),
        ],
        far=range(2),
    )
    return (
        features[None],
        latent_grad.reshape(1, C0, 1, CELLS),
        first_weight_grad.reshape(64, C1, C0),
        second_weight_grad.reshape(64, C2, C1),
        sum1[0:2, 0:C1],
        sum2[0:2, 0:C2],
    )


def solution(mesh):
    volume = P(("group", "rep"), None, "space", None)
    in_specs = (volume, P(), P(), P(), P(), P(), P(), volume)
    out_specs = (
        volume,
        volume,
        P("group", None, None),
        P("group", None, None),
        P("group", None),
        P("group", None),
    )
    return jax.shard_map(local, mesh=mesh, in_specs=in_specs, out_specs=out_specs, check_vma=False)
```
